32 devices in a mesh: dp: 2 (over x), expert: 4 (over z), shard: 4 (over y, core).
Axes of the slice: x: 2, y: 2, z: 4, core: 2. Of those that a mesh axis runs over, the one named last changes fastest.
Arguments:
- tokens: bfloat16 [256, 6144], P(('dp', 'expert', 'shard')), may hold values from -6 to 6
- gate_up_weight: bfloat16 [4, 2, 8192, 6144], P(None, None, ('dp', 'expert', 'shard')), may hold values from -0.078125 to 0.078125
- down_weight: bfloat16 [4, 8192, 6144], P(None, ('dp', 'expert', 'shard')), may hold values from -0.0625 to 0.0625
- expert_ids: int32 [256, 2], P(('dp', 'expert', 'shard')), may hold values from 0 to 3, as said below
- slot_ids: int32 [256, 2], P(('dp', 'expert', 'shard')), may hold values from 0 to 7, as said below
- gate_values: float32 [256, 2], P(('dp', 'expert', 'shard')), may hold values from 0.1 to 1
- old_place: int32 [4], replicated, may hold values from 0 to 3, each once
- new_place: int32 [4], replicated, may hold values from 0 to 3, each once
Outputs:
- mixed_out: bfloat16 [256, 6144], P(('dp', 'expert', 'shard'))
The draws below stay inside these ranges and needn't reach their ends.
Inputs may be any that keep to these rules, and one draw needn't show every extreme that they name: `expert_ids`: each token names 2 different experts; among the 8 tokens of one block no expert is named more than 8 times, and one expert is named exactly 8 times in every block. `slot_ids`: within one block, two choices that name the same expert have different slots. `old_place`: each expert number appears once. `new_place`: each expert number appears once.
All inputs are finite; a program needn't handle non-finite values.
Results may differ from the reference program's by a relative error of at most 0.02.
Values may be sent and summed in bfloat16 or wider, within the bound.
No kernel may reach another device: no remote copies, remote signals or barrier semaphores. Data moves between devices by JAX's collectives and lax.ppermute only.
A program may use at most 192 MiB of HBM per device.

```python
import jax
import jax.numpy as jnp
from jax import lax

D = 6144
FF = 8192
TOP = 2
TOK_DEV = 8
EXPERTS = 4
BLOCKS = 32
TOKENS = 256
CAP = 8
CLASSES = 4


def routing_table(key):
    base_key = jax.random.fold_in(key, 7177)
    favour = jax.random.randint(jax.random.fold_in(base_key, 1), (), 0, EXPERTS).astype(jnp.int32)

    def one_block(block_index):
        block_key = jax.random.fold_in(base_key, block_index + 2)
        key_rank, key_cells, key_offset, key_order, key_flip = jax.random.split(block_key, 5)
        others = jax.random.permutation(key_rank, EXPERTS - 1).astype(jnp.int32) + 1
        run_ranks = jnp.concatenate([jnp.zeros((1,), jnp.int32), others])
        run_expert = (favour + run_ranks) % EXPERTS
        cell_pick = jax.random.permutation(key_cells, (EXPERTS - 1) * CAP).astype(jnp.int32)[:2 * TOK_DEV - CAP]
        chosen = cell_pick // CAP + 1
        run_numbers = jnp.arange(EXPERTS, dtype=jnp.int32)
        counts = jnp.sum((chosen[None, :] == run_numbers[:, None]).astype(jnp.int32), axis=1)
        counts = jnp.where(run_numbers == 0, CAP, counts).astype(jnp.int32)
        run_ends = jnp.cumsum(counts).astype(jnp.int32)
        starts = run_ends - counts
        entries = jnp.arange(2 * TOK_DEV, dtype=jnp.int32)
        run_of = jnp.sum((entries[:, None] >= run_ends[None, :]).astype(jnp.int32), axis=1)
        in_run = entries - starts[run_of]
        expert = run_expert[run_of]
        offset = jax.random.randint(key_offset, (EXPERTS,), 0, CAP).astype(jnp.int32)
        slot_of = (in_run + offset[expert]) % CAP
        pair_expert = jnp.stack([expert[:TOK_DEV], expert[TOK_DEV:]], axis=1)
        pair_slot = jnp.stack([slot_of[:TOK_DEV], slot_of[TOK_DEV:]], axis=1)
        shuffle = jax.random.permutation(key_order, TOK_DEV)
        pair_expert = pair_expert[shuffle]
        pair_slot = pair_slot[shuffle]
        flipped = jax.random.randint(key_flip, (TOK_DEV, 1), 0, 2)
        pair_expert = jnp.where(flipped == 1, pair_expert[:, ::-1], pair_expert)
        pair_slot = jnp.where(flipped == 1, pair_slot[:, ::-1], pair_slot)
        return (pair_expert, pair_slot)
    experts_all, slots_all = jax.vmap(one_block)(jnp.arange(TOKENS // TOK_DEV, dtype=jnp.int32))
    return (experts_all.reshape(TOKENS, TOP).astype(jnp.int32), slots_all.reshape(TOKENS, TOP).astype(jnp.int32))


def draw_expert_ids(key, part):
    return routing_table(key)[0]


def draw_slot_ids(key, part):
    return routing_table(key)[1]


def block_levels(key, extent, cuts, low, top_value):
    level = 1.0
    for dim, shards_of in cuts:
        heights = jax.random.uniform(jax.random.fold_in(jax.random.fold_in(key, 6), dim), (shards_of,), jnp.float32, low / len(cuts), top_value / len(cuts))
        level = level * jnp.repeat(jnp.exp(heights), extent[dim] // shards_of).reshape((-1,) + (1,) * (len(extent) - 1 - dim))
    return level


def centred(stream_key, dims, spread, limit, pieces=(), kind=jnp.bfloat16):
    values = spread * jax.random.normal(stream_key, dims, jnp.float32)
    if pieces:
        values = values * block_levels(stream_key, dims, pieces, -0.22, 0.18)
    return jnp.clip(values, -limit, limit).astype(kind)


def setup_inputs(seed: int = 0) -> dict:
    key_list = jax.random.split(jax.random.key(seed), 9)
    tokens = centred(key_list[0], (TOKENS, D), 1.0, 6.0, ((0, 32),))
    gate_up_weight = centred(key_list[1], (EXPERTS, 2, FF, D), D ** -0.5, 0.078125, ((2, 32),))
    down_weight = centred(key_list[2], (EXPERTS, FF, D), FF ** -0.5, 0.0625, ((1, 32),))
    expert_ids = draw_expert_ids(jax.random.fold_in(key_list[8], 71), 0)
    slot_ids = draw_slot_ids(jax.random.fold_in(key_list[8], 71), 0)
    gate_values = jnp.clip(0.1 + 0.9 * jax.random.uniform(key_list[5], (TOKENS, TOP), jnp.float32) ** block_levels(key_list[5], (TOKENS, TOP), ((0, 32),), -0.2, 0.2), 0.1, 1.0)
    old_place = jax.random.permutation(key_list[6], EXPERTS).astype(jnp.int32)
    new_place = jax.random.permutation(key_list[7], EXPERTS).astype(jnp.int32)
    return {"tokens": tokens, "gate_up_weight": gate_up_weight, "down_weight": down_weight, "expert_ids": expert_ids, "slot_ids": slot_ids, "gate_values": gate_values, "old_place": old_place, "new_place": new_place}


def reference(tokens, gate_up_weight, down_weight, expert_ids, slot_ids, gate_values, old_place, new_place):
    cell_count = EXPERTS * CAP
    matches = (new_place[:, None] == old_place[None, :]).astype(jnp.int32)
    slot_order = jnp.sum(matches * jnp.arange(EXPERTS, dtype=jnp.int32)[None, :], axis=1).astype(jnp.int32)
    ordered_in = jnp.take(gate_up_weight, slot_order, axis=0)
    ordered_down = jnp.take(down_weight, slot_order, axis=0)
    cell_ids = (expert_ids * CAP + slot_ids).reshape(BLOCKS, TOK_DEV, TOP)
    cell_range = jnp.arange(cell_count, dtype=jnp.int32)
    cell_hits = (cell_ids[:, :, :, None] == cell_range[None, None, None, :]).astype(jnp.float32)
    token_picks = jnp.sum(cell_hits, axis=2)
    token_blocks = tokens.reshape(BLOCKS, TOK_DEV, D).astype(jnp.float32)
    dispatched = jnp.einsum("btc,btd->bcd", token_picks, token_blocks, precision=lax.Precision.HIGHEST).astype(jnp.bfloat16)
    per_expert = dispatched.reshape(BLOCKS, EXPERTS, CAP, D).transpose(1, 0, 2, 3).reshape(EXPERTS, BLOCKS * CAP, D)
    sliver = FF // BLOCKS
    groups = FF // (CLASSES * sliver)

    def one_expert(operands):
        expert_rows, pair_in, down_rows = operands
        gate_part = jnp.dot(expert_rows, pair_in[0].T, preferred_element_type=jnp.float32)
        up_part = jnp.dot(expert_rows, pair_in[1].T, preferred_element_type=jnp.float32)
        hidden = (jax.nn.silu(gate_part) * up_part).astype(jnp.bfloat16)
        row_total = expert_rows.shape[0]
        hidden_classes = hidden.reshape(row_total, groups, CLASSES, sliver)
        down_classes = down_rows.reshape(groups, CLASSES, sliver, D)

        def add_class(total, class_index):
            piece = lax.dynamic_index_in_dim(hidden_classes, class_index, 2, keepdims=False).reshape(row_total, groups * sliver)
            weight_piece = lax.dynamic_index_in_dim(down_classes, class_index, 1, keepdims=False).reshape(groups * sliver, D)
            partial_value = jnp.dot(piece, weight_piece, preferred_element_type=jnp.float32).astype(jnp.bfloat16)
            partial_value = lax.optimization_barrier(partial_value)
            return total + partial_value.astype(jnp.float32), class_index

        total, unused_index = lax.scan(add_class, jnp.zeros((row_total, D), jnp.float32), jnp.arange(CLASSES, dtype=jnp.int32))
        return total.astype(jnp.bfloat16)

    expert_out = lax.map(one_expert, (per_expert, ordered_in, ordered_down))
    returned = expert_out.reshape(EXPERTS, BLOCKS, CAP, D).transpose(1, 0, 2, 3).reshape(BLOCKS, cell_count, D)
    combine_weights = jnp.sum(cell_hits * gate_values.reshape(BLOCKS, TOK_DEV, TOP)[:, :, :, None], axis=2)
    mixed_out = jnp.einsum("btc,bcd->btd", combine_weights, returned.astype(jnp.float32), precision=lax.Precision.HIGHEST)
    return mixed_out.reshape(TOKENS, D).astype(jnp.bfloat16)
```

```python
import jax
import jax.numpy as jnp
from jax import lax
from jax.sharding import PartitionSpec as P

AXES = ("dp", "expert", "shard")


def slot_coefficients(expert_ids, gate_values, old_place, new_place):
    matches = (new_place[:, None] == old_place[None, :]).astype(jnp.float32)
    picks = (expert_ids[:, :, None] == jnp.arange(new_place.shape[0], dtype=jnp.int32)).astype(jnp.float32)
    by_expert = jnp.sum(picks * gate_values[:, :, None], axis=1)
    return jnp.sum(by_expert[:, :, None] * matches[None, :, :], axis=1)


def local(
    tokens, gate_up_weight, down_weight, expert_ids, slot_ids, gate_values, old_place, new_place
):
    experts, _, sliver, model_width = gate_up_weight.shape
    coefficients = slot_coefficients(expert_ids, gate_values, old_place, new_place)
    all_tokens = lax.all_gather(tokens, AXES, axis=0, tiled=True)
    all_coefficients = lax.all_gather(coefficients, AXES, axis=0, tiled=True)
    pre_act = jnp.einsum(
        "td,eghd->tegh", all_tokens, gate_up_weight, preferred_element_type=jnp.float32
    )
    hidden = jax.nn.silu(pre_act[:, :, 0]) * pre_act[:, :, 1]
    hidden = (hidden * all_coefficients[:, :, None]).astype(jnp.bfloat16)
    partial = jnp.dot(
        hidden.reshape(-1, experts * sliver),
        down_weight.reshape(experts * sliver, model_width),
        preferred_element_type=jnp.float32,
    ).astype(jnp.bfloat16)
    return lax.psum_scatter(partial, AXES, scatter_dimension=0, tiled=True)


def solution(mesh):
    in_specs = (
        P(AXES, None),
        P(None, None, AXES, None),
        P(None, AXES, None),
        P(AXES, None),
        P(AXES, None),
        P(AXES, None),
        P(),
        P(),
    )
    return jax.shard_map(
        local, mesh=mesh, in_specs=in_specs, out_specs=P(AXES, None), check_vma=False
    )
```

```python
import jax
import jax.numpy as jnp
from jax import lax
from jax.sharding import PartitionSpec as P

AXES = ("dp", "expert", "shard")
LANES = 128


def slot_coefficients(expert_ids, gate_values, old_place, new_place):
    matches = (new_place[:, None] == old_place[None, :]).astype(jnp.float32)
    picks = (expert_ids[:, :, None] == jnp.arange(new_place.shape[0], dtype=jnp.int32)).astype(jnp.float32)
    by_expert = jnp.sum(picks * gate_values[:, :, None], axis=1)
    return jnp.sum(by_expert[:, :, None] * matches[None, :, :], axis=1)


def split_exact(value):
    pieces = []
    for _ in range(3):
        piece = lax.reduce_precision(value, exponent_bits=8, mantissa_bits=7)
        pieces.append(piece.astype(jnp.bfloat16))
        value = value - piece
    return pieces


class Line:
    def __init__(self, name, ways, stride, size):
        self.name, self.ways, self.stride, self.size = name, ways, stride, size

    def shift(self, value, step):
        pairs = []
        for index in range(self.ways):
            digit = index // self.stride % self.size
            target = (digit + step) % self.size
            pairs.append((index, index + (target - digit) * self.stride))
        return lax.ppermute(value, self.name, pairs)

    def gather(self, block, dim):
        return jnp.stack([block] + [self.shift(block, s) for s in range(1, self.size)], axis=dim)

    def reduce(self, slots, dim):
        own = lax.index_in_dim(slots, 0, dim, keepdims=False).astype(jnp.float32)
        for s in range(1, self.size):
            sent = lax.index_in_dim(slots, s, dim, keepdims=False)
            own = own + self.shift(sent, self.size - s).astype(jnp.float32)
        return own.astype(jnp.bfloat16)


def local(
    tokens, gate_up_weight, down_weight, expert_ids, slot_ids, gate_values, old_place, new_place
):
    experts, _, sliver, model_width = gate_up_weight.shape
    rows = tokens.shape[0]
    half = model_width // 2
    ways = {name: lax.axis_size(name) for name in AXES}
    cores = 2 if ways["shard"] % 2 == 0 else 1
    x_line = Line("dp", ways["dp"], 1, ways["dp"])
    z_line = Line("expert", ways["expert"], 1, ways["expert"])
    y_line = Line("shard", ways["shard"], cores, ways["shard"] // cores)
    core_line = Line("shard", ways["shard"], 1, cores)

    coefficients = slot_coefficients(expert_ids, gate_values, old_place, new_place)
    extra = jnp.concatenate(split_exact(coefficients), axis=1)
    extra = jnp.pad(extra, ((0, 0), (0, -extra.shape[1] % LANES)))
    parts = [
        jnp.concatenate([tokens[:, :half], extra], axis=1),
        tokens[:, half:],
    ]
    gathered = []
    for number, part in enumerate(parts):
        block = z_line.gather(part, 0)
        if number == 0:
            block = x_line.gather(y_line.gather(block, 0), 0)
        else:
            block = y_line.gather(x_line.gather(block, 0), 1)
        block = core_line.gather(block, 0)
        gathered.append(block.reshape(-1, part.shape[1]))
    weigh = gathered[0][:, half : half + 3 * experts].astype(jnp.float32)
    weigh = weigh.reshape(-1, 3, experts).sum(axis=1)
    flat_in = gate_up_weight.reshape(-1, model_width)
    pre_act = sum(
        lax.dot_general(
            rows_of[:, :half],
            flat_in[:, number * half : (number + 1) * half],
            (((1,), (1,)), ((), ())),
            preferred_element_type=jnp.float32,
        )
        for number, rows_of in enumerate(gathered)
    ).reshape(-1, experts, 2, sliver)
    hidden = jax.nn.silu(pre_act[:, :, 0]) * pre_act[:, :, 1]
    hidden = (hidden * weigh[:, :, None]).astype(jnp.bfloat16).reshape(-1, experts * sliver)
    flat_down = down_weight.reshape(-1, model_width)
    results = []
    for number in range(2):
        block = jnp.dot(
            hidden,
            flat_down[:, number * half : (number + 1) * half],
            preferred_element_type=jnp.float32,
        ).astype(jnp.bfloat16)
        block = block.reshape(
            core_line.size, x_line.size, y_line.size, z_line.size, rows, half
        )
        block = core_line.reduce(block, 0)
        if number == 0:
            block = y_line.reduce(x_line.reduce(block, 0), 0)
        else:
            block = x_line.reduce(y_line.reduce(block, 1), 0)
        results.append(z_line.reduce(block, 0))
    return jnp.concatenate(results, axis=1)


def solution(mesh):
    in_specs = (
        P(AXES, None),
        P(None, None, AXES, None),
        P(None, AXES, None),
        P(AXES, None),
        P(AXES, None),
        P(AXES, None),
        P(),
        P(),
    )
    return jax.shard_map(
        local, mesh=mesh, in_specs=in_specs, out_specs=P(AXES, None), check_vma=False
    )
```

```python
import jax
import jax.numpy as jnp
from jax import lax
from jax.experimental import pallas as pl
from jax.experimental.pallas import tpu as pltpu
from jax.sharding import PartitionSpec as P

AXES = ("dp", "expert", "shard")
LANES = 128
ROW_BLOCK = 256
VMEM_LIMIT = 28 * 2**20


def slot_coefficients(expert_ids, gate_values, old_place, new_place):
    matches = (new_place[:, None] == old_place[None, :]).astype(jnp.float32)
    picks = (expert_ids[:, :, None] == jnp.arange(new_place.shape[0], dtype=jnp.int32)).astype(jnp.float32)
    by_expert = jnp.sum(picks * gate_values[:, :, None], axis=1)
    return jnp.sum(by_expert[:, :, None] * matches[None, :, :], axis=1)


def split_exact(value):
    pieces = []
    for _ in range(3):
        piece = lax.reduce_precision(value, exponent_bits=8, mantissa_bits=7)
        pieces.append(piece.astype(jnp.bfloat16))
        value = value - piece
    return pieces


class Digit:
    def __init__(self, name, ways, stride, size):
        self.name, self.ways, self.stride, self.size = name, ways, stride, size

    def shift(self, value, step):
        pairs = []
        for index in range(self.ways):
            digit = index // self.stride % self.size
            target = (digit + step) % self.size
            pairs.append((index, index + (target - digit) * self.stride))
        return lax.ppermute(value, self.name, pairs)

    def gather(self, block, dim):
        return jnp.stack([block] + [self.shift(block, s) for s in range(1, self.size)], axis=dim)

    def reduce(self, slots, dim):
        own = lax.index_in_dim(slots, 0, dim, keepdims=False).astype(jnp.float32)
        for s in range(1, self.size):
            sent = lax.index_in_dim(slots, s, dim, keepdims=False)
            own = own + self.shift(sent, self.size - s).astype(jnp.float32)
        return own.astype(jnp.bfloat16)


def digits_of(name, ways, low=1):
    digits, stride = [], low
    while stride < ways:
        left = ways // stride
        size = 2 if left % 2 == 0 else left
        digits.append(Digit(name, ways, stride, size))
        stride *= size
    return digits[::-1]


def hidden_kernel(experts, steps, first_ref, second_ref, extra_ref, w_ref, hidden_ref):
    half = second_ref.shape[1]
    units = w_ref.shape[2]
    weights = w_ref[0].reshape(2 * units, w_ref.shape[3])
    contract = (((1,), (1,)), ((), ()))
    pre = lax.dot_general(
        first_ref[...], weights[:, :half], contract, preferred_element_type=jnp.float32
    )
    pre += lax.dot_general(
        second_ref[...], weights[:, half:], contract, preferred_element_type=jnp.float32
    )
    slot = pl.program_id(1) // steps
    extra = extra_ref[...].astype(jnp.float32)
    lane = lax.broadcasted_iota(jnp.int32, extra.shape, 1)
    mine = (lane == slot) | (lane == slot + experts) | (lane == slot + 2 * experts)
    weigh = jnp.sum(jnp.where(mine, extra, 0.0), axis=1, keepdims=True)
    gate, up = pre[:, :units], pre[:, units:]
    hidden_ref[...] = (gate / (1.0 + jnp.exp(-gate)) * up * weigh).astype(hidden_ref.dtype)


def hidden_of(first, second, gate_up_weight):
    experts, _, sliver, model_width = gate_up_weight.shape
    rows, half = second.shape
    row_block = min(ROW_BLOCK, rows)
    units = min(LANES, sliver)
    steps = sliver // units
    if units % LANES:
        return hidden_plain(first, second, gate_up_weight)

    def kernel(*refs):
        hidden_kernel(experts, steps, *refs)

    return pl.pallas_call(
        kernel,
        grid=(rows // row_block, experts * steps),
        in_specs=[
            pl.BlockSpec((row_block, half), lambda r, i: (r, 0)),
            pl.BlockSpec((row_block, half), lambda r, i: (r, 0)),
            pl.BlockSpec((row_block, LANES), lambda r, i: (r, half // LANES)),
            pl.BlockSpec((1, 2, units, model_width), lambda r, i: (i // steps, 0, i % steps, 0)),
        ],
        out_specs=pl.BlockSpec((row_block, units), lambda r, i: (r, i)),
        out_shape=jax.ShapeDtypeStruct((rows, experts * sliver), jnp.bfloat16),
        compiler_params=pltpu.CompilerParams(vmem_limit_bytes=VMEM_LIMIT),
        cost_estimate=pl.CostEstimate(
            flops=4 * rows * experts * sliver * model_width,
            bytes_accessed=2 * (gate_up_weight.size + rows * model_width),
            transcendentals=rows * experts * sliver,
        ),
    )(first, second, first, gate_up_weight)


def hidden_plain(first, second, gate_up_weight):
    experts, _, sliver, model_width = gate_up_weight.shape
    half = second.shape[1]
    weigh = first[:, half : half + 3 * experts].astype(jnp.float32)
    weigh = weigh.reshape(-1, 3, experts).sum(axis=1)
    tokens = jnp.concatenate([first[:, :half], second], axis=1)
    hidden = []
    for slot in range(experts):
        gate, up = (
            lax.dot_general(
                tokens,
                gate_up_weight[slot, side],
                (((1,), (1,)), ((), ())),
                preferred_element_type=jnp.float32,
            )
            for side in range(2)
        )
        hidden.append((jax.nn.silu(gate) * up * weigh[:, slot : slot + 1]).astype(jnp.bfloat16))
    return jnp.concatenate(hidden, axis=1)


def down_kernel(hidden_ref, w_ref, out_ref):
    out_ref[...] = jnp.dot(
        hidden_ref[...], w_ref[...], preferred_element_type=jnp.float32
    ).astype(out_ref.dtype)


def down_of(hidden, flat_down, part, columns):
    rows, depth = hidden.shape
    row_block = min(ROW_BLOCK, rows)
    block = columns
    for candidate in (512, 384, 256, 128):
        if columns % candidate == 0:
            block = candidate
            break
    steps = columns // block
    return pl.pallas_call(
        down_kernel,
        grid=(rows // row_block, steps),
        in_specs=[
            pl.BlockSpec((row_block, depth), lambda r, j: (r, 0)),
            pl.BlockSpec((depth, block), lambda r, j: (0, part * steps + j)),
        ],
        out_specs=pl.BlockSpec((row_block, block), lambda r, j: (r, j)),
        out_shape=jax.ShapeDtypeStruct((rows, columns), jnp.bfloat16),
        compiler_params=pltpu.CompilerParams(vmem_limit_bytes=VMEM_LIMIT),
        cost_estimate=pl.CostEstimate(
            flops=2 * rows * depth * columns,
            bytes_accessed=2 * (depth * columns + rows * depth + rows * columns),
            transcendentals=0,
        ),
    )(hidden, flat_down)


def local(
    tokens, gate_up_weight, down_weight, expert_ids, slot_ids, gate_values, old_place, new_place
):
    model_width = tokens.shape[1]
    rows = tokens.shape[0]
    half = model_width // 2
    ways = {name: lax.axis_size(name) for name in AXES}
    cores = 2 if ways["shard"] % 2 == 0 else 1
    x_digits = digits_of("dp", ways["dp"])
    z_digits = digits_of("expert", ways["expert"])
    y_digits = digits_of("shard", ways["shard"], cores)
    core_digits = [Digit("shard", ways["shard"], 1, cores)]
    dim_order = core_digits + x_digits[::-1] + y_digits[::-1] + z_digits[::-1]
    routes = [z_digits + y_digits + x_digits, z_digits + x_digits + y_digits]

    coefficients = slot_coefficients(expert_ids, gate_values, old_place, new_place)
    extra = jnp.concatenate(split_exact(coefficients), axis=1)
    extra = jnp.pad(extra, ((0, 0), (0, -extra.shape[1] % LANES)))
    parts = [
        jnp.concatenate([tokens[:, :half], extra], axis=1),
        tokens[:, half:],
    ]
    gathered = []
    for part, route in zip(parts, routes):
        block, held = part, []
        for digit in route + core_digits:
            dim = sum(dim_order.index(other) < dim_order.index(digit) for other in held)
            block = digit.gather(block, dim)
            held.append(digit)
        gathered.append(block.reshape(-1, part.shape[1]))
    hidden = hidden_of(gathered[0], gathered[1], gate_up_weight)
    flat_down = down_weight.reshape(-1, model_width)
    results = []
    for number, route in enumerate(routes):
        block = down_of(hidden, flat_down, number, half)
        block = block.reshape([digit.size for digit in dim_order] + [rows, half])
        held = list(dim_order)
        for digit in core_digits + route[::-1]:
            block = digit.reduce(block, held.index(digit))
            held.remove(digit)
        results.append(block)
    return jnp.concatenate(results, axis=1)


def solution(mesh):
    in_specs = (
        P(AXES, None),
        P(None, None, AXES, None),
        P(None, AXES, None),
        P(AXES, None),
        P(AXES, None),
        P(AXES, None),
        P(),
        P(),
    )
    return jax.shard_map(
        local, mesh=mesh, in_specs=in_specs, out_specs=P(AXES, None), check_vma=False
    )
```

```python
import jax
import jax.numpy as jnp
from jax import lax
from jax.experimental import pallas as pl
from jax.experimental.pallas import tpu as pltpu
from jax.sharding import PartitionSpec as P

AXES = ("dp", "expert", "shard")
LANES = 128
ROW_BLOCK = 256
PIECES = 4
FETCH_LIMIT = 1 * 2**20
HIDDEN_LIMIT = 32 * 2**20
DOWN_LIMIT = 8 * 2**20


def slot_coefficients(expert_ids, gate_values, old_place, new_place):
    matches = (new_place[:, None] == old_place[None, :]).astype(jnp.float32)
    picks = (expert_ids[:, :, None] == jnp.arange(new_place.shape[0], dtype=jnp.int32)).astype(jnp.float32)
    by_expert = jnp.sum(picks * gate_values[:, :, None], axis=1)
    return jnp.sum(by_expert[:, :, None] * matches[None, :, :], axis=1)


def split_exact(value):
    pieces = []
    for _ in range(3):
        piece = lax.reduce_precision(value, exponent_bits=8, mantissa_bits=7)
        pieces.append(piece.astype(jnp.bfloat16))
        value = value - piece
    return pieces


class Digit:
    def __init__(self, name, ways, stride, size):
        self.name, self.ways, self.stride, self.size = name, ways, stride, size

    def shift(self, value, step):
        pairs = []
        for index in range(self.ways):
            digit = index // self.stride % self.size
            target = (digit + step) % self.size
            pairs.append((index, index + (target - digit) * self.stride))
        return lax.ppermute(value, self.name, pairs)

    def gather(self, block, dim):
        return jnp.stack([block] + [self.shift(block, s) for s in range(1, self.size)], axis=dim)

    def reduce(self, slots, dim):
        own = lax.index_in_dim(slots, 0, dim, keepdims=False).astype(jnp.float32)
        for s in range(1, self.size):
            sent = lax.index_in_dim(slots, s, dim, keepdims=False)
            own = own + self.shift(sent, self.size - s).astype(jnp.float32)
        return own.astype(jnp.bfloat16)


def digits_of(name, ways, low=1):
    digits, stride = [], low
    while stride < ways:
        left = ways // stride
        size = 2 if left % 2 == 0 else left
        digits.append(Digit(name, ways, stride, size))
        stride *= size
    return digits[::-1]


def resident(value):
    return pltpu.with_memory_space_constraint(value, pltpu.VMEM)


def in_hbm(value):
    return pltpu.with_memory_space_constraint(value, pltpu.HBM)


def fetch_kernel(w_ref, after_ref, out_ref, sem):
    del after_ref
    copy = pltpu.make_async_copy(w_ref, out_ref, sem)
    copy.start()
    copy.wait()


def fetched(weight, after):
    return pl.pallas_call(
        fetch_kernel,
        in_specs=[pl.BlockSpec(memory_space=pl.ANY)] * 2,
        out_specs=pl.BlockSpec(memory_space=pltpu.VMEM),
        out_shape=pltpu.VMEM(weight.shape, weight.dtype),
        scratch_shapes=[pltpu.SemaphoreType.DMA],
        compiler_params=pltpu.CompilerParams(vmem_limit_bytes=FETCH_LIMIT),
        cost_estimate=pl.CostEstimate(
            flops=0, bytes_accessed=2 * weight.size, transcendentals=0
        ),
    )(in_hbm(weight), after)


def hidden_kernel(first_ref, second_ref, w_hbm, hidden_ref, w_ref, sems):
    experts, _, sliver, model_width = w_hbm.shape
    half = model_width // 2
    depth = model_width // PIECES

    def copy(slot, piece):
        columns = pl.ds(piece * depth, depth)
        return pltpu.make_async_copy(
            w_hbm.at[slot, :, :, columns], w_ref.at[slot, :, :, columns], sems.at[slot, piece]
        )

    @pl.when(pl.program_id(0) == 0)
    def start():
        for slot in range(experts):
            for piece in range(PIECES):
                copy(slot, piece).start()

    extra = first_ref[:, half:].astype(jnp.float32)
    lane = lax.broadcasted_iota(jnp.int32, extra.shape, 1)
    for slot in range(experts):
        pre = None
        for piece in range(PIECES):
            pl.when(pl.program_id(0) == 0)(copy(slot, piece).wait)
            at = piece * depth
            weights = w_ref[slot, :, :, at : at + depth].reshape(2 * sliver, depth)
            if at < half:
                rows = first_ref[:, at : at + depth]
            else:
                rows = second_ref[:, at - half : at - half + depth]
            product = lax.dot_general(
                weights, rows, (((1,), (1,)), ((), ())), preferred_element_type=jnp.float32
            )
            pre = product if pre is None else pre + product
        gate, up = pre[:sliver], pre[sliver:]
        hidden = (gate / (1.0 + jnp.exp(-gate)) * up).T
        mine = (lane == slot) | (lane == slot + experts) | (lane == slot + 2 * experts)
        weigh = jnp.sum(jnp.where(mine, extra, 0.0), axis=1, keepdims=True)
        hidden_ref[slot] = (hidden * weigh).astype(hidden_ref.dtype)


def hidden_of(first, second, gate_up_weight):
    experts, _, sliver, model_width = gate_up_weight.shape
    rows, half = second.shape
    row_block = min(ROW_BLOCK, rows)
    if rows == row_block:
        first, second = resident(first), resident(second)
        row_specs = [pl.BlockSpec(memory_space=pltpu.VMEM)] * 2
    else:
        row_specs = [
            pl.BlockSpec((row_block, first.shape[1]), lambda r: (r, 0)),
            pl.BlockSpec((row_block, half), lambda r: (r, 0)),
        ]
    return pl.pallas_call(
        hidden_kernel,
        grid=(rows // row_block,),
        in_specs=row_specs + [pl.BlockSpec(memory_space=pl.ANY)],
        out_specs=pl.BlockSpec((experts, row_block, sliver), lambda r: (0, r, 0)),
        out_shape=jax.ShapeDtypeStruct((experts, rows, sliver), jnp.bfloat16),
        scratch_shapes=[
            pltpu.VMEM(gate_up_weight.shape, gate_up_weight.dtype),
            pltpu.SemaphoreType.DMA((experts, PIECES)),
        ],
        compiler_params=pltpu.CompilerParams(vmem_limit_bytes=HIDDEN_LIMIT),
        cost_estimate=pl.CostEstimate(
            flops=4 * rows * experts * sliver * model_width,
            bytes_accessed=2 * (gate_up_weight.size + rows * model_width),
            transcendentals=rows * experts * sliver,
        ),
    )(first, second, in_hbm(gate_up_weight))


def down_kernel(part, hidden_ref, w_ref, out_ref):
    experts, _, sliver = hidden_ref.shape
    columns = out_ref.shape[1]
    block = next(size for size in (512, 384, 256, 128, columns) if columns % size == 0)

    def one_block(step, carry):
        at = pl.multiple_of(step * block, block)
        taken = pl.ds(pl.multiple_of(part * columns + step * block, block), block)
        hidden = jnp.concatenate([hidden_ref[slot] for slot in range(experts)], axis=1)
        weights = w_ref[:, :, taken].reshape(experts * sliver, block)
        out_ref[:, pl.ds(at, block)] = jnp.dot(
            hidden, weights, preferred_element_type=jnp.float32
        ).astype(out_ref.dtype)
        return carry

    lax.fori_loop(0, columns // block, one_block, 0)


def down_of(hidden, down_weight, part, columns):
    experts, rows, sliver = hidden.shape
    row_block = min(ROW_BLOCK, rows)

    def kernel(*refs):
        down_kernel(part, *refs)

    return pl.pallas_call(
        kernel,
        grid=(rows // row_block,),
        in_specs=[
            pl.BlockSpec((experts, row_block, sliver), lambda r: (0, r, 0)),
            pl.BlockSpec(memory_space=pltpu.VMEM),
        ],
        out_specs=pl.BlockSpec((row_block, columns), lambda r: (r, 0)),
        out_shape=jax.ShapeDtypeStruct((rows, columns), jnp.bfloat16),
        compiler_params=pltpu.CompilerParams(vmem_limit_bytes=DOWN_LIMIT),
        cost_estimate=pl.CostEstimate(
            flops=2 * rows * experts * sliver * columns,
            bytes_accessed=2 * (experts * sliver * columns + rows * experts * sliver + rows * columns),
            transcendentals=0,
        ),
    )(hidden, down_weight)


def local(
    tokens, gate_up_weight, down_weight, expert_ids, slot_ids, gate_values, old_place, new_place
):
    model_width = tokens.shape[1]
    rows = tokens.shape[0]
    half = model_width // 2
    ways = {name: lax.axis_size(name) for name in AXES}
    cores = 2 if ways["shard"] % 2 == 0 else 1
    x_digits = digits_of("dp", ways["dp"])
    z_digits = digits_of("expert", ways["expert"])
    y_digits = digits_of("shard", ways["shard"], cores)
    core_digits = [Digit("shard", ways["shard"], 1, cores)]
    dim_order = core_digits + x_digits[::-1] + y_digits[::-1] + z_digits[::-1]
    routes = [z_digits + y_digits + x_digits, z_digits + x_digits + y_digits]

    coefficients = slot_coefficients(expert_ids, gate_values, old_place, new_place)
    extra = jnp.concatenate(split_exact(coefficients), axis=1)
    extra = jnp.pad(extra, ((0, 0), (0, -extra.shape[1] % LANES)))
    parts = [
        jnp.concatenate([tokens[:, :half], extra], axis=1),
        tokens[:, half:],
    ]
    blocks, held = list(parts), [[], []]
    last = len(routes[0]) - 1
    for step in range(last + 2):
        if step == last:
            before_last = blocks[0]
        if step == last + 1:
            blocks[1], down_weight = lax.optimization_barrier(
                (blocks[1], fetched(down_weight, before_last))
            )
        for number in (1, 0):
            digit = (routes[number] + core_digits)[step]
            dim = sum(dim_order.index(other) < dim_order.index(digit) for other in held[number])
            blocks[number] = digit.gather(blocks[number], dim)
            held[number].append(digit)
    gathered = [block.reshape(-1, part.shape[1]) for block, part in zip(blocks, parts)]
    hidden = hidden_of(gathered[0], gathered[1], gate_up_weight)
    down_weight = resident(down_weight)
    results = []
    for number, route in enumerate(routes):
        block = down_of(hidden, down_weight, number, half)
        block = block.reshape([digit.size for digit in dim_order] + [rows, half])
        held = list(dim_order)
        for digit in core_digits + route[::-1]:
            block = digit.reduce(block, held.index(digit))
            held.remove(digit)
        results.append(block)
    return jnp.concatenate(results, axis=1)


def solution(mesh):
    in_specs = (
        P(AXES, None),
        P(None, None, AXES, None),
        P(None, AXES, None),
        P(AXES, None),
        P(AXES, None),
        P(AXES, None),
        P(),
        P(),
    )
    return jax.shard_map(
        local, mesh=mesh, in_specs=in_specs, out_specs=P(AXES, None), check_vma=False
    )
```

```python
import jax
import jax.numpy as jnp
from jax import lax
from jax.experimental import pallas as pl
from jax.experimental.pallas import tpu as pltpu
from jax.sharding import PartitionSpec as P

AXES = ("dp", "expert", "shard")
LANES = 128
ROW_BLOCK = 256
PIECES = 2
FETCH_LIMIT = 1 * 2**20
GATE_UP_LIMIT = 24 * 2**20
DOWN_LIMIT = 8 * 2**20


def slot_coefficients(expert_ids, gate_values, old_place, new_place):
    matches = (new_place[:, None] == old_place[None, :]).astype(jnp.float32)
    picks = (expert_ids[:, :, None] == jnp.arange(new_place.shape[0], dtype=jnp.int32)).astype(jnp.float32)
    by_expert = jnp.sum(picks * gate_values[:, :, None], axis=1)
    return jnp.sum(by_expert[:, :, None] * matches[None, :, :], axis=1)


def split_exact(value):
    pieces = []
    for _ in range(3):
        piece = lax.reduce_precision(value, exponent_bits=8, mantissa_bits=7)
        pieces.append(piece.astype(jnp.bfloat16))
        value = value - piece
    return pieces


class Digit:
    def __init__(self, name, ways, stride, size):
        self.name, self.ways, self.stride, self.size = name, ways, stride, size

    def shift(self, value, step):
        pairs = []
        for index in range(self.ways):
            digit = index // self.stride % self.size
            target = (digit + step) % self.size
            pairs.append((index, index + (target - digit) * self.stride))
        return lax.ppermute(value, self.name, pairs)

    def gather(self, block, dim):
        return jnp.stack([block] + [self.shift(block, s) for s in range(1, self.size)], axis=dim)

    def reduce(self, slots, dim):
        own = lax.index_in_dim(slots, 0, dim, keepdims=False).astype(jnp.float32)
        for s in range(1, self.size):
            sent = lax.index_in_dim(slots, s, dim, keepdims=False)
            own = own + self.shift(sent, self.size - s).astype(jnp.float32)
        return own.astype(jnp.bfloat16)


def digits_of(name, ways, low=1):
    digits, stride = [], low
    while stride < ways:
        left = ways // stride
        size = 2 if left % 2 == 0 else left
        digits.append(Digit(name, ways, stride, size))
        stride *= size
    return digits[::-1]


def resident(value):
    return pltpu.with_memory_space_constraint(value, pltpu.VMEM)


def in_hbm(value):
    return pltpu.with_memory_space_constraint(value, pltpu.HBM)


def fetch_kernel(w_ref, after_ref, out_ref, sem):
    del after_ref
    copy = pltpu.make_async_copy(w_ref, out_ref, sem)
    copy.start()
    copy.wait()


def fetched(weight, after):
    return pl.pallas_call(
        fetch_kernel,
        in_specs=[pl.BlockSpec(memory_space=pl.ANY)] * 2,
        out_specs=pl.BlockSpec(memory_space=pltpu.VMEM),
        out_shape=pltpu.VMEM(weight.shape, weight.dtype),
        scratch_shapes=[pltpu.SemaphoreType.DMA],
        compiler_params=pltpu.CompilerParams(vmem_limit_bytes=FETCH_LIMIT),
        cost_estimate=pl.CostEstimate(
            flops=0, bytes_accessed=2 * weight.size, transcendentals=0
        ),
    )(in_hbm(weight), after)


def gate_up_kernel(part, rows_ref, *refs):
    last = part == 0
    if last:
        sum_ref, w_hbm, out_ref, w_ref, turned_ref, sems = refs
    else:
        w_hbm, out_ref, w_ref, turned_ref, sems = refs
    experts, _, sliver, half = w_ref.shape
    depth = half // PIECES

    def copy(slot, piece):
        return pltpu.make_async_copy(
            w_hbm.at[slot, :, :, pl.ds(part * half + piece * depth, depth)],
            w_ref.at[slot, :, :, pl.ds(piece * depth, depth)],
            sems.at[slot, piece],
        )

    @pl.when(pl.program_id(0) == 0)
    def start():
        for slot in range(experts):
            for piece in range(PIECES):
                copy(slot, piece).start()

    for piece in range(PIECES):
        at = piece * depth
        turned_ref[at : at + depth] = rows_ref[:, at : at + depth].T
    if last:
        extra = rows_ref[:, half:].astype(jnp.float32)
        lane = lax.broadcasted_iota(jnp.int32, extra.shape, 1)
    for slot in range(experts):
        pre = sum_ref[slot] if last else None
        for piece in range(PIECES):
            pl.when(pl.program_id(0) == 0)(copy(slot, piece).wait)
            at = piece * depth
            product = jnp.dot(
                w_ref[slot, :, :, at : at + depth].reshape(2 * sliver, depth),
                turned_ref[at : at + depth],
                preferred_element_type=jnp.float32,
            )
            pre = product if pre is None else pre + product
        if not last:
            out_ref[slot] = pre
            continue
        gate, up = pre[:sliver], pre[sliver:]
        hidden = (gate / (1.0 + jnp.exp(-gate)) * up).T
        mine = (lane == slot) | (lane == slot + experts) | (lane == slot + 2 * experts)
        weigh = jnp.sum(jnp.where(mine, extra, 0.0), axis=1, keepdims=True)
        out_ref[slot] = (hidden * weigh).astype(out_ref.dtype)


def gate_up_of(part, rows_of_part, sums, gate_up_weight):
    experts, _, sliver, model_width = gate_up_weight.shape
    half = model_width // 2
    rows, width = rows_of_part.shape
    row_block = min(ROW_BLOCK, rows)
    whole = rows == row_block
    operands = [rows_of_part] if sums is None else [rows_of_part, sums]
    if whole:
        operands = [resident(operand) for operand in operands]
        specs = [pl.BlockSpec(memory_space=pltpu.VMEM)] * len(operands)
    else:
        specs = [
            pl.BlockSpec((row_block, width), lambda r: (r, 0)),
            pl.BlockSpec((experts, 2 * sliver, row_block), lambda r: (0, 0, r)),
        ][: len(operands)]
    if sums is None:
        out_spec = pl.BlockSpec((experts, 2 * sliver, row_block), lambda r: (0, 0, r))
        out_shape = jax.ShapeDtypeStruct((experts, 2 * sliver, rows), jnp.float32)
    else:
        out_spec = pl.BlockSpec((experts, row_block, sliver), lambda r: (0, r, 0))
        out_shape = jax.ShapeDtypeStruct((experts, rows, sliver), jnp.bfloat16)
    if whole:
        out_spec = pl.BlockSpec(memory_space=pltpu.VMEM)
        out_shape = pltpu.VMEM(out_shape.shape, out_shape.dtype)

    def kernel(*refs):
        gate_up_kernel(part, *refs)

    return pl.pallas_call(
        kernel,
        grid=(rows // row_block,),
        in_specs=specs + [pl.BlockSpec(memory_space=pl.ANY)],
        out_specs=out_spec,
        out_shape=out_shape,
        scratch_shapes=[
            pltpu.VMEM((experts, 2, sliver, half), gate_up_weight.dtype),
            pltpu.VMEM((half, row_block), rows_of_part.dtype),
            pltpu.SemaphoreType.DMA((experts, PIECES)),
        ],
        compiler_params=pltpu.CompilerParams(vmem_limit_bytes=GATE_UP_LIMIT),
        cost_estimate=pl.CostEstimate(
            flops=2 * rows * experts * sliver * model_width,
            bytes_accessed=gate_up_weight.size + rows * model_width,
            transcendentals=rows * experts * sliver,
        ),
    )(*operands, in_hbm(gate_up_weight))


def down_kernel(part, hidden_ref, w_ref, out_ref):
    experts, _, sliver = hidden_ref.shape
    columns = out_ref.shape[1]
    block = next(size for size in (1024, 512, 384, 256, 128, columns) if columns % size == 0)

    def one_block(step, carry):
        at = pl.multiple_of(step * block, block)
        taken = pl.ds(pl.multiple_of(part * columns + step * block, block), block)
        hidden = jnp.concatenate([hidden_ref[slot] for slot in range(experts)], axis=1)
        weights = w_ref[:, :, taken].reshape(experts * sliver, block)
        out_ref[:, pl.ds(at, block)] = jnp.dot(
            hidden, weights, preferred_element_type=jnp.float32
        ).astype(out_ref.dtype)
        return carry

    lax.fori_loop(0, columns // block, one_block, 0)


def down_of(hidden, down_weight, part, columns):
    experts, rows, sliver = hidden.shape
    row_block = min(ROW_BLOCK, rows)

    def kernel(*refs):
        down_kernel(part, *refs)

    return pl.pallas_call(
        kernel,
        grid=(rows // row_block,),
        in_specs=[
            pl.BlockSpec((experts, row_block, sliver), lambda r: (0, r, 0)),
            pl.BlockSpec(memory_space=pltpu.VMEM),
        ],
        out_specs=pl.BlockSpec((row_block, columns), lambda r: (r, 0)),
        out_shape=jax.ShapeDtypeStruct((rows, columns), jnp.bfloat16),
        compiler_params=pltpu.CompilerParams(vmem_limit_bytes=DOWN_LIMIT),
        cost_estimate=pl.CostEstimate(
            flops=2 * rows * experts * sliver * columns,
            bytes_accessed=2 * (experts * sliver * columns + rows * experts * sliver + rows * columns),
            transcendentals=0,
        ),
    )(hidden, down_weight)


def local(
    tokens, gate_up_weight, down_weight, expert_ids, slot_ids, gate_values, old_place, new_place
):
    model_width = tokens.shape[1]
    rows = tokens.shape[0]
    half = model_width // 2
    ways = {name: lax.axis_size(name) for name in AXES}
    cores = 2 if ways["shard"] % 2 == 0 else 1
    x_digits = digits_of("dp", ways["dp"])
    z_digits = digits_of("expert", ways["expert"])
    y_digits = digits_of("shard", ways["shard"], cores)
    core_digits = [Digit("shard", ways["shard"], 1, cores)]
    dim_order = core_digits + x_digits[::-1] + y_digits[::-1] + z_digits[::-1]
    routes = [z_digits + y_digits + x_digits, z_digits + x_digits + y_digits]

    coefficients = slot_coefficients(expert_ids, gate_values, old_place, new_place)
    extra = jnp.concatenate(split_exact(coefficients), axis=1)
    extra = jnp.pad(extra, ((0, 0), (0, -extra.shape[1] % LANES)))
    parts = [
        jnp.concatenate([tokens[:, :half], extra], axis=1),
        tokens[:, half:],
    ]
    blocks, held = list(parts), [[], []]
    last = len(routes[0]) - 1
    for step in range(last + 2):
        if step == last:
            before_last = blocks[0]
        if step == last + 1:
            blocks[1], down_weight = lax.optimization_barrier(
                (blocks[1], fetched(down_weight, before_last))
            )
        for number in (1, 0):
            digit = (routes[number] + core_digits)[step]
            dim = sum(dim_order.index(other) < dim_order.index(digit) for other in held[number])
            blocks[number] = digit.gather(blocks[number], dim)
            held[number].append(digit)
    gathered = [block.reshape(-1, part.shape[1]) for block, part in zip(blocks, parts)]
    sums = gate_up_of(1, gathered[1], None, gate_up_weight)
    hidden = gate_up_of(0, gathered[0], sums, gate_up_weight)
    down_weight = resident(down_weight)
    results = []
    for number, route in enumerate(routes):
        block = down_of(hidden, down_weight, number, half)
        block = block.reshape([digit.size for digit in dim_order] + [rows, half])
        held = list(dim_order)
        for digit in core_digits + route[::-1]:
            block = digit.reduce(block, held.index(digit))
            held.remove(digit)
        results.append(block)
    return jnp.concatenate(results, axis=1)


def solution(mesh):
    in_specs = (
        P(AXES, None),
        P(None, None, AXES, None),
        P(None, AXES, None),
        P(AXES, None),
        P(AXES, None),
        P(AXES, None),
        P(),
        P(),
    )
    return jax.shard_map(
        local, mesh=mesh, in_specs=in_specs, out_specs=P(AXES, None), check_vma=False
    )
```

```python
import jax
import jax.numpy as jnp
from jax import lax
from jax.experimental import pallas as pl
from jax.experimental.pallas import tpu as pltpu
from jax.sharding import PartitionSpec as P

AXES = ("dp", "expert", "shard")
LANES = 128
ROW_BLOCK = 256
PIECES = 2
FETCH_LIMIT = 1 * 2**20
GATE_UP_LIMIT = 24 * 2**20
DOWN_LIMIT = 8 * 2**20


def slot_coefficients(expert_ids, gate_values, old_place, new_place):
    matches = (new_place[:, None] == old_place[None, :]).astype(jnp.float32)
    picks = (expert_ids[:, :, None] == jnp.arange(new_place.shape[0], dtype=jnp.int32)).astype(jnp.float32)
    by_expert = jnp.sum(picks * gate_values[:, :, None], axis=1)
    return jnp.sum(by_expert[:, :, None] * matches[None, :, :], axis=1)


def split_exact(value):
    pieces = []
    for _ in range(3):
        piece = lax.reduce_precision(value, exponent_bits=8, mantissa_bits=7)
        pieces.append(piece.astype(jnp.bfloat16))
        value = value - piece
    return pieces


class Digit:
    def __init__(self, name, ways, stride, size):
        self.name, self.ways, self.stride, self.size = name, ways, stride, size

    def shift(self, value, step):
        pairs = []
        for index in range(self.ways):
            digit = index // self.stride % self.size
            target = (digit + step) % self.size
            pairs.append((index, index + (target - digit) * self.stride))
        return lax.ppermute(value, self.name, pairs)

    def gather(self, block, dim):
        return jnp.stack([block] + [self.shift(block, s) for s in range(1, self.size)], axis=dim)

    def reduce(self, slots, dim):
        own = lax.index_in_dim(slots, 0, dim, keepdims=False).astype(jnp.float32)
        for s in range(1, self.size):
            sent = lax.index_in_dim(slots, s, dim, keepdims=False)
            own = own + self.shift(sent, self.size - s).astype(jnp.float32)
        return own.astype(jnp.bfloat16)


def digits_of(name, ways, low=1):
    digits, stride = [], low
    while stride < ways:
        left = ways // stride
        size = 2 if left % 2 == 0 else left
        digits.append(Digit(name, ways, stride, size))
        stride *= size
    return digits[::-1]


def resident(value):
    return pltpu.with_memory_space_constraint(value, pltpu.VMEM)


def in_hbm(value):
    return pltpu.with_memory_space_constraint(value, pltpu.HBM)


def fetch_kernel(w_ref, after_ref, out_ref, sem):
    del after_ref
    copy = pltpu.make_async_copy(w_ref, out_ref, sem)
    copy.start()
    copy.wait()


def fetched(weight, after):
    return pl.pallas_call(
        fetch_kernel,
        in_specs=[pl.BlockSpec(memory_space=pl.ANY)] * 2,
        out_specs=pl.BlockSpec(memory_space=pltpu.VMEM),
        out_shape=pltpu.VMEM(weight.shape, weight.dtype),
        scratch_shapes=[pltpu.SemaphoreType.DMA],
        compiler_params=pltpu.CompilerParams(vmem_limit_bytes=FETCH_LIMIT),
        cost_estimate=pl.CostEstimate(
            flops=0, bytes_accessed=2 * weight.size, transcendentals=0
        ),
    )(in_hbm(weight), after)


def gate_up_kernel(part, rows_ref, *refs):
    last = part == 0
    if last:
        sum_ref, w_hbm, out_ref, w_ref, sems = refs
    else:
        w_hbm, out_ref, w_ref, sems = refs
    experts, _, sliver, half = w_ref.shape
    depth = half // PIECES
    group = 2 if experts % 2 == 0 else 1
    units = 2 * sliver

    def copy(slot, piece):
        return pltpu.make_async_copy(
            w_hbm.at[pl.ds(slot, group), :, :, pl.ds(part * half + piece * depth, depth)],
            w_ref.at[pl.ds(slot, group), :, :, pl.ds(piece * depth, depth)],
            sems.at[slot // group, piece],
        )

    @pl.when(pl.program_id(0) == 0)
    def start():
        for slot in range(0, experts, group):
            for piece in range(PIECES):
                copy(slot, piece).start()

    if last:
        extra = rows_ref[:, half:].astype(jnp.float32)
        lane = lax.broadcasted_iota(jnp.int32, extra.shape, 1)
    for first in range(0, experts, group):
        columns = slice(first * units, (first + group) * units)
        pre = sum_ref[:, columns] if last else None
        for piece in range(PIECES):
            pl.when(pl.program_id(0) == 0)(copy(first, piece).wait)
            at = piece * depth
            product = lax.dot_general(
                rows_ref[:, at : at + depth],
                w_ref[first : first + group, :, :, at : at + depth].reshape(group * units, depth),
                (((1,), (1,)), ((), ())),
                preferred_element_type=jnp.float32,
            )
            pre = product if pre is None else pre + product
        if not last:
            out_ref[:, columns] = pre
            continue
        for slot in range(first, first + group):
            at = (slot - first) * units
            gate, up = pre[:, at : at + sliver], pre[:, at + sliver : at + units]
            mine = (lane == slot) | (lane == slot + experts) | (lane == slot + 2 * experts)
            weigh = jnp.sum(jnp.where(mine, extra, 0.0), axis=1, keepdims=True)
            hidden = gate / (1.0 + jnp.exp(-gate)) * up * weigh
            out_ref[slot] = hidden.astype(out_ref.dtype)


def gate_up_of(part, rows_of_part, sums, gate_up_weight):
    experts, _, sliver, model_width = gate_up_weight.shape
    half = model_width // 2
    rows, width = rows_of_part.shape
    row_block = min(ROW_BLOCK, rows)
    whole = rows == row_block
    units = experts * 2 * sliver
    operands = [rows_of_part] if sums is None else [rows_of_part, sums]
    if whole:
        operands = [resident(operand) for operand in operands]
        specs = [pl.BlockSpec(memory_space=pltpu.VMEM)] * len(operands)
    else:
        specs = [
            pl.BlockSpec((row_block, width), lambda r: (r, 0)),
            pl.BlockSpec((row_block, units), lambda r: (r, 0)),
        ][: len(operands)]
    if sums is None:
        out_spec = pl.BlockSpec((row_block, units), lambda r: (r, 0))
        out_shape = jax.ShapeDtypeStruct((rows, units), jnp.float32)
    else:
        out_spec = pl.BlockSpec((experts, row_block, sliver), lambda r: (0, r, 0))
        out_shape = jax.ShapeDtypeStruct((experts, rows, sliver), jnp.bfloat16)
    if whole:
        out_spec = pl.BlockSpec(memory_space=pltpu.VMEM)
        out_shape = pltpu.VMEM(out_shape.shape, out_shape.dtype)

    def kernel(*refs):
        gate_up_kernel(part, *refs)

    return pl.pallas_call(
        kernel,
        grid=(rows // row_block,),
        in_specs=specs + [pl.BlockSpec(memory_space=pl.ANY)],
        out_specs=out_spec,
        out_shape=out_shape,
        scratch_shapes=[
            pltpu.VMEM((experts, 2, sliver, half), gate_up_weight.dtype),
            pltpu.SemaphoreType.DMA((experts, PIECES)),
        ],
        compiler_params=pltpu.CompilerParams(vmem_limit_bytes=GATE_UP_LIMIT),
        cost_estimate=pl.CostEstimate(
            flops=2 * rows * experts * sliver * model_width,
            bytes_accessed=gate_up_weight.size + rows * model_width,
            transcendentals=rows * experts * sliver,
        ),
    )(*operands, in_hbm(gate_up_weight))


def down_kernel(part, hidden_ref, w_ref, out_ref):
    experts, _, sliver = hidden_ref.shape
    columns = out_ref.shape[1]
    block = next(size for size in (1024, 512, 384, 256, 128, columns) if columns % size == 0)

    def one_block(step, carry):
        at = pl.multiple_of(step * block, block)
        taken = pl.ds(pl.multiple_of(part * columns + step * block, block), block)
        hidden = jnp.concatenate([hidden_ref[slot] for slot in range(experts)], axis=1)
        weights = w_ref[:, :, taken].reshape(experts * sliver, block)
        out_ref[:, pl.ds(at, block)] = jnp.dot(
            hidden, weights, preferred_element_type=jnp.float32
        ).astype(out_ref.dtype)
        return carry

    lax.fori_loop(0, columns // block, one_block, 0)


def down_of(hidden, down_weight, part, columns):
    experts, rows, sliver = hidden.shape
    row_block = min(ROW_BLOCK, rows)

    def kernel(*refs):
        down_kernel(part, *refs)

    return pl.pallas_call(
        kernel,
        grid=(rows // row_block,),
        in_specs=[
            pl.BlockSpec((experts, row_block, sliver), lambda r: (0, r, 0)),
            pl.BlockSpec(memory_space=pltpu.VMEM),
        ],
        out_specs=pl.BlockSpec((row_block, columns), lambda r: (r, 0)),
        out_shape=jax.ShapeDtypeStruct((rows, columns), jnp.bfloat16),
        compiler_params=pltpu.CompilerParams(vmem_limit_bytes=DOWN_LIMIT),
        cost_estimate=pl.CostEstimate(
            flops=2 * rows * experts * sliver * columns,
            bytes_accessed=2 * (experts * sliver * columns + rows * experts * sliver + rows * columns),
            transcendentals=0,
        ),
    )(hidden, down_weight)


def local(
    tokens, gate_up_weight, down_weight, expert_ids, slot_ids, gate_values, old_place, new_place
):
    model_width = tokens.shape[1]
    rows = tokens.shape[0]
    half = model_width // 2
    ways = {name: lax.axis_size(name) for name in AXES}
    cores = 2 if ways["shard"] % 2 == 0 else 1
    x_digits = digits_of("dp", ways["dp"])
    z_digits = digits_of("expert", ways["expert"])
    y_digits = digits_of("shard", ways["shard"], cores)
    core_digits = [Digit("shard", ways["shard"], 1, cores)]
    dim_order = core_digits + x_digits[::-1] + y_digits[::-1] + z_digits[::-1]
    routes = [z_digits + y_digits + x_digits, z_digits + x_digits + y_digits]

    coefficients = slot_coefficients(expert_ids, gate_values, old_place, new_place)
    extra = jnp.concatenate(split_exact(coefficients), axis=1)
    extra = jnp.pad(extra, ((0, 0), (0, -extra.shape[1] % LANES)))
    parts = [
        jnp.concatenate([tokens[:, :half], extra], axis=1),
        tokens[:, half:],
    ]
    blocks, held = list(parts), [[], []]
    last = len(routes[0]) - 1
    for step in range(last + 2):
        if step == last:
            before_last = blocks[0]
        if step == last + 1:
            blocks[1], down_weight = lax.optimization_barrier(
                (blocks[1], fetched(down_weight, before_last))
            )
        for number in (1, 0):
            digit = (routes[number] + core_digits)[step]
            dim = sum(dim_order.index(other) < dim_order.index(digit) for other in held[number])
            blocks[number] = digit.gather(blocks[number], dim)
            held[number].append(digit)
    gathered = [block.reshape(-1, part.shape[1]) for block, part in zip(blocks, parts)]
    sums = gate_up_of(1, gathered[1], None, gate_up_weight)
    hidden = gate_up_of(0, gathered[0], sums, gate_up_weight)
    down_weight = resident(down_weight)
    results = []
    for number, route in enumerate(routes):
        block = down_of(hidden, down_weight, number, half)
        block = block.reshape([digit.size for digit in dim_order] + [rows, half])
        held = list(dim_order)
        for digit in core_digits + route[::-1]:
            block = digit.reduce(block, held.index(digit))
            held.remove(digit)
        results.append(block)
    return jnp.concatenate(results, axis=1)


def solution(mesh):
    in_specs = (
        P(AXES, None),
        P(None, None, AXES, None),
        P(None, AXES, None),
        P(AXES, None),
        P(AXES, None),
        P(AXES, None),
        P(),
        P(),
    )
    return jax.shard_map(
        local, mesh=mesh, in_specs=in_specs, out_specs=P(AXES, None), check_vma=False
    )
```

```python
import math

import jax
import jax.numpy as jnp
from jax import lax
from jax.experimental import pallas as pl
from jax.experimental.pallas import tpu as pltpu
from jax.sharding import PartitionSpec as P

AXES = ("dp", "expert", "shard")
LANES = 128
ROW_BLOCK = 256
FETCH_LIMIT = 1 * 2**20
GATE_UP_LIMIT = 8 * 2**20
DOWN_LIMIT = 8 * 2**20


def slot_coefficients(expert_ids, gate_values, old_place, new_place):
    matches = (new_place[:, None] == old_place[None, :]).astype(jnp.float32)
    picks = (expert_ids[:, :, None] == jnp.arange(new_place.shape[0], dtype=jnp.int32)).astype(jnp.float32)
    by_expert = jnp.sum(picks * gate_values[:, :, None], axis=1)
    return jnp.sum(by_expert[:, :, None] * matches[None, :, :], axis=1)


def split_exact(value):
    pieces = []
    for _ in range(3):
        piece = lax.reduce_precision(value, exponent_bits=8, mantissa_bits=7)
        pieces.append(piece.astype(jnp.bfloat16))
        value = value - piece
    return pieces


class Digit:
    def __init__(self, name, ways, stride, size):
        self.name, self.ways, self.stride, self.size = name, ways, stride, size

    def shift(self, value, step):
        pairs = []
        for index in range(self.ways):
            digit = index // self.stride % self.size
            target = (digit + step) % self.size
            pairs.append((index, index + (target - digit) * self.stride))
        return lax.ppermute(value, self.name, pairs)

    def gather(self, block, dim):
        return jnp.stack([block] + [self.shift(block, s) for s in range(1, self.size)], axis=dim)

    def reduce(self, slots, dim):
        own = lax.index_in_dim(slots, 0, dim, keepdims=False).astype(jnp.float32)
        for s in range(1, self.size):
            sent = lax.index_in_dim(slots, s, dim, keepdims=False)
            own = own + self.shift(sent, self.size - s).astype(jnp.float32)
        return own.astype(jnp.bfloat16)


def digits_of(name, ways, low=1):
    digits, stride = [], low
    while stride < ways:
        left = ways // stride
        size = 2 if left % 2 == 0 else left
        digits.append(Digit(name, ways, stride, size))
        stride *= size
    return digits[::-1]


def resident(value):
    return pltpu.with_memory_space_constraint(value, pltpu.VMEM)


def in_hbm(value):
    return pltpu.with_memory_space_constraint(value, pltpu.HBM)


def fetch_kernel(take, w_ref, after_ref, out_ref, sem):
    del after_ref
    copy = pltpu.make_async_copy(take(w_ref), out_ref, sem)
    copy.start()
    copy.wait()


def fetched(weight, take, shape, after):
    def kernel(*refs):
        fetch_kernel(take, *refs)

    return pl.pallas_call(
        kernel,
        in_specs=[pl.BlockSpec(memory_space=pl.ANY)] * 2,
        out_specs=pl.BlockSpec(memory_space=pltpu.VMEM),
        out_shape=pltpu.VMEM(shape, weight.dtype),
        scratch_shapes=[pltpu.SemaphoreType.DMA],
        compiler_params=pltpu.CompilerParams(vmem_limit_bytes=FETCH_LIMIT),
        cost_estimate=pl.CostEstimate(
            flops=0, bytes_accessed=4 * math.prod(shape), transcendentals=0
        ),
    )(in_hbm(weight), after)


def gate_up_kernel(last, take, rows_ref, *refs):
    if last:
        sum_ref, w_ref, next_hbm, out_ref, next_ref, sem = refs
    else:
        w_ref, next_hbm, out_ref, next_ref, sem = refs
    experts, _, sliver, half = w_ref.shape
    group = 2 if experts % 2 == 0 else 1
    units = 2 * sliver
    copy = pltpu.make_async_copy(take(next_hbm), next_ref, sem)
    pl.when(pl.program_id(0) == 0)(copy.start)
    if last:
        extra = rows_ref[:, half:].astype(jnp.float32)
        lane = lax.broadcasted_iota(jnp.int32, extra.shape, 1)
    for first in range(0, experts, group):
        columns = slice(first * units, (first + group) * units)
        pre = lax.dot_general(
            rows_ref[:, :half],
            w_ref[first : first + group].reshape(group * units, half),
            (((1,), (1,)), ((), ())),
            preferred_element_type=jnp.float32,
        )
        if not last:
            out_ref[:, columns] = pre
            continue
        pre += sum_ref[:, columns]
        for slot in range(first, first + group):
            at = (slot - first) * units
            gate, up = pre[:, at : at + sliver], pre[:, at + sliver : at + units]
            mine = (lane == slot) | (lane == slot + experts) | (lane == slot + 2 * experts)
            weigh = jnp.sum(jnp.where(mine, extra, 0.0), axis=1, keepdims=True)
            hidden = gate / (1.0 + jnp.exp(-gate)) * up * weigh
            out_ref[slot] = hidden.astype(out_ref.dtype)
    pl.when(pl.program_id(0) == 0)(copy.wait)


def gate_up_of(rows_of_part, sums, weights, next_weight, take, next_shape):
    experts, _, sliver, half = weights.shape
    rows, width = rows_of_part.shape
    row_block = min(ROW_BLOCK, rows)
    whole = rows == row_block
    last = sums is not None
    units = experts * 2 * sliver
    operands = [rows_of_part, sums] if last else [rows_of_part]
    if whole:
        operands = [resident(operand) for operand in operands]
        specs = [pl.BlockSpec(memory_space=pltpu.VMEM)] * len(operands)
    else:
        specs = [
            pl.BlockSpec((row_block, width), lambda r: (r, 0)),
            pl.BlockSpec((row_block, units), lambda r: (r, 0)),
        ][: len(operands)]
    if last:
        out_spec = pl.BlockSpec((experts, row_block, sliver), lambda r: (0, r, 0))
        out_shape = jax.ShapeDtypeStruct((experts, rows, sliver), jnp.bfloat16)
    else:
        out_spec = pl.BlockSpec((row_block, units), lambda r: (r, 0))
        out_shape = jax.ShapeDtypeStruct((rows, units), jnp.float32)
    if whole:
        out_spec = pl.BlockSpec(memory_space=pltpu.VMEM)
        out_shape = pltpu.VMEM(out_shape.shape, out_shape.dtype)

    def kernel(*refs):
        gate_up_kernel(last, take, *refs)

    return pl.pallas_call(
        kernel,
        grid=(rows // row_block,),
        in_specs=specs
        + [pl.BlockSpec(memory_space=pltpu.VMEM), pl.BlockSpec(memory_space=pl.ANY)],
        out_specs=[out_spec, pl.BlockSpec(memory_space=pltpu.VMEM)],
        out_shape=[out_shape, pltpu.VMEM(next_shape, next_weight.dtype)],
        scratch_shapes=[pltpu.SemaphoreType.DMA],
        compiler_params=pltpu.CompilerParams(vmem_limit_bytes=GATE_UP_LIMIT),
        cost_estimate=pl.CostEstimate(
            flops=4 * rows * experts * sliver * half,
            bytes_accessed=2 * math.prod(next_shape) + 4 * rows * units,
            transcendentals=rows * experts * sliver,
        ),
    )(*operands, resident(weights), in_hbm(next_weight))


def down_kernel(part, hidden_ref, w_ref, out_ref):
    experts, _, sliver = hidden_ref.shape
    columns = out_ref.shape[1]
    block = next(size for size in (1024, 512, 384, 256, 128, columns) if columns % size == 0)

    def one_block(step, carry):
        at = pl.multiple_of(step * block, block)
        taken = pl.ds(pl.multiple_of(part * columns + step * block, block), block)
        hidden = jnp.concatenate([hidden_ref[slot] for slot in range(experts)], axis=1)
        weights = w_ref[:, :, taken].reshape(experts * sliver, block)
        out_ref[:, pl.ds(at, block)] = jnp.dot(
            hidden, weights, preferred_element_type=jnp.float32
        ).astype(out_ref.dtype)
        return carry

    lax.fori_loop(0, columns // block, one_block, 0)


def down_of(hidden, down_weight, part, columns):
    experts, rows, sliver = hidden.shape
    row_block = min(ROW_BLOCK, rows)

    def kernel(*refs):
        down_kernel(part, *refs)

    return pl.pallas_call(
        kernel,
        grid=(rows // row_block,),
        in_specs=[
            pl.BlockSpec((experts, row_block, sliver), lambda r: (0, r, 0)),
            pl.BlockSpec(memory_space=pltpu.VMEM),
        ],
        out_specs=pl.BlockSpec((row_block, columns), lambda r: (r, 0)),
        out_shape=jax.ShapeDtypeStruct((rows, columns), jnp.bfloat16),
        compiler_params=pltpu.CompilerParams(vmem_limit_bytes=DOWN_LIMIT),
        cost_estimate=pl.CostEstimate(
            flops=2 * rows * experts * sliver * columns,
            bytes_accessed=2 * (experts * sliver * columns + rows * experts * sliver + rows * columns),
            transcendentals=0,
        ),
    )(hidden, down_weight)


def local(
    tokens, gate_up_weight, down_weight, expert_ids, slot_ids, gate_values, old_place, new_place
):
    model_width = tokens.shape[1]
    rows = tokens.shape[0]
    half = model_width // 2
    ways = {name: lax.axis_size(name) for name in AXES}
    cores = 2 if ways["shard"] % 2 == 0 else 1
    x_digits = digits_of("dp", ways["dp"])
    z_digits = digits_of("expert", ways["expert"])
    y_digits = digits_of("shard", ways["shard"], cores)
    core_digits = [Digit("shard", ways["shard"], 1, cores)]
    dim_order = core_digits + x_digits[::-1] + y_digits[::-1] + z_digits[::-1]
    routes = [z_digits + y_digits + x_digits, z_digits + x_digits + y_digits]

    coefficients = slot_coefficients(expert_ids, gate_values, old_place, new_place)
    extra = jnp.concatenate(split_exact(coefficients), axis=1)
    extra = jnp.pad(extra, ((0, 0), (0, -extra.shape[1] % LANES)))
    parts = [
        jnp.concatenate([tokens[:, :half], extra], axis=1),
        tokens[:, half:],
    ]
    half_shape = gate_up_weight.shape[:3] + (half,)

    def take_first(ref):
        return ref.at[:, :, :, pl.ds(0, half)]

    def take_second(ref):
        return ref.at[:, :, :, pl.ds(half, half)]

    blocks, held = list(parts), [[], []]
    last = len(routes[0]) - 1
    for step in range(last + 2):
        if step == last:
            before_last = blocks[0]
        if step == last + 1:
            first_weights = fetched(gate_up_weight, take_second, half_shape, before_last)
            blocks[1], first_weights = lax.optimization_barrier((blocks[1], first_weights))
        for number in (1, 0):
            digit = (routes[number] + core_digits)[step]
            dim = sum(dim_order.index(other) < dim_order.index(digit) for other in held[number])
            blocks[number] = digit.gather(blocks[number], dim)
            held[number].append(digit)
    gathered = [block.reshape(-1, part.shape[1]) for block, part in zip(blocks, parts)]
    sums, weights = gate_up_of(
        gathered[1], None, first_weights, gate_up_weight, take_first, half_shape
    )
    hidden, down_weight = gate_up_of(
        gathered[0], sums, weights, down_weight, lambda ref: ref, down_weight.shape
    )
    down_weight = resident(down_weight)
    results = []
    for number, route in enumerate(routes):
        block = down_of(hidden, down_weight, number, half)
        block = block.reshape([digit.size for digit in dim_order] + [rows, half])
        held = list(dim_order)
        for digit in core_digits + route[::-1]:
            block = digit.reduce(block, held.index(digit))
            held.remove(digit)
        results.append(block)
    return jnp.concatenate(results, axis=1)


def solution(mesh):
    in_specs = (
        P(AXES, None),
        P(None, None, AXES, None),
        P(None, AXES, None),
        P(AXES, None),
        P(AXES, None),
        P(AXES, None),
        P(),
        P(),
    )
    return jax.shard_map(
        local, mesh=mesh, in_specs=in_specs, out_specs=P(AXES, None), check_vma=False
    )
```

```python
import math

import jax
import jax.numpy as jnp
from jax import lax
from jax.experimental import pallas as pl
from jax.experimental.pallas import tpu as pltpu
from jax.sharding import PartitionSpec as P

AXES = ("dp", "expert", "shard")
LANES = 128
ROW_BLOCK = 256
FETCH_LIMIT = 1 * 2**20
GATE_UP_LIMIT = 8 * 2**20
DOWN_LIMIT = 8 * 2**20


def slot_coefficients(expert_ids, gate_values, old_place, new_place):
    matches = (new_place[:, None] == old_place[None, :]).astype(jnp.float32)
    picks = (expert_ids[:, :, None] == jnp.arange(new_place.shape[0], dtype=jnp.int32)).astype(jnp.float32)
    by_expert = jnp.sum(picks * gate_values[:, :, None], axis=1)
    return jnp.sum(by_expert[:, :, None] * matches[None, :, :], axis=1)


def split_exact(value):
    pieces = []
    for _ in range(3):
        piece = lax.reduce_precision(value, exponent_bits=8, mantissa_bits=7)
        pieces.append(piece.astype(jnp.bfloat16))
        value = value - piece
    return pieces


class Digit:
    def __init__(self, name, ways, stride, size):
        self.name, self.ways, self.stride, self.size = name, ways, stride, size

    def shift(self, value, step):
        pairs = []
        for index in range(self.ways):
            digit = index // self.stride % self.size
            target = (digit + step) % self.size
            pairs.append((index, index + (target - digit) * self.stride))
        return lax.ppermute(value, self.name, pairs)

    def gather(self, block, dim):
        return jnp.stack([block] + [self.shift(block, s) for s in range(1, self.size)], axis=dim)

    def reduce(self, slots, dim):
        own = lax.index_in_dim(slots, 0, dim, keepdims=False).astype(jnp.float32)
        for s in range(1, self.size):
            sent = lax.index_in_dim(slots, s, dim, keepdims=False)
            own = own + self.shift(sent, self.size - s).astype(jnp.float32)
        return own.astype(jnp.bfloat16)


def digits_of(name, ways, low=1):
    digits, stride = [], low
    while stride < ways:
        left = ways // stride
        size = 2 if left % 2 == 0 else left
        digits.append(Digit(name, ways, stride, size))
        stride *= size
    return digits[::-1]


def resident(value):
    return pltpu.with_memory_space_constraint(value, pltpu.VMEM)


def in_hbm(value):
    return pltpu.with_memory_space_constraint(value, pltpu.HBM)


def fetch_kernel(take, w_ref, after_ref, out_ref, sem):
    del after_ref
    copy = pltpu.make_async_copy(take(w_ref), out_ref, sem)
    copy.start()
    copy.wait()


def fetched(weight, take, shape, after):
    def kernel(*refs):
        fetch_kernel(take, *refs)

    return pl.pallas_call(
        kernel,
        in_specs=[pl.BlockSpec(memory_space=pl.ANY)] * 2,
        out_specs=pl.BlockSpec(memory_space=pltpu.VMEM),
        out_shape=pltpu.VMEM(shape, weight.dtype),
        scratch_shapes=[pltpu.SemaphoreType.DMA],
        compiler_params=pltpu.CompilerParams(vmem_limit_bytes=FETCH_LIMIT),
        cost_estimate=pl.CostEstimate(
            flops=0, bytes_accessed=4 * math.prod(shape), transcendentals=0
        ),
    )(in_hbm(weight), after)


def gate_up_kernel(last, take, pieces, *refs):
    row_refs, refs = refs[:2], refs[2:]
    if last:
        sum_ref, refs = refs[0], refs[1:]
    w_refs, (next_hbm, out_ref, next_ref, sem) = refs[:pieces], refs[pieces:]
    held, _, sliver, half = w_refs[0].shape
    experts = held * pieces
    group = experts // 2 if experts % 2 == 0 else experts
    units = 2 * sliver
    depth = half // 2
    copy = pltpu.make_async_copy(take(next_hbm), next_ref, sem)
    pl.when(pl.program_id(0) == 0)(copy.start)
    if last:
        extra = row_refs[1][:, depth:].astype(jnp.float32)
        lane = lax.broadcasted_iota(jnp.int32, extra.shape, 1)
    for first in range(0, experts, group):
        columns = slice(first * units, (first + group) * units)
        w_ref, at_slot = w_refs[first // held], first % held
        pre = sum_ref[:, columns] if last else None
        for number, row_ref in enumerate(row_refs):
            product = lax.dot_general(
                row_ref[:, :depth],
                w_ref[
                    at_slot : at_slot + group, :, :, number * depth : (number + 1) * depth
                ].reshape(group * units, depth),
                (((1,), (1,)), ((), ())),
                preferred_element_type=jnp.float32,
            )
            pre = product if pre is None else pre + product
        if not last:
            out_ref[:, columns] = pre
            continue
        for slot in range(first, first + group):
            at = (slot - first) * units
            gate, up = pre[:, at : at + sliver], pre[:, at + sliver : at + units]
            mine = (lane == slot) | (lane == slot + experts) | (lane == slot + 2 * experts)
            weigh = jnp.sum(jnp.where(mine, extra, 0.0), axis=1, keepdims=True)
            hidden = (0.5 * gate) * (1.0 + jnp.tanh(0.5 * gate)) * up * weigh
            out_ref[slot] = hidden.astype(out_ref.dtype)
    pl.when(pl.program_id(0) == 0)(copy.wait)


def gate_up_of(row_parts, sums, weights, next_weight, take, next_shape):
    held, _, sliver, half = weights[0].shape
    pieces = len(weights)
    experts = held * pieces
    rows = row_parts[0].shape[0]
    row_block = min(ROW_BLOCK, rows)
    whole = rows == row_block
    last = sums is not None
    units = experts * 2 * sliver
    operands = list(row_parts) + ([sums] if last else [])
    if whole:
        specs = [pl.BlockSpec(memory_space=pltpu.VMEM)] * len(operands)
        operands = [resident(operand) for operand in operands]
    else:
        specs = [
            pl.BlockSpec((row_block, operand.shape[1]), lambda r: (r, 0)) for operand in operands
        ]
    if last:
        out_spec = pl.BlockSpec((experts, row_block, sliver), lambda r: (0, r, 0))
        out_shape = jax.ShapeDtypeStruct((experts, rows, sliver), jnp.bfloat16)
    else:
        out_spec = pl.BlockSpec((row_block, units), lambda r: (r, 0))
        out_shape = jax.ShapeDtypeStruct((rows, units), jnp.float32)
    if whole:
        out_spec = pl.BlockSpec(memory_space=pltpu.VMEM)
        out_shape = pltpu.VMEM(out_shape.shape, out_shape.dtype)

    def kernel(*refs):
        gate_up_kernel(last, take, pieces, *refs)

    return pl.pallas_call(
        kernel,
        grid=(rows // row_block,),
        in_specs=specs
        + [pl.BlockSpec(memory_space=pltpu.VMEM)] * pieces
        + [pl.BlockSpec(memory_space=pl.ANY)],
        out_specs=[out_spec, pl.BlockSpec(memory_space=pltpu.VMEM)],
        out_shape=[out_shape, pltpu.VMEM(next_shape, next_weight.dtype)],
        scratch_shapes=[pltpu.SemaphoreType.DMA],
        compiler_params=pltpu.CompilerParams(vmem_limit_bytes=GATE_UP_LIMIT),
        cost_estimate=pl.CostEstimate(
            flops=4 * rows * experts * sliver * half,
            bytes_accessed=2 * math.prod(next_shape) + 4 * rows * units,
            transcendentals=rows * experts * sliver,
        ),
    )(*operands, *(resident(weight) for weight in weights), in_hbm(next_weight))


def down_kernel(part, hidden_ref, w_ref, out_ref):
    experts, _, sliver = hidden_ref.shape
    columns = out_ref.shape[1]
    block = next(size for size in (1536, 1024, 512, 384, 256, 128, columns) if columns % size == 0)

    def one_block(step, carry):
        at = pl.multiple_of(step * block, block)
        taken = pl.ds(pl.multiple_of(part * columns + step * block, block), block)
        hidden = jnp.concatenate([hidden_ref[slot] for slot in range(experts)], axis=1)
        weights = w_ref[:, :, taken].reshape(experts * sliver, block)
        out_ref[:, pl.ds(at, block)] = jnp.dot(
            hidden, weights, preferred_element_type=jnp.float32
        ).astype(out_ref.dtype)
        return carry

    lax.fori_loop(0, columns // block, one_block, 0)


def down_of(hidden, down_weight, part, columns):
    experts, rows, sliver = hidden.shape
    row_block = min(ROW_BLOCK, rows)

    def kernel(*refs):
        down_kernel(part, *refs)

    return pl.pallas_call(
        kernel,
        grid=(rows // row_block,),
        in_specs=[
            pl.BlockSpec((experts, row_block, sliver), lambda r: (0, r, 0)),
            pl.BlockSpec(memory_space=pltpu.VMEM),
        ],
        out_specs=pl.BlockSpec((row_block, columns), lambda r: (r, 0)),
        out_shape=jax.ShapeDtypeStruct((rows, columns), jnp.bfloat16),
        compiler_params=pltpu.CompilerParams(vmem_limit_bytes=DOWN_LIMIT),
        cost_estimate=pl.CostEstimate(
            flops=2 * rows * experts * sliver * columns,
            bytes_accessed=2 * (experts * sliver * columns + rows * experts * sliver + rows * columns),
            transcendentals=0,
        ),
    )(hidden, down_weight)


def local(
    tokens, gate_up_weight, down_weight, expert_ids, slot_ids, gate_values, old_place, new_place
):
    model_width = tokens.shape[1]
    rows = tokens.shape[0]
    half = model_width // 2
    ways = {name: lax.axis_size(name) for name in AXES}
    cores = 2 if ways["shard"] % 2 == 0 else 1
    x_digits = digits_of("dp", ways["dp"])
    z_digits = digits_of("expert", ways["expert"])
    y_digits = digits_of("shard", ways["shard"], cores)
    core_digits = [Digit("shard", ways["shard"], 1, cores)]
    dim_order = core_digits + x_digits[::-1] + y_digits[::-1] + z_digits[::-1]
    routes = [y_digits + x_digits, x_digits + y_digits]
    quarter = half // 2

    def gather(block, digit, held):
        dim = sum(dim_order.index(other) < dim_order.index(digit) for other in held)
        return digit.gather(block, dim)

    def reduce(block, digit, held):
        return digit.reduce(block, sum(other in held for other in dim_order[: dim_order.index(digit)]))

    coefficients = slot_coefficients(expert_ids, gate_values, old_place, new_place)
    extra = jnp.concatenate(split_exact(coefficients), axis=1)
    extra = jnp.pad(extra, ((0, 0), (0, -extra.shape[1] % LANES)))

    experts = gate_up_weight.shape[0]
    pieces = 2 if experts % 2 == 0 else 1
    half_shape = gate_up_weight.shape[:3] + (half,)
    piece_shape = (experts // pieces,) + half_shape[1:]

    def take_piece(number):
        slots = pl.ds(number * (experts // pieces), experts // pieces)
        return lambda ref: ref.at[slots, :, :, pl.ds(half, half)]

    def take_first(ref):
        return ref.at[:, :, :, pl.ds(0, half)]

    halves = [jnp.concatenate([tokens[:, :half], extra], axis=1), tokens[:, half:]]
    first_weights, held = [], []
    for step, digit in enumerate(z_digits):
        halves = [gather(block, digit, held) for block in halves]
        held.append(digit)
        if step == 0:
            fresh = fetched(gate_up_weight, take_piece(0), piece_shape, halves[1])
            halves[0], fresh = lax.optimization_barrier((halves[0], fresh))
            first_weights.append(fresh)
    quarters = [[block[..., :quarter], block[..., quarter:]] for block in halves]
    for step in range(len(routes[0])):
        for number in (1, 0):
            for side in (0, 1):
                done = held + routes[side][:step]
                quarters[number][side] = gather(quarters[number][side], routes[side][step], done)
    for piece in range(len(first_weights), pieces):
        fresh = fetched(gate_up_weight, take_piece(piece), piece_shape, quarters[1][0])
        quarters[0][0], fresh = lax.optimization_barrier((quarters[0][0], fresh))
        first_weights.append(fresh)
    for digit in core_digits:
        quarters = [
            [gather(block, digit, dim_order[len(core_digits) :]) for block in pair]
            for pair in quarters
        ]
    gathered = [[block.reshape(-1, block.shape[-1]) for block in pair] for pair in quarters]
    sums, weights = gate_up_of(
        gathered[1], None, first_weights, gate_up_weight, take_first, half_shape
    )
    hidden, down_weight = gate_up_of(
        gathered[0], sums, [weights], down_weight, lambda ref: ref, down_weight.shape
    )
    down_weight = resident(down_weight)
    order = [(1, 0), (1, 1), (0, 0), (0, 1)]
    blocks, left = {}, list(dim_order)
    for digit in core_digits:
        left.remove(digit)
    for place, (number, side) in enumerate(order):
        if place >= 2:
            before = order[place - 2]
            hidden, blocks[before] = lax.optimization_barrier((hidden, blocks[before]))
        block = down_of(hidden, down_weight, 2 * number + side, quarter)
        block = block.reshape([digit.size for digit in dim_order] + [rows, quarter])
        for digit in core_digits:
            block = reduce(block, digit, dim_order)
        blocks[number, side] = block
    blocks = lax.optimization_barrier(blocks)
    pairs = {number: [blocks[number, side] for side in (0, 1)] for number in (0, 1)}
    helds = [list(left), list(left)]

    def after(first, second):
        return lax.optimization_barrier((first, second))[0]

    for step in range(len(left)):
        waiting = pairs[0]
        for number in (1, 0):
            if step == len(routes[0]):
                pairs[number] = [jnp.concatenate(pairs[number], axis=-1)]
            moved = []
            for side, block in enumerate(pairs[number]):
                digit = (routes[side][::-1] + z_digits[::-1])[step]
                moved.append(reduce(block, digit, helds[side]))
            pairs[number] = after(moved, waiting) if number else moved
        for side in (0, 1):
            helds[side].remove((routes[side][::-1] + z_digits[::-1])[step])
    return jnp.concatenate([pairs[number][0] for number in (0, 1)], axis=1)


def solution(mesh):
    in_specs = (
        P(AXES, None),
        P(None, None, AXES, None),
        P(None, AXES, None),
        P(AXES, None),
        P(AXES, None),
        P(AXES, None),
        P(),
        P(),
    )
    return jax.shard_map(
        local, mesh=mesh, in_specs=in_specs, out_specs=P(AXES, None), check_vma=False
    )
```

```python
import itertools
import math

import jax
import jax.numpy as jnp
from jax import lax
from jax.experimental import pallas as pl
from jax.experimental.pallas import tpu as pltpu
from jax.sharding import PartitionSpec as P

AXES = ("dp", "expert", "shard")
LANES = 128
ROW_BLOCK = 256
FETCH_LIMIT = 1 * 2**20
GATE_UP_LIMIT = 8 * 2**20
DOWN_LIMIT = 8 * 2**20


def slot_coefficients(expert_ids, gate_values, old_place, new_place):
    matches = (new_place[:, None] == old_place[None, :]).astype(jnp.float32)
    picks = (expert_ids[:, :, None] == jnp.arange(new_place.shape[0], dtype=jnp.int32)).astype(jnp.float32)
    by_expert = jnp.sum(picks * gate_values[:, :, None], axis=1)
    return jnp.sum(by_expert[:, :, None] * matches[None, :, :], axis=1)


def split_exact(value):
    pieces = []
    for _ in range(3):
        piece = lax.reduce_precision(value, exponent_bits=8, mantissa_bits=7)
        pieces.append(piece.astype(jnp.bfloat16))
        value = value - piece
    return pieces


class Digit:
    def __init__(self, name, stride, size):
        self.name, self.stride, self.size = name, stride, size


class Exchange:
    def __init__(self, ways, digits):
        self.ways, self.digits = ways, digits
        self.size = digits[0].size

    def shift(self, value, step):
        places = list(itertools.product(*(range(self.ways[name]) for name in AXES)))
        pairs = []
        for place in places:
            digit = self.digits[place[-1] % len(self.digits)]
            axis = AXES.index(digit.name)
            value_of = place[axis] // digit.stride % digit.size
            target = list(place)
            target[axis] += ((value_of + step) % digit.size - value_of) * digit.stride
            pairs.append((places.index(place), places.index(tuple(target))))
        return lax.ppermute(value, AXES, pairs)

    def arriving(self, block):
        return [self.shift(block, s) for s in range(1, self.size)]

    def gather(self, block):
        return jnp.stack([block] + self.arriving(block))

    def reduce(self, slots):
        own = slots[0].astype(jnp.float32)
        for s in range(1, self.size):
            own = own + self.shift(slots[s], self.size - s).astype(jnp.float32)
        return own.astype(jnp.bfloat16)


def digits_of(name, ways, low=1):
    digits, stride = [], low
    while stride < ways:
        left = ways // stride
        size = 2 if left % 2 == 0 else left
        digits.append(Digit(name, stride, size))
        stride *= size
    return digits[::-1]


def resident(value):
    return pltpu.with_memory_space_constraint(value, pltpu.VMEM)


def in_hbm(value):
    return pltpu.with_memory_space_constraint(value, pltpu.HBM)


def fetch_kernel(take, w_ref, after_ref, out_ref, sem):
    del after_ref
    copy = pltpu.make_async_copy(take(w_ref), out_ref, sem)
    copy.start()
    copy.wait()


def fetched(weight, take, shape, after):
    def kernel(*refs):
        fetch_kernel(take, *refs)

    return pl.pallas_call(
        kernel,
        in_specs=[pl.BlockSpec(memory_space=pl.ANY)] * 2,
        out_specs=pl.BlockSpec(memory_space=pltpu.VMEM),
        out_shape=pltpu.VMEM(shape, weight.dtype),
        scratch_shapes=[pltpu.SemaphoreType.DMA],
        compiler_params=pltpu.CompilerParams(vmem_limit_bytes=FETCH_LIMIT),
        cost_estimate=pl.CostEstimate(
            flops=0, bytes_accessed=4 * math.prod(shape), transcendentals=0
        ),
    )(in_hbm(weight), after)


def gate_up_kernel(last, take, pieces, row_ref, *refs):
    sum_refs, refs = (refs[:pieces], refs[pieces:]) if last else ((), refs)
    w_refs, (next_hbm, out_ref, next_ref, sem) = refs[:pieces], refs[pieces:]
    held, _, sliver, half = w_refs[0].shape
    experts = held * pieces
    units = 2 * sliver
    width = row_ref.shape[1] // 2
    depth = half // 2
    spans = [(0, half, 0)] if width == depth else [(0, depth, 0), (width, depth, depth)]
    copy = pltpu.make_async_copy(take(next_hbm), next_ref, sem)
    pl.when(pl.program_id(0) == 0)(copy.start)
    if last:
        extra = row_ref[:, depth:width].astype(jnp.float32)
        lane = lax.broadcasted_iota(jnp.int32, extra.shape, 1)
    for piece, w_ref in enumerate(w_refs):
        pre = sum_refs[piece][...] if last else None
        for at, span, w_at in spans:
            product = lax.dot_general(
                row_ref[:, at : at + span],
                w_ref[:, :, :, w_at : w_at + span].reshape(held * units, span),
                (((1,), (1,)), ((), ())),
                preferred_element_type=jnp.float32,
            )
            pre = product if pre is None else pre + product
        if not last:
            out_ref[...] = pre
            continue
        for number in range(held):
            slot, at = piece * held + number, number * units
            gate, up = pre[:, at : at + sliver], pre[:, at + sliver : at + units]
            mine = (lane == slot) | (lane == slot + experts) | (lane == slot + 2 * experts)
            weigh = jnp.sum(jnp.where(mine, extra, 0.0), axis=1, keepdims=True)
            hidden = (0.5 * gate) * (1.0 + jnp.tanh(0.5 * gate)) * up * weigh
            out_ref[slot] = hidden.astype(out_ref.dtype)
    pl.when(pl.program_id(0) == 0)(copy.wait)


def gate_up_of(row_part, sums, weights, next_weight, take, next_shape):
    held, _, sliver, half = weights[0].shape
    pieces = len(weights)
    experts = held * pieces
    rows = row_part.shape[0]
    row_block = min(ROW_BLOCK, rows)
    whole = rows == row_block
    last = sums is not None
    units = experts * 2 * sliver
    operands = [row_part] + (sums if last else [])
    if whole:
        specs = [pl.BlockSpec(memory_space=pltpu.VMEM)] * len(operands)
        operands = [resident(operand) for operand in operands]
    else:
        specs = [
            pl.BlockSpec((row_block, operand.shape[1]), lambda r: (r, 0)) for operand in operands
        ]
    if last:
        out_spec = pl.BlockSpec((experts, row_block, sliver), lambda r: (0, r, 0))
        out_shape = jax.ShapeDtypeStruct((experts, rows, sliver), jnp.bfloat16)
    else:
        out_spec = pl.BlockSpec((row_block, units), lambda r: (r, 0))
        out_shape = jax.ShapeDtypeStruct((rows, units), jnp.float32)
    if whole:
        out_spec = pl.BlockSpec(memory_space=pltpu.VMEM)
        out_shape = pltpu.VMEM(out_shape.shape, out_shape.dtype)

    def kernel(*refs):
        gate_up_kernel(last, take, pieces, *refs)

    return pl.pallas_call(
        kernel,
        grid=(rows // row_block,),
        in_specs=specs
        + [pl.BlockSpec(memory_space=pltpu.VMEM)] * pieces
        + [pl.BlockSpec(memory_space=pl.ANY)],
        out_specs=[out_spec, pl.BlockSpec(memory_space=pltpu.VMEM)],
        out_shape=[out_shape, pltpu.VMEM(next_shape, next_weight.dtype)],
        scratch_shapes=[pltpu.SemaphoreType.DMA],
        compiler_params=pltpu.CompilerParams(vmem_limit_bytes=GATE_UP_LIMIT),
        cost_estimate=pl.CostEstimate(
            flops=4 * rows * experts * sliver * half,
            bytes_accessed=2 * math.prod(next_shape) + 4 * rows * units,
            transcendentals=rows * experts * sliver,
        ),
    )(*operands, *(resident(weight) for weight in weights), in_hbm(next_weight))


def down_kernel(part_ref, hidden_ref, w_ref, out_ref):
    experts, _, sliver = hidden_ref.shape
    columns = out_ref.shape[1]
    taken = pl.ds(pl.multiple_of(part_ref[0] * columns, columns), columns)
    hidden = jnp.concatenate([hidden_ref[slot] for slot in range(experts)], axis=1)
    weights = w_ref[:, :, taken].reshape(experts * sliver, columns)
    out_ref[...] = jnp.dot(hidden, weights, preferred_element_type=jnp.float32).astype(
        out_ref.dtype
    )


def down_of(hidden, down_weight, part, columns):
    experts, rows, sliver = hidden.shape
    row_block = min(ROW_BLOCK, rows)
    return pl.pallas_call(
        down_kernel,
        grid=(rows // row_block,),
        in_specs=[
            pl.BlockSpec(memory_space=pltpu.SMEM),
            pl.BlockSpec((experts, row_block, sliver), lambda r: (0, r, 0)),
            pl.BlockSpec(memory_space=pltpu.VMEM),
        ],
        out_specs=pl.BlockSpec((row_block, columns), lambda r: (r, 0)),
        out_shape=jax.ShapeDtypeStruct((rows, columns), jnp.bfloat16),
        compiler_params=pltpu.CompilerParams(vmem_limit_bytes=DOWN_LIMIT),
        cost_estimate=pl.CostEstimate(
            flops=2 * rows * experts * sliver * columns,
            bytes_accessed=2 * (experts * sliver * columns + rows * experts * sliver + rows * columns),
            transcendentals=0,
        ),
    )(part.reshape(1).astype(jnp.int32), hidden, down_weight)


def after(value, other):
    return lax.optimization_barrier((value, other))[0]


def local(
    tokens, gate_up_weight, down_weight, expert_ids, slot_ids, gate_values, old_place, new_place
):
    rows, model_width = tokens.shape
    half, quarter = model_width // 2, model_width // 4
    experts = gate_up_weight.shape[0]
    ways = {name: lax.axis_size(name) for name in AXES}
    core = Exchange(ways, [Digit("shard", 1, 2)])
    along_z = [Exchange(ways, [digit]) for digit in digits_of("expert", ways["expert"])]
    route = digits_of("shard", ways["shard"], 2) + digits_of("dp", ways["dp"])
    along_xy = [Exchange(ways, list(pair)) for pair in zip(route, route[::-1])]
    core_index = lax.axis_index("shard") % 2
    is_first = core_index == 0
    hops = len(along_xy)

    def own_first(low, high):
        return jnp.where(is_first, low, high), jnp.where(is_first, high, low)

    def as_own(block):
        return jnp.flip(block.transpose(*range(hops)[::-1], *range(hops, block.ndim)), hops)

    coefficients = slot_coefficients(expert_ids, gate_values, old_place, new_place)
    extra = jnp.concatenate(split_exact(coefficients), axis=1)
    extra = jnp.pad(extra, ((0, 0), (0, -extra.shape[1] % LANES)))

    pieces = 2 if experts % 2 == 0 else 1
    held = experts // pieces
    piece_shape = (held,) + gate_up_weight.shape[1:3] + (half,)

    def take(number, piece):
        slots = pl.ds(piece * held, held)
        return lambda ref: ref.at[slots, :, :, pl.ds(number * half, half)]

    blocks = [
        jnp.concatenate([tokens[:, :quarter], extra, tokens[:, quarter:half], extra], axis=1),
        tokens[:, half:],
    ]
    first_weights = []

    def fetch(blocks):
        if len(first_weights) < pieces:
            place = take(1, len(first_weights))
            fresh = fetched(gate_up_weight, place, piece_shape, blocks[1])
            waiting, fresh = lax.optimization_barrier((blocks[0], fresh))
            first_weights.append(fresh)
            return [waiting, blocks[1]]
        return blocks

    def split(block):
        side = block.shape[-1] // 2
        kept, sent = own_first(block[..., :side], block[..., side:])
        return jnp.stack([kept, core.shift(sent, 1)])

    def both_sides(block):
        sides = own_first(block, as_own(core.shift(block, 1)))
        block = jnp.concatenate(sides, axis=-1)
        return block.reshape(-1, block.shape[-1])

    def in_step(step, blocks):
        moved = step(blocks[1])
        return [step(blocks[0]), after(moved, blocks[0])]

    for number, exchange in enumerate(along_z):
        blocks = in_step(exchange.gather, blocks)
        if number == 0:
            blocks = fetch(blocks)
    blocks = in_step(split, blocks)
    for exchange in along_xy[:-1]:
        blocks = in_step(exchange.gather, blocks)
        blocks = fetch(blocks)
    sums, weights = [], []

    def add_first_half(piece, row_part):
        pre, fresh = gate_up_of(
            row_part, None, [first_weights[piece]], gate_up_weight, take(0, piece), piece_shape
        )
        sums.append(pre)
        weights.append(fresh)

    arrived = along_xy[-1].arriving(blocks[1])
    arriving = along_xy[-1].arriving(blocks[0])
    row_part = both_sides(jnp.stack([after(blocks[1], blocks[0])] + arrived))
    add_first_half(0, row_part)
    last_block = jnp.stack([after(blocks[0], sums[0])] + arriving)
    gathered = both_sides(last_block)
    for piece in range(1, pieces):
        add_first_half(piece, after(row_part, last_block))
    hidden, down_weight = gate_up_of(
        gathered, sums, weights, down_weight, lambda ref: ref, down_weight.shape
    )
    down_weight = resident(down_weight)

    blocks = [None, None]
    shape = [exchange.size for exchange in along_xy[::-1]] + [2]
    shape += [exchange.size for exchange in along_z[::-1]] + [rows, quarter]
    for number in (1, 0):
        sent = down_of(hidden, down_weight, 2 * number + 1 - core_index, quarter)
        arrived = as_own(core.shift(sent.reshape(shape), 1))
        kept = down_of(hidden, down_weight, 2 * number + core_index, quarter).reshape(shape)
        total = kept.astype(jnp.float32) + arrived.astype(jnp.float32)
        blocks[number] = total.astype(jnp.bfloat16)
        hidden = after(hidden, blocks[number])

    def join(block):
        return jnp.concatenate(own_first(block[0], core.shift(block[1], 1)), axis=-1)

    steps = [exchange.reduce for exchange in along_xy[::-1]] + [join]
    steps += [exchange.reduce for exchange in along_z[::-1]]
    for step in steps:
        blocks = in_step(step, blocks)
    return jnp.concatenate(blocks, axis=1)


def solution(mesh):
    in_specs = (
        P(AXES, None),
        P(None, None, AXES, None),
        P(None, AXES, None),
        P(AXES, None),
        P(AXES, None),
        P(AXES, None),
        P(),
        P(),
    )
    return jax.shard_map(
        local, mesh=mesh, in_specs=in_specs, out_specs=P(AXES, None), check_vma=False
    )
```

```python
import itertools
import math

import jax
import jax.numpy as jnp
from jax import lax
from jax.experimental import pallas as pl
from jax.experimental.pallas import tpu as pltpu
from jax.sharding import PartitionSpec as P

AXES = ("dp", "expert", "shard")
LANES = 128
ROW_BLOCK = 256
FETCH_LIMIT = 1 * 2**20
GATE_UP_LIMIT = 8 * 2**20
DOWN_LIMIT = 8 * 2**20


def slot_coefficients(expert_ids, gate_values, old_place, new_place):
    matches = (new_place[:, None] == old_place[None, :]).astype(jnp.float32)
    picks = (expert_ids[:, :, None] == jnp.arange(new_place.shape[0], dtype=jnp.int32)).astype(jnp.float32)
    by_expert = jnp.sum(picks * gate_values[:, :, None], axis=1)
    return jnp.sum(by_expert[:, :, None] * matches[None, :, :], axis=1)


def split_exact(value):
    pieces = []
    for _ in range(3):
        piece = lax.reduce_precision(value, exponent_bits=8, mantissa_bits=7)
        pieces.append(piece.astype(jnp.bfloat16))
        value = value - piece
    return pieces


class Digit:
    def __init__(self, name, stride, size):
        self.name, self.stride, self.size = name, stride, size


class Exchange:
    def __init__(self, ways, digits):
        self.ways, self.digits = ways, digits
        self.size = digits[0].size

    def shift(self, value, step):
        places = list(itertools.product(*(range(self.ways[name]) for name in AXES)))
        pairs = []
        for place in places:
            digit = self.digits[place[-1] % len(self.digits)]
            axis = AXES.index(digit.name)
            value_of = place[axis] // digit.stride % digit.size
            target = list(place)
            target[axis] += ((value_of + step) % digit.size - value_of) * digit.stride
            pairs.append((places.index(place), places.index(tuple(target))))
        return lax.ppermute(value, AXES, pairs)

    def arriving(self, block):
        return [self.shift(block, s) for s in range(1, self.size)]

    def gather(self, block):
        return jnp.stack([block] + self.arriving(block))

    def reduce(self, slots):
        own = slots[0].astype(jnp.float32)
        for s in range(1, self.size):
            own = own + self.shift(slots[s], self.size - s).astype(jnp.float32)
        return own.astype(jnp.bfloat16)


def digits_of(name, ways, low=1):
    digits, stride = [], low
    while stride < ways:
        left = ways // stride
        size = 2 if left % 2 == 0 else left
        digits.append(Digit(name, stride, size))
        stride *= size
    return digits[::-1]


def resident(value):
    return pltpu.with_memory_space_constraint(value, pltpu.VMEM)


def in_hbm(value):
    return pltpu.with_memory_space_constraint(value, pltpu.HBM)


def fetch_kernel(take, w_ref, after_ref, out_ref, sem):
    del after_ref
    copy = pltpu.make_async_copy(take(w_ref), out_ref, sem)
    copy.start()
    copy.wait()


def fetched(weight, take, shape, after):
    def kernel(*refs):
        fetch_kernel(take, *refs)

    return pl.pallas_call(
        kernel,
        in_specs=[pl.BlockSpec(memory_space=pl.ANY)] * 2,
        out_specs=pl.BlockSpec(memory_space=pltpu.VMEM),
        out_shape=pltpu.VMEM(shape, weight.dtype),
        scratch_shapes=[pltpu.SemaphoreType.DMA],
        compiler_params=pltpu.CompilerParams(vmem_limit_bytes=FETCH_LIMIT),
        cost_estimate=pl.CostEstimate(
            flops=0, bytes_accessed=4 * math.prod(shape), transcendentals=0
        ),
    )(in_hbm(weight), after)


def gate_up_kernel(last, take, pieces, row_ref, *refs):
    sum_refs, refs = (refs[:pieces], refs[pieces:]) if last else ((), refs)
    w_refs, (next_hbm, out_ref, next_ref, sem) = refs[:pieces], refs[pieces:]
    held, _, sliver, half = w_refs[0].shape
    experts = held * pieces
    units = 2 * sliver
    width = row_ref.shape[1] // 2
    depth = half // 2
    spans = [(0, half, 0)] if width == depth else [(0, depth, 0), (width, depth, depth)]
    copy = pltpu.make_async_copy(take(next_hbm), next_ref, sem)
    pl.when(pl.program_id(0) == 0)(copy.start)
    if last:
        extra = row_ref[:, depth:width].astype(jnp.float32)
        lane = lax.broadcasted_iota(jnp.int32, extra.shape, 1)
    for piece, w_ref in enumerate(w_refs):
        pre = sum_refs[piece][...] if last else None
        for at, span, w_at in spans:
            product = lax.dot_general(
                row_ref[:, at : at + span],
                w_ref[:, :, :, w_at : w_at + span].reshape(held * units, span),
                (((1,), (1,)), ((), ())),
                preferred_element_type=jnp.float32,
            )
            pre = product if pre is None else pre + product
        if not last:
            out_ref[...] = pre
            continue
        for number in range(held):
            slot, at = piece * held + number, number * units
            gate, up = pre[:, at : at + sliver], pre[:, at + sliver : at + units]
            mine = (lane == slot) | (lane == slot + experts) | (lane == slot + 2 * experts)
            weigh = jnp.sum(jnp.where(mine, extra, 0.0), axis=1, keepdims=True)
            hidden = (0.5 * gate) * (1.0 + jnp.tanh(0.5 * gate)) * up * weigh
            out_ref[slot] = hidden.astype(out_ref.dtype)
    pl.when(pl.program_id(0) == 0)(copy.wait)


def gate_up_of(row_part, sums, weights, next_weight, take, next_shape):
    held, _, sliver, half = weights[0].shape
    pieces = len(weights)
    experts = held * pieces
    rows = row_part.shape[0]
    row_block = min(ROW_BLOCK, rows)
    whole = rows == row_block
    last = sums is not None
    units = experts * 2 * sliver
    operands = [row_part] + (sums if last else [])
    if whole:
        specs = [pl.BlockSpec(memory_space=pltpu.VMEM)] * len(operands)
        operands = [resident(operand) for operand in operands]
    else:
        specs = [
            pl.BlockSpec((row_block, operand.shape[1]), lambda r: (r, 0)) for operand in operands
        ]
    if last:
        out_spec = pl.BlockSpec((experts, row_block, sliver), lambda r: (0, r, 0))
        out_shape = jax.ShapeDtypeStruct((experts, rows, sliver), jnp.bfloat16)
    else:
        out_spec = pl.BlockSpec((row_block, units), lambda r: (r, 0))
        out_shape = jax.ShapeDtypeStruct((rows, units), jnp.float32)
    if whole:
        out_spec = pl.BlockSpec(memory_space=pltpu.VMEM)
        out_shape = pltpu.VMEM(out_shape.shape, out_shape.dtype)

    def kernel(*refs):
        gate_up_kernel(last, take, pieces, *refs)

    return pl.pallas_call(
        kernel,
        grid=(rows // row_block,),
        in_specs=specs
        + [pl.BlockSpec(memory_space=pltpu.VMEM)] * pieces
        + [pl.BlockSpec(memory_space=pl.ANY)],
        out_specs=[out_spec, pl.BlockSpec(memory_space=pltpu.VMEM)],
        out_shape=[out_shape, pltpu.VMEM(next_shape, next_weight.dtype)],
        scratch_shapes=[pltpu.SemaphoreType.DMA],
        compiler_params=pltpu.CompilerParams(vmem_limit_bytes=GATE_UP_LIMIT),
        cost_estimate=pl.CostEstimate(
            flops=4 * rows * experts * sliver * half,
            bytes_accessed=2 * math.prod(next_shape) + 4 * rows * units,
            transcendentals=rows * experts * sliver,
        ),
    )(*operands, *(resident(weight) for weight in weights), in_hbm(next_weight))


def down_kernel(place, part_ref, hidden_ref, w_ref, out_ref):
    experts, _, sliver = hidden_ref.shape
    columns = out_ref.shape[1]
    taken = pl.ds(pl.multiple_of(part_ref[place] * columns, columns), columns)
    hidden = jnp.concatenate([hidden_ref[slot] for slot in range(experts)], axis=1)
    weights = w_ref[:, :, taken].reshape(experts * sliver, columns)
    out_ref[...] = jnp.dot(hidden, weights, preferred_element_type=jnp.float32).astype(
        out_ref.dtype
    )


def down_of(hidden, down_weight, parts, place, columns):
    def kernel(*refs):
        down_kernel(place, *refs)

    experts, rows, sliver = hidden.shape
    row_block = min(ROW_BLOCK, rows)
    return pl.pallas_call(
        kernel,
        grid=(rows // row_block,),
        in_specs=[
            pl.BlockSpec(memory_space=pltpu.SMEM),
            pl.BlockSpec((experts, row_block, sliver), lambda r: (0, r, 0)),
            pl.BlockSpec(memory_space=pltpu.VMEM),
        ],
        out_specs=pl.BlockSpec((row_block, columns), lambda r: (r, 0)),
        out_shape=jax.ShapeDtypeStruct((rows, columns), jnp.bfloat16),
        compiler_params=pltpu.CompilerParams(vmem_limit_bytes=DOWN_LIMIT),
        cost_estimate=pl.CostEstimate(
            flops=2 * rows * experts * sliver * columns,
            bytes_accessed=2 * (experts * sliver * columns + rows * experts * sliver + rows * columns),
            transcendentals=0,
        ),
    )(parts, hidden, down_weight)


def after(value, other):
    return lax.optimization_barrier((value, other))[0]


def local(
    tokens, gate_up_weight, down_weight, expert_ids, slot_ids, gate_values, old_place, new_place
):
    rows, model_width = tokens.shape
    half, quarter = model_width // 2, model_width // 4
    experts = gate_up_weight.shape[0]
    ways = {name: lax.axis_size(name) for name in AXES}
    core = Exchange(ways, [Digit("shard", 1, 2)])
    along_z = [Exchange(ways, [digit]) for digit in digits_of("expert", ways["expert"])]
    route = digits_of("shard", ways["shard"], 2) + digits_of("dp", ways["dp"])
    along_xy = [Exchange(ways, list(pair)) for pair in zip(route, route[::-1])]
    core_index = lax.axis_index("shard") % 2
    part_numbers = jnp.stack([3 - core_index, 1 - core_index, 2 + core_index, core_index])
    core_mask = jnp.full((1, LANES), core_index == 0)
    hops = len(along_xy)

    def own_first(low, high):
        mask = jnp.broadcast_to(core_mask[0, :1], low.shape)
        return jnp.where(mask, low, high), jnp.where(mask, high, low)

    def as_own(block):
        return jnp.flip(block.transpose(*range(hops)[::-1], *range(hops, block.ndim)), hops)

    coefficients = slot_coefficients(expert_ids, gate_values, old_place, new_place)
    extra = jnp.concatenate(split_exact(coefficients), axis=1)
    extra = jnp.pad(extra, ((0, 0), (0, -extra.shape[1] % LANES)))

    pieces = 2 if experts % 2 == 0 else 1
    held = experts // pieces
    piece_shape = (held,) + gate_up_weight.shape[1:3] + (half,)

    def take(number, piece):
        slots = pl.ds(piece * held, held)
        return lambda ref: ref.at[slots, :, :, pl.ds(number * half, half)]

    blocks = [
        jnp.concatenate([tokens[:, :quarter], extra, tokens[:, quarter:half], extra], axis=1),
        tokens[:, half:],
    ]
    blocks[0], part_numbers, core_mask = lax.optimization_barrier(
        (blocks[0], part_numbers, core_mask)
    )
    first_weights = []

    def fetch(blocks):
        if len(first_weights) < pieces:
            place = take(1, len(first_weights))
            fresh = fetched(gate_up_weight, place, piece_shape, blocks[1])
            waiting, fresh = lax.optimization_barrier((blocks[0], fresh))
            first_weights.append(fresh)
            return [waiting, blocks[1]]
        return blocks

    def split(block):
        side = block.shape[-1] // 2
        kept, sent = own_first(block[..., :side], block[..., side:])
        return jnp.stack([kept, core.shift(sent, 1)])

    def both_sides(block):
        sides = own_first(block, as_own(core.shift(block, 1)))
        block = jnp.concatenate(sides, axis=-1)
        return block.reshape(-1, block.shape[-1])

    def in_step(step, blocks):
        moved = step(blocks[1])
        return [step(blocks[0]), after(moved, blocks[0])]

    for number, exchange in enumerate(along_z):
        blocks = in_step(exchange.gather, blocks)
        if number == 0:
            blocks = fetch(blocks)
    blocks = [split(block) for block in blocks]
    for exchange in along_xy[:-1]:
        blocks = in_step(exchange.gather, blocks)
        blocks = fetch(blocks)
    sums, weights = [], []

    def add_first_half(piece, row_part):
        pre, fresh = gate_up_of(
            row_part, None, [first_weights[piece]], gate_up_weight, take(0, piece), piece_shape
        )
        sums.append(pre)
        weights.append(fresh)

    arrived = along_xy[-1].arriving(blocks[1])
    arriving = along_xy[-1].arriving(blocks[0])
    row_part = both_sides(jnp.stack([after(blocks[1], blocks[0])] + arrived))
    add_first_half(0, row_part)
    last_block = jnp.stack([after(blocks[0], sums[0])] + arriving)
    gathered = both_sides(last_block)
    for piece in range(1, pieces):
        add_first_half(piece, after(row_part, last_block))
    hidden, down_weight = gate_up_of(
        gathered, sums, weights, down_weight, lambda ref: ref, down_weight.shape
    )
    down_weight = resident(down_weight)

    blocks = [None, None]
    shape = [exchange.size for exchange in along_xy[::-1]] + [2]
    shape += [exchange.size for exchange in along_z[::-1]] + [rows, quarter]
    sent = [down_of(hidden, down_weight, part_numbers, place, quarter) for place in (0, 1)]
    kept = [down_of(hidden, down_weight, part_numbers, place, quarter) for place in (2, 3)]
    for number in (1, 0):
        arrived = as_own(core.shift(sent[1 - number].reshape(shape), 1))
        total = kept[1 - number].reshape(shape).astype(jnp.float32) + arrived.astype(jnp.float32)
        blocks[number] = total.astype(jnp.bfloat16)

    def join(block):
        return jnp.concatenate(own_first(block[0], core.shift(block[1], 1)), axis=-1)

    steps = [exchange.reduce for exchange in along_xy[::-1]] + [join]
    steps += [exchange.reduce for exchange in along_z[::-1]]
    for step in steps:
        blocks = in_step(step, blocks)
    return jnp.concatenate(blocks, axis=1)


def solution(mesh):
    in_specs = (
        P(AXES, None),
        P(None, None, AXES, None),
        P(None, AXES, None),
        P(AXES, None),
        P(AXES, None),
        P(AXES, None),
        P(),
        P(),
    )
    return jax.shard_map(
        local, mesh=mesh, in_specs=in_specs, out_specs=P(AXES, None), check_vma=False
    )
```

```python
import math

import jax
import jax.numpy as jnp
from jax import lax
from jax.experimental import pallas as pl
from jax.experimental.pallas import tpu as pltpu
from jax.sharding import PartitionSpec as P

AXES = ("dp", "expert", "shard")
LANES = 128
ROW_BLOCK = 256
FETCH_LIMIT = 1 * 2**20
GATE_UP_LIMIT = 8 * 2**20
DOWN_LIMIT = 8 * 2**20


def slot_coefficients(expert_ids, gate_values, old_place, new_place):
    matches = (new_place[:, None] == old_place[None, :]).astype(jnp.float32)
    picks = (expert_ids[:, :, None] == jnp.arange(new_place.shape[0], dtype=jnp.int32)).astype(jnp.float32)
    by_expert = jnp.sum(picks * gate_values[:, :, None], axis=1)
    return jnp.sum(by_expert[:, :, None] * matches[None, :, :], axis=1)


def split_exact(value):
    pieces = []
    for _ in range(3):
        piece = lax.reduce_precision(value, exponent_bits=8, mantissa_bits=7)
        pieces.append(piece.astype(jnp.bfloat16))
        value = value - piece
    return pieces


class Digit:
    def __init__(self, name, ways, stride, size):
        self.name, self.ways, self.stride, self.size = name, ways, stride, size

    def shift(self, value, step):
        pairs = []
        for index in range(self.ways):
            digit = index // self.stride % self.size
            target = (digit + step) % self.size
            pairs.append((index, index + (target - digit) * self.stride))
        return lax.ppermute(value, self.name, pairs)

    def gather(self, block, dim):
        return jnp.stack([block] + [self.shift(block, s) for s in range(1, self.size)], axis=dim)

    def reduce(self, slots, dim):
        own = lax.index_in_dim(slots, 0, dim, keepdims=False).astype(jnp.float32)
        for s in range(1, self.size):
            sent = lax.index_in_dim(slots, s, dim, keepdims=False)
            own = own + self.shift(sent, self.size - s).astype(jnp.float32)
        return own.astype(jnp.bfloat16)


def digits_of(name, ways, low=1):
    digits, stride = [], low
    while stride < ways:
        left = ways // stride
        size = 2 if left % 2 == 0 else left
        digits.append(Digit(name, ways, stride, size))
        stride *= size
    return digits[::-1]


def resident(value):
    return pltpu.with_memory_space_constraint(value, pltpu.VMEM)


def in_hbm(value):
    return pltpu.with_memory_space_constraint(value, pltpu.HBM)


def fetch_kernel(take, w_ref, after_ref, out_ref, sem):
    del after_ref
    copy = pltpu.make_async_copy(take(w_ref), out_ref, sem)
    copy.start()
    copy.wait()


def fetched(weight, take, shape, after):
    def kernel(*refs):
        fetch_kernel(take, *refs)

    return pl.pallas_call(
        kernel,
        in_specs=[pl.BlockSpec(memory_space=pl.ANY)] * 2,
        out_specs=pl.BlockSpec(memory_space=pltpu.VMEM),
        out_shape=pltpu.VMEM(shape, weight.dtype),
        scratch_shapes=[pltpu.SemaphoreType.DMA],
        compiler_params=pltpu.CompilerParams(vmem_limit_bytes=FETCH_LIMIT),
        cost_estimate=pl.CostEstimate(
            flops=0, bytes_accessed=4 * math.prod(shape), transcendentals=0
        ),
    )(in_hbm(weight), after)


def gate_up_kernel(last, take, pieces, row_ref, *refs):
    if last:
        sum_ref, refs = refs[0], refs[1:]
    w_refs, (next_hbm, out_ref, next_ref, sem) = refs[:pieces], refs[pieces:]
    held, _, sliver, half = w_refs[0].shape
    experts = held * pieces
    group = experts // 2 if experts % 2 == 0 else experts
    units = 2 * sliver
    depths = 2 if last else 1
    depth = half // depths
    copy = pltpu.make_async_copy(take(next_hbm), next_ref, sem)
    pl.when(pl.program_id(0) == 0)(copy.start)
    if last:
        extra = row_ref[:, half:].astype(jnp.float32)
        lane = lax.broadcasted_iota(jnp.int32, extra.shape, 1)
    for first in range(0, experts, group):
        columns = slice(first * units, (first + group) * units)
        w_ref, at_slot = w_refs[first // held], first % held
        pre = sum_ref[:, columns] if last else None
        for at in range(0, half, depth):
            product = lax.dot_general(
                row_ref[:, at : at + depth],
                w_ref[at_slot : at_slot + group, :, :, at : at + depth].reshape(
                    group * units, depth
                ),
                (((1,), (1,)), ((), ())),
                preferred_element_type=jnp.float32,
            )
            pre = product if pre is None else pre + product
        if not last:
            out_ref[:, columns] = pre
            continue
        for slot in range(first, first + group):
            at = (slot - first) * units
            gate, up = pre[:, at : at + sliver], pre[:, at + sliver : at + units]
            mine = (lane == slot) | (lane == slot + experts) | (lane == slot + 2 * experts)
            weigh = jnp.sum(jnp.where(mine, extra, 0.0), axis=1, keepdims=True)
            hidden = (0.5 * gate) * (1.0 + jnp.tanh(0.5 * gate)) * up * weigh
            out_ref[slot] = hidden.astype(out_ref.dtype)
    pl.when(pl.program_id(0) == 0)(copy.wait)


def gate_up_of(row_part, sums, weights, next_weight, take, next_shape):
    held, _, sliver, half = weights[0].shape
    pieces = len(weights)
    experts = held * pieces
    rows = row_part.shape[0]
    row_block = min(ROW_BLOCK, rows)
    whole = rows == row_block
    last = sums is not None
    units = experts * 2 * sliver
    operands = [row_part, sums] if last else [row_part]
    if whole:
        specs = [pl.BlockSpec(memory_space=pltpu.VMEM)] * len(operands)
        operands = [resident(operand) for operand in operands]
    else:
        specs = [
            pl.BlockSpec((row_block, operand.shape[1]), lambda r: (r, 0)) for operand in operands
        ]
    if last:
        out_spec = pl.BlockSpec((experts, row_block, sliver), lambda r: (0, r, 0))
        out_shape = jax.ShapeDtypeStruct((experts, rows, sliver), jnp.bfloat16)
    else:
        out_spec = pl.BlockSpec((row_block, units), lambda r: (r, 0))
        out_shape = jax.ShapeDtypeStruct((rows, units), jnp.float32)
    if whole:
        out_spec = pl.BlockSpec(memory_space=pltpu.VMEM)
        out_shape = pltpu.VMEM(out_shape.shape, out_shape.dtype)

    def kernel(*refs):
        gate_up_kernel(last, take, pieces, *refs)

    return pl.pallas_call(
        kernel,
        grid=(rows // row_block,),
        in_specs=specs
        + [pl.BlockSpec(memory_space=pltpu.VMEM)] * pieces
        + [pl.BlockSpec(memory_space=pl.ANY)],
        out_specs=[out_spec, pl.BlockSpec(memory_space=pltpu.VMEM)],
        out_shape=[out_shape, pltpu.VMEM(next_shape, next_weight.dtype)],
        scratch_shapes=[pltpu.SemaphoreType.DMA],
        compiler_params=pltpu.CompilerParams(vmem_limit_bytes=GATE_UP_LIMIT),
        cost_estimate=pl.CostEstimate(
            flops=4 * rows * experts * sliver * half,
            bytes_accessed=2 * math.prod(next_shape) + 4 * rows * units,
            transcendentals=rows * experts * sliver,
        ),
    )(*operands, *(resident(weight) for weight in weights), in_hbm(next_weight))


def down_kernel(part, hidden_ref, w_ref, out_ref):
    experts, _, sliver = hidden_ref.shape
    columns = out_ref.shape[1]
    block = next(size for size in (1536, 1024, 512, 384, 256, 128, columns) if columns % size == 0)

    def one_block(step, carry):
        at = pl.multiple_of(step * block, block)
        taken = pl.ds(pl.multiple_of(part * columns + step * block, block), block)
        hidden = jnp.concatenate([hidden_ref[slot] for slot in range(experts)], axis=1)
        weights = w_ref[:, :, taken].reshape(experts * sliver, block)
        out_ref[:, pl.ds(at, block)] = jnp.dot(
            hidden, weights, preferred_element_type=jnp.float32
        ).astype(out_ref.dtype)
        return carry

    lax.fori_loop(0, columns // block, one_block, 0)


def down_of(hidden, down_weight, part, columns):
    experts, rows, sliver = hidden.shape
    row_block = min(ROW_BLOCK, rows)

    def kernel(*refs):
        down_kernel(part, *refs)

    return pl.pallas_call(
        kernel,
        grid=(rows // row_block,),
        in_specs=[
            pl.BlockSpec((experts, row_block, sliver), lambda r: (0, r, 0)),
            pl.BlockSpec(memory_space=pltpu.VMEM),
        ],
        out_specs=pl.BlockSpec((row_block, columns), lambda r: (r, 0)),
        out_shape=jax.ShapeDtypeStruct((rows, columns), jnp.bfloat16),
        compiler_params=pltpu.CompilerParams(vmem_limit_bytes=DOWN_LIMIT),
        cost_estimate=pl.CostEstimate(
            flops=2 * rows * experts * sliver * columns,
            bytes_accessed=2 * (experts * sliver * columns + rows * experts * sliver + rows * columns),
            transcendentals=0,
        ),
    )(hidden, down_weight)


def local(
    tokens, gate_up_weight, down_weight, expert_ids, slot_ids, gate_values, old_place, new_place
):
    model_width = tokens.shape[1]
    rows = tokens.shape[0]
    half = model_width // 2
    ways = {name: lax.axis_size(name) for name in AXES}
    cores = 2 if ways["shard"] % 2 == 0 else 1
    x_digits = digits_of("dp", ways["dp"])
    z_digits = digits_of("expert", ways["expert"])
    y_digits = digits_of("shard", ways["shard"], cores)
    core_digits = [Digit("shard", ways["shard"], 1, cores)]
    dim_order = core_digits + x_digits[::-1] + y_digits[::-1] + z_digits[::-1]
    routes = [z_digits + y_digits + x_digits, z_digits + x_digits + y_digits]

    coefficients = slot_coefficients(expert_ids, gate_values, old_place, new_place)
    extra = jnp.concatenate(split_exact(coefficients), axis=1)
    extra = jnp.pad(extra, ((0, 0), (0, -extra.shape[1] % LANES)))
    parts = [
        jnp.concatenate([tokens[:, :half], extra], axis=1),
        tokens[:, half:],
    ]
    half_shape = gate_up_weight.shape[:3] + (half,)

    def take_second(ref):
        return ref.at[:, :, :, pl.ds(half, half)]

    def take_first(ref):
        return ref.at[:, :, :, pl.ds(0, half)]

    blocks, held = list(parts), [[], []]
    last = len(routes[0]) - 1
    for step in range(last + 2):
        if step == last:
            before_last = blocks[0]
        if step == last + 1:
            first_weights = fetched(gate_up_weight, take_second, half_shape, before_last)
            blocks[1], first_weights = lax.optimization_barrier((blocks[1], first_weights))
        for number in (1, 0):
            digit = (routes[number] + core_digits)[step]
            dim = sum(dim_order.index(other) < dim_order.index(digit) for other in held[number])
            blocks[number] = digit.gather(blocks[number], dim)
            held[number].append(digit)
    gathered = [block.reshape(-1, part.shape[1]) for block, part in zip(blocks, parts)]
    sums, next_weights = gate_up_of(
        gathered[1], None, [first_weights], gate_up_weight, take_first, half_shape
    )
    hidden, down_weight = gate_up_of(
        gathered[0], sums, [next_weights], down_weight, lambda ref: ref, down_weight.shape
    )
    down_weight = resident(down_weight)
    results = []
    for number, route in enumerate(routes):
        block = down_of(hidden, down_weight, number, half)
        block = block.reshape([digit.size for digit in dim_order] + [rows, half])
        held = list(dim_order)
        for digit in core_digits + route[::-1]:
            block = digit.reduce(block, held.index(digit))
            held.remove(digit)
        results.append(block)
    return jnp.concatenate(results, axis=1)


def solution(mesh):
    in_specs = (
        P(AXES, None),
        P(None, None, AXES, None),
        P(None, AXES, None),
        P(AXES, None),
        P(AXES, None),
        P(AXES, None),
        P(),
        P(),
    )
    return jax.shard_map(
        local, mesh=mesh, in_specs=in_specs, out_specs=P(AXES, None), check_vma=False
    )
```

```python
import math

import jax
import jax.numpy as jnp
from jax import lax
from jax.experimental import pallas as pl
from jax.experimental.pallas import tpu as pltpu
from jax.sharding import PartitionSpec as P

AXES = ("dp", "expert", "shard")
LANES = 128
ROW_BLOCK = 256
FETCH_LIMIT = 1 * 2**20
GATE_UP_LIMIT = 8 * 2**20
DOWN_LIMIT = 8 * 2**20


def pack_kernel(tokens_ref, ids_ref, gates_ref, old_ref, new_ref, out_ref):
    rows, width = tokens_ref.shape
    choices = ids_ref.shape[0]
    out_ref[:, :width] = tokens_ref[...]
    square = (rows, rows)
    diagonal = lax.broadcasted_iota(jnp.int32, square, 0) == lax.broadcasted_iota(
        jnp.int32, square, 1
    )
    lane = lax.broadcasted_iota(jnp.int32, (rows, out_ref.shape[1] - width), 1)
    extra = jnp.zeros(lane.shape, jnp.float32)
    old = old_ref[...]
    index = lax.broadcasted_iota(jnp.int32, old.shape, 1).astype(jnp.float32)
    for choice in range(choices):
        ids = ids_ref[choice : choice + 1, :]
        slot = jnp.zeros(ids.shape, jnp.float32)
        for expert in range(old_ref.shape[1]):
            place = new_ref[:, expert : expert + 1]
            of_expert = jnp.sum(jnp.where(old == place, index, 0.0), axis=1, keepdims=True)
            slot = jnp.where(ids == expert, of_expert, slot)
        left = gates_ref[choice : choice + 1, :]
        values = [slot]
        for _ in range(3):
            values.append(left.astype(jnp.bfloat16).astype(jnp.float32))
            left = left - values[-1]
        for place, value in enumerate(values):
            column = jnp.sum(jnp.where(diagonal, value, 0.0), axis=1, keepdims=True)
            extra = jnp.where(lane == place * choices + choice, column, extra)
    out_ref[:, width:] = extra.astype(out_ref.dtype)


def packed(tokens, width, expert_ids, gate_values, old_place, new_place):
    rows, choices = expert_ids.shape
    experts = old_place.shape[0]
    lanes = -(-4 * choices // LANES) * LANES
    small = pl.BlockSpec((choices, rows), lambda i: (0, 0))
    place = pl.BlockSpec((1, experts), lambda i: (0, 0))
    operands = (tokens, expert_ids.T, gate_values.T, old_place[None, :], new_place[None, :])
    return pl.pallas_call(
        pack_kernel,
        grid=(1,),
        in_specs=[pl.BlockSpec((rows, width), lambda i: (0, 0)), small, small, place, place],
        out_specs=pl.BlockSpec((rows, width + lanes), lambda i: (0, 0)),
        out_shape=jax.ShapeDtypeStruct((rows, width + lanes), tokens.dtype),
        cost_estimate=pl.CostEstimate(
            flops=0, bytes_accessed=4 * rows * width, transcendentals=0
        ),
    )(*(in_hbm(operand) for operand in operands))


class Digit:
    def __init__(self, name, ways, stride, size):
        self.name, self.ways, self.stride, self.size = name, ways, stride, size

    def shift(self, value, step):
        pairs = []
        for index in range(self.ways):
            digit = index // self.stride % self.size
            target = (digit + step) % self.size
            pairs.append((index, index + (target - digit) * self.stride))
        return lax.ppermute(value, self.name, pairs)

    def gather(self, block, dim):
        return jnp.stack([block] + [self.shift(block, s) for s in range(1, self.size)], axis=dim)

    def reduce(self, slots, dim):
        own = lax.index_in_dim(slots, 0, dim, keepdims=False).astype(jnp.float32)
        for s in range(1, self.size):
            sent = lax.index_in_dim(slots, s, dim, keepdims=False)
            own = own + self.shift(sent, self.size - s).astype(jnp.float32)
        return own.astype(jnp.bfloat16)


def digits_of(name, ways, low=1):
    digits, stride = [], low
    while stride < ways:
        left = ways // stride
        size = 2 if left % 2 == 0 else left
        digits.append(Digit(name, ways, stride, size))
        stride *= size
    return digits[::-1]


def resident(value):
    return pltpu.with_memory_space_constraint(value, pltpu.VMEM)


def in_hbm(value):
    return pltpu.with_memory_space_constraint(value, pltpu.HBM)


def fetch_kernel(take, w_ref, after_ref, out_ref, sem):
    del after_ref
    copy = pltpu.make_async_copy(take(w_ref), out_ref, sem)
    copy.start()
    copy.wait()


def fetched(weight, take, shape, after):
    def kernel(*refs):
        fetch_kernel(take, *refs)

    return pl.pallas_call(
        kernel,
        in_specs=[pl.BlockSpec(memory_space=pl.ANY)] * 2,
        out_specs=pl.BlockSpec(memory_space=pltpu.VMEM),
        out_shape=pltpu.VMEM(shape, weight.dtype),
        scratch_shapes=[pltpu.SemaphoreType.DMA],
        compiler_params=pltpu.CompilerParams(vmem_limit_bytes=FETCH_LIMIT),
        cost_estimate=pl.CostEstimate(
            flops=0, bytes_accessed=4 * math.prod(shape), transcendentals=0
        ),
    )(in_hbm(weight), after)


def gate_up_kernel(choices, take, pieces, row_ref, *refs):
    last = choices > 0
    if last:
        sum_ref, refs = refs[0], refs[1:]
    w_refs, (next_hbm, out_ref, next_ref, sem) = refs[:pieces], refs[pieces:]
    held, _, sliver, half = w_refs[0].shape
    experts = held * pieces
    group = experts // 2 if experts % 2 == 0 else experts
    units = 2 * sliver
    depths = 2 if last else 1
    depth = half // depths
    copy = pltpu.make_async_copy(take(next_hbm), next_ref, sem)
    pl.when(pl.program_id(0) == 0)(copy.start)
    if last:
        extra = row_ref[:, half:].astype(jnp.float32)
        lane = lax.broadcasted_iota(jnp.int32, extra.shape, 1)
        chosen, gates = [], []
        for choice in range(choices):
            mine = (lane >= choices) & (lane < 4 * choices) & (lane % choices == choice)
            chosen.append(jnp.sum(jnp.where(lane == choice, extra, 0.0), axis=1, keepdims=True))
            gates.append(jnp.sum(jnp.where(mine, extra, 0.0), axis=1, keepdims=True))
    for first in range(0, experts, group):
        columns = slice(first * units, (first + group) * units)
        w_ref, at_slot = w_refs[first // held], first % held
        pre = sum_ref[:, columns] if last else None
        for at in range(0, half, depth):
            product = lax.dot_general(
                row_ref[:, at : at + depth],
                w_ref[at_slot : at_slot + group, :, :, at : at + depth].reshape(
                    group * units, depth
                ),
                (((1,), (1,)), ((), ())),
                preferred_element_type=jnp.float32,
            )
            pre = product if pre is None else pre + product
        if not last:
            out_ref[:, columns] = pre
            continue
        for slot in range(first, first + group):
            at = (slot - first) * units
            gate, up = pre[:, at : at + sliver], pre[:, at + sliver : at + units]
            weigh = sum(
                jnp.where(choice == slot, gate_value, 0.0)
                for choice, gate_value in zip(chosen, gates)
            )
            hidden = (0.5 * gate) * (1.0 + jnp.tanh(0.5 * gate)) * up * weigh
            out_ref[slot] = hidden.astype(out_ref.dtype)
    pl.when(pl.program_id(0) == 0)(copy.wait)


def gate_up_of(row_part, others, weights, next_weight, take, next_shape, choices=0):
    held, _, sliver, half = weights[0].shape
    pieces = len(weights)
    experts = held * pieces
    rows = row_part.shape[0]
    row_block = min(ROW_BLOCK, rows)
    whole = rows == row_block
    last = choices > 0
    units = experts * 2 * sliver
    operands = [row_part] + others
    if whole:
        specs = [pl.BlockSpec(memory_space=pltpu.VMEM)] * len(operands)
        operands = [resident(operand) for operand in operands]
    else:
        specs = [
            pl.BlockSpec((row_block, operand.shape[1]), lambda r: (r, 0)) for operand in operands
        ]
    if last:
        out_spec = pl.BlockSpec((experts, row_block, sliver), lambda r: (0, r, 0))
        out_shape = jax.ShapeDtypeStruct((experts, rows, sliver), jnp.bfloat16)
    else:
        out_spec = pl.BlockSpec((row_block, units), lambda r: (r, 0))
        out_shape = jax.ShapeDtypeStruct((rows, units), jnp.float32)
    if whole:
        out_spec = pl.BlockSpec(memory_space=pltpu.VMEM)
        out_shape = pltpu.VMEM(out_shape.shape, out_shape.dtype)

    def kernel(*refs):
        gate_up_kernel(choices, take, pieces, *refs)

    return pl.pallas_call(
        kernel,
        grid=(rows // row_block,),
        in_specs=specs
        + [pl.BlockSpec(memory_space=pltpu.VMEM)] * pieces
        + [pl.BlockSpec(memory_space=pl.ANY)],
        out_specs=[out_spec, pl.BlockSpec(memory_space=pltpu.VMEM)],
        out_shape=[out_shape, pltpu.VMEM(next_shape, next_weight.dtype)],
        scratch_shapes=[pltpu.SemaphoreType.DMA],
        compiler_params=pltpu.CompilerParams(vmem_limit_bytes=GATE_UP_LIMIT),
        cost_estimate=pl.CostEstimate(
            flops=4 * rows * experts * sliver * half,
            bytes_accessed=2 * math.prod(next_shape) + 4 * rows * units,
            transcendentals=rows * experts * sliver,
        ),
    )(*operands, *(resident(weight) for weight in weights), in_hbm(next_weight))


def down_kernel(part, hidden_ref, w_ref, out_ref):
    experts, _, sliver = hidden_ref.shape
    columns = out_ref.shape[1]
    block = next(size for size in (1536, 1024, 512, 384, 256, 128, columns) if columns % size == 0)

    def one_block(step, carry):
        at = pl.multiple_of(step * block, block)
        taken = pl.ds(pl.multiple_of(part * columns + step * block, block), block)
        hidden = jnp.concatenate([hidden_ref[slot] for slot in range(experts)], axis=1)
        weights = w_ref[:, :, taken].reshape(experts * sliver, block)
        out_ref[:, pl.ds(at, block)] = jnp.dot(
            hidden, weights, preferred_element_type=jnp.float32
        ).astype(out_ref.dtype)
        return carry

    lax.fori_loop(0, columns // block, one_block, 0)


def down_of(hidden, down_weight, part, columns):
    experts, rows, sliver = hidden.shape
    row_block = min(ROW_BLOCK, rows)

    def kernel(*refs):
        down_kernel(part, *refs)

    return pl.pallas_call(
        kernel,
        grid=(rows // row_block,),
        in_specs=[
            pl.BlockSpec((experts, row_block, sliver), lambda r: (0, r, 0)),
            pl.BlockSpec(memory_space=pltpu.VMEM),
        ],
        out_specs=pl.BlockSpec((row_block, columns), lambda r: (r, 0)),
        out_shape=jax.ShapeDtypeStruct((rows, columns), jnp.bfloat16),
        compiler_params=pltpu.CompilerParams(vmem_limit_bytes=DOWN_LIMIT),
        cost_estimate=pl.CostEstimate(
            flops=2 * rows * experts * sliver * columns,
            bytes_accessed=2 * (experts * sliver * columns + rows * experts * sliver + rows * columns),
            transcendentals=0,
        ),
    )(hidden, down_weight)


def local(
    tokens, gate_up_weight, down_weight, expert_ids, slot_ids, gate_values, old_place, new_place
):
    model_width = tokens.shape[1]
    rows = tokens.shape[0]
    half = model_width // 2
    ways = {name: lax.axis_size(name) for name in AXES}
    cores = 2 if ways["shard"] % 2 == 0 else 1
    x_digits = digits_of("dp", ways["dp"])
    z_digits = digits_of("expert", ways["expert"])
    y_digits = digits_of("shard", ways["shard"], cores)
    core_digits = [Digit("shard", ways["shard"], 1, cores)]
    dim_order = core_digits + x_digits[::-1] + y_digits[::-1] + z_digits[::-1]
    routes = [z_digits + y_digits + x_digits, z_digits + x_digits + y_digits]

    choices = expert_ids.shape[1]
    parts = [packed(tokens, half, expert_ids, gate_values, old_place, new_place), tokens[:, half:]]
    half_shape = gate_up_weight.shape[:3] + (half,)

    def take_second(ref):
        return ref.at[:, :, :, pl.ds(half, half)]

    def take_first(ref):
        return ref.at[:, :, :, pl.ds(0, half)]

    blocks, held = list(parts), [[], []]
    last = len(routes[0]) - 1
    for step in range(last + 2):
        if step == last:
            before_last = blocks[0]
        if step == last + 1:
            first_weights = fetched(gate_up_weight, take_second, half_shape, before_last)
            blocks[1], first_weights = lax.optimization_barrier((blocks[1], first_weights))
        for number in (1, 0):
            digit = (routes[number] + core_digits)[step]
            dim = sum(dim_order.index(other) < dim_order.index(digit) for other in held[number])
            blocks[number] = digit.gather(blocks[number], dim)
            held[number].append(digit)
    gathered = [block.reshape(-1, part.shape[1]) for block, part in zip(blocks, parts)]
    sums, next_weights = gate_up_of(
        gathered[1], [], [first_weights], gate_up_weight, take_first, half_shape
    )
    hidden, down_weight = gate_up_of(
        gathered[0],
        [sums],
        [next_weights],
        down_weight,
        lambda ref: ref,
        down_weight.shape,
        choices,
    )
    down_weight = resident(down_weight)
    results = []
    for number, route in enumerate(routes):
        block = down_of(hidden, down_weight, number, half)
        block = block.reshape([digit.size for digit in dim_order] + [rows, half])
        held = list(dim_order)
        for digit in core_digits + route[::-1]:
            block = digit.reduce(block, held.index(digit))
            held.remove(digit)
        results.append(block)
    return jnp.concatenate(results, axis=1)


def solution(mesh):
    in_specs = (
        P(AXES, None),
        P(None, None, AXES, None),
        P(None, AXES, None),
        P(AXES, None),
        P(AXES, None),
        P(AXES, None),
        P(),
        P(),
    )
    return jax.shard_map(
        local, mesh=mesh, in_specs=in_specs, out_specs=P(AXES, None), check_vma=False
    )
```

```python
import math

import jax
import jax.numpy as jnp
from jax import lax
from jax.experimental import pallas as pl
from jax.experimental.pallas import tpu as pltpu
from jax.sharding import PartitionSpec as P

AXES = ("dp", "expert", "shard")
LANES = 128
ROW_BLOCK = 256
FETCH_LIMIT = 1 * 2**20
GATE_UP_LIMIT = 8 * 2**20
DOWN_LIMIT = 8 * 2**20


def slot_coefficients(expert_ids, gate_values, old_place, new_place):
    matches = (new_place[:, None] == old_place[None, :]).astype(jnp.float32)
    picks = (expert_ids[:, :, None] == jnp.arange(new_place.shape[0], dtype=jnp.int32)).astype(jnp.float32)
    by_expert = jnp.sum(picks * gate_values[:, :, None], axis=1)
    return jnp.sum(by_expert[:, :, None] * matches[None, :, :], axis=1)


def split_exact(value):
    pieces = []
    for _ in range(3):
        piece = lax.reduce_precision(value, exponent_bits=8, mantissa_bits=7)
        pieces.append(piece.astype(jnp.bfloat16))
        value = value - piece
    return pieces


class Digit:
    def __init__(self, name, ways, stride, size):
        self.name, self.ways, self.stride, self.size = name, ways, stride, size

    def shift(self, value, step):
        pairs = []
        for index in range(self.ways):
            digit = index // self.stride % self.size
            target = (digit + step) % self.size
            pairs.append((index, index + (target - digit) * self.stride))
        return lax.ppermute(value, self.name, pairs)

    def gather(self, block, dim):
        return jnp.stack([block] + [self.shift(block, s) for s in range(1, self.size)], axis=dim)

    def reduce(self, slots, dim):
        own = lax.index_in_dim(slots, 0, dim, keepdims=False).astype(jnp.float32)
        for s in range(1, self.size):
            sent = lax.index_in_dim(slots, s, dim, keepdims=False)
            own = own + self.shift(sent, self.size - s).astype(jnp.float32)
        return own.astype(jnp.bfloat16)


def digits_of(name, ways, low=1):
    digits, stride = [], low
    while stride < ways:
        left = ways // stride
        size = 2 if left % 2 == 0 else left
        digits.append(Digit(name, ways, stride, size))
        stride *= size
    return digits[::-1]


def resident(value):
    return pltpu.with_memory_space_constraint(value, pltpu.VMEM)


def in_hbm(value):
    return pltpu.with_memory_space_constraint(value, pltpu.HBM)


def slot_copies(source, target, sems):
    return [
        pltpu.make_async_copy(source.at[slot], target.at[slot], sems.at[slot])
        for slot in range(target.shape[0])
    ]


def fetch_kernel(take, w_ref, after_ref, out_ref, sems):
    del after_ref
    copies = slot_copies(take(w_ref), out_ref, sems)
    for copy in copies:
        copy.start()
    for copy in copies:
        copy.wait()


def fetched(weight, take, shape, after):
    def kernel(*refs):
        fetch_kernel(take, *refs)

    return pl.pallas_call(
        kernel,
        in_specs=[pl.BlockSpec(memory_space=pl.ANY)] * 2,
        out_specs=pl.BlockSpec(memory_space=pltpu.VMEM),
        out_shape=pltpu.VMEM(shape, weight.dtype),
        scratch_shapes=[pltpu.SemaphoreType.DMA((shape[0],))],
        compiler_params=pltpu.CompilerParams(vmem_limit_bytes=FETCH_LIMIT),
        cost_estimate=pl.CostEstimate(
            flops=0, bytes_accessed=4 * math.prod(shape), transcendentals=0
        ),
    )(in_hbm(weight), after)


def gate_up_kernel(last, take, pieces, row_ref, *refs):
    if last:
        sum_ref, refs = refs[0], refs[1:]
    w_refs, (next_hbm, out_ref, next_ref, sems) = refs[:pieces], refs[pieces:]
    held, _, sliver, half = w_refs[0].shape
    experts = held * pieces
    group = experts // 2 if experts % 2 == 0 else experts
    units = 2 * sliver
    depths = 2 if last else 1
    depth = half // depths
    copies = slot_copies(take(next_hbm), next_ref, sems)
    for copy in copies:
        pl.when(pl.program_id(0) == 0)(copy.start)
    if last:
        extra = row_ref[:, half:].astype(jnp.float32)
        lane = lax.broadcasted_iota(jnp.int32, extra.shape, 1)
    for first in range(0, experts, group):
        columns = slice(first * units, (first + group) * units)
        w_ref, at_slot = w_refs[first // held], first % held
        pre = sum_ref[:, columns] if last else None
        for at in range(0, half, depth):
            product = lax.dot_general(
                row_ref[:, at : at + depth],
                w_ref[at_slot : at_slot + group, :, :, at : at + depth].reshape(
                    group * units, depth
                ),
                (((1,), (1,)), ((), ())),
                preferred_element_type=jnp.float32,
            )
            pre = product if pre is None else pre + product
        if not last:
            out_ref[:, columns] = pre
            continue
        for slot in range(first, first + group):
            at = (slot - first) * units
            gate, up = pre[:, at : at + sliver], pre[:, at + sliver : at + units]
            mine = (lane == slot) | (lane == slot + experts) | (lane == slot + 2 * experts)
            weigh = jnp.sum(jnp.where(mine, extra, 0.0), axis=1, keepdims=True)
            hidden = (0.5 * gate) * (1.0 + jnp.tanh(0.5 * gate)) * up * weigh
            out_ref[slot] = hidden.astype(out_ref.dtype)
    for copy in copies:
        pl.when(pl.program_id(0) == 0)(copy.wait)


def gate_up_of(row_part, sums, weights, next_weight, take, next_shape):
    held, _, sliver, half = weights[0].shape
    pieces = len(weights)
    experts = held * pieces
    rows = row_part.shape[0]
    row_block = min(ROW_BLOCK, rows)
    whole = rows == row_block
    last = sums is not None
    units = experts * 2 * sliver
    operands = [row_part, sums] if last else [row_part]
    if whole:
        specs = [pl.BlockSpec(memory_space=pltpu.VMEM)] * len(operands)
        operands = [resident(operand) for operand in operands]
    else:
        specs = [
            pl.BlockSpec((row_block, operand.shape[1]), lambda r: (r, 0)) for operand in operands
        ]
    if last:
        out_spec = pl.BlockSpec((experts, row_block, sliver), lambda r: (0, r, 0))
        out_shape = jax.ShapeDtypeStruct((experts, rows, sliver), jnp.bfloat16)
    else:
        out_spec = pl.BlockSpec((row_block, units), lambda r: (r, 0))
        out_shape = jax.ShapeDtypeStruct((rows, units), jnp.float32)
    if whole:
        out_spec = pl.BlockSpec(memory_space=pltpu.VMEM)
        out_shape = pltpu.VMEM(out_shape.shape, out_shape.dtype)

    def kernel(*refs):
        gate_up_kernel(last, take, pieces, *refs)

    return pl.pallas_call(
        kernel,
        grid=(rows // row_block,),
        in_specs=specs
        + [pl.BlockSpec(memory_space=pltpu.VMEM)] * pieces
        + [pl.BlockSpec(memory_space=pl.ANY)],
        out_specs=[out_spec, pl.BlockSpec(memory_space=pltpu.VMEM)],
        out_shape=[out_shape, pltpu.VMEM(next_shape, next_weight.dtype)],
        scratch_shapes=[pltpu.SemaphoreType.DMA((next_shape[0],))],
        compiler_params=pltpu.CompilerParams(vmem_limit_bytes=GATE_UP_LIMIT),
        cost_estimate=pl.CostEstimate(
            flops=4 * rows * experts * sliver * half,
            bytes_accessed=2 * math.prod(next_shape) + 4 * rows * units,
            transcendentals=rows * experts * sliver,
        ),
    )(*operands, *(resident(weight) for weight in weights), in_hbm(next_weight))


def down_kernel(part, hidden_ref, w_ref, out_ref):
    experts, _, sliver = hidden_ref.shape
    columns = out_ref.shape[1]
    block = next(size for size in (1536, 1024, 512, 384, 256, 128, columns) if columns % size == 0)

    def one_block(step, carry):
        at = pl.multiple_of(step * block, block)
        taken = pl.ds(pl.multiple_of(part * columns + step * block, block), block)
        hidden = jnp.concatenate([hidden_ref[slot] for slot in range(experts)], axis=1)
        weights = w_ref[:, :, taken].reshape(experts * sliver, block)
        out_ref[:, pl.ds(at, block)] = jnp.dot(
            hidden, weights, preferred_element_type=jnp.float32
        ).astype(out_ref.dtype)
        return carry

    lax.fori_loop(0, columns // block, one_block, 0)


def down_of(hidden, down_weight, part, columns):
    experts, rows, sliver = hidden.shape
    row_block = min(ROW_BLOCK, rows)

    def kernel(*refs):
        down_kernel(part, *refs)

    return pl.pallas_call(
        kernel,
        grid=(rows // row_block,),
        in_specs=[
            pl.BlockSpec((experts, row_block, sliver), lambda r: (0, r, 0)),
            pl.BlockSpec(memory_space=pltpu.VMEM),
        ],
        out_specs=pl.BlockSpec((row_block, columns), lambda r: (r, 0)),
        out_shape=jax.ShapeDtypeStruct((rows, columns), jnp.bfloat16),
        compiler_params=pltpu.CompilerParams(vmem_limit_bytes=DOWN_LIMIT),
        cost_estimate=pl.CostEstimate(
            flops=2 * rows * experts * sliver * columns,
            bytes_accessed=2 * (experts * sliver * columns + rows * experts * sliver + rows * columns),
            transcendentals=0,
        ),
    )(hidden, down_weight)


def local(
    tokens, gate_up_weight, down_weight, expert_ids, slot_ids, gate_values, old_place, new_place
):
    model_width = tokens.shape[1]
    rows = tokens.shape[0]
    half = model_width // 2
    ways = {name: lax.axis_size(name) for name in AXES}
    cores = 2 if ways["shard"] % 2 == 0 else 1
    x_digits = digits_of("dp", ways["dp"])
    z_digits = digits_of("expert", ways["expert"])
    y_digits = digits_of("shard", ways["shard"], cores)
    core_digits = [Digit("shard", ways["shard"], 1, cores)]
    dim_order = core_digits + x_digits[::-1] + y_digits[::-1] + z_digits[::-1]
    routes = [z_digits + y_digits + x_digits, z_digits + x_digits + y_digits]

    coefficients = slot_coefficients(expert_ids, gate_values, old_place, new_place)
    extra = jnp.concatenate(split_exact(coefficients), axis=1)
    extra = jnp.pad(extra, ((0, 0), (0, -extra.shape[1] % LANES)))
    parts = [
        jnp.concatenate([tokens[:, :half], extra], axis=1),
        tokens[:, half:],
    ]
    half_shape = gate_up_weight.shape[:3] + (half,)

    def take_second(ref):
        return ref.at[:, :, :, pl.ds(half, half)]

    def take_first(ref):
        return ref.at[:, :, :, pl.ds(0, half)]

    blocks, held = list(parts), [[], []]
    last = len(routes[0]) - 1
    for step in range(last + 2):
        if step == last:
            before_last = blocks[0]
        if step == last + 1:
            first_weights = fetched(gate_up_weight, take_second, half_shape, before_last)
            blocks[1], first_weights = lax.optimization_barrier((blocks[1], first_weights))
        for number in (1, 0):
            digit = (routes[number] + core_digits)[step]
            dim = sum(dim_order.index(other) < dim_order.index(digit) for other in held[number])
            blocks[number] = digit.gather(blocks[number], dim)
            held[number].append(digit)
    gathered = [block.reshape(-1, part.shape[1]) for block, part in zip(blocks, parts)]
    sums, next_weights = gate_up_of(
        gathered[1], None, [first_weights], gate_up_weight, take_first, half_shape
    )
    hidden, down_weight = gate_up_of(
        gathered[0], sums, [next_weights], down_weight, lambda ref: ref, down_weight.shape
    )
    down_weight = resident(down_weight)
    results = []
    for number, route in enumerate(routes):
        block = down_of(hidden, down_weight, number, half)
        block = block.reshape([digit.size for digit in dim_order] + [rows, half])
        held = list(dim_order)
        for digit in core_digits + route[::-1]:
            block = digit.reduce(block, held.index(digit))
            held.remove(digit)
        results.append(block)
    return jnp.concatenate(results, axis=1)


def solution(mesh):
    in_specs = (
        P(AXES, None),
        P(None, None, AXES, None),
        P(None, AXES, None),
        P(AXES, None),
        P(AXES, None),
        P(AXES, None),
        P(),
        P(),
    )
    return jax.shard_map(
        local, mesh=mesh, in_specs=in_specs, out_specs=P(AXES, None), check_vma=False
    )
```

```python
import math

import jax
import jax.numpy as jnp
from jax import lax
from jax.experimental import pallas as pl
from jax.experimental.pallas import tpu as pltpu
from jax.sharding import PartitionSpec as P

AXES = ("dp", "expert", "shard")
LANES = 128
MATRIX = 256
ROW_BLOCK = 256
FETCH_LIMIT = 1 * 2**20
GATE_UP_LIMIT = 8 * 2**20
DOWN_LIMIT = 12 * 2**20
REORDER_LIMIT = 48 * 2**20


def slot_coefficients(expert_ids, gate_values, old_place, new_place):
    matches = (new_place[:, None] == old_place[None, :]).astype(jnp.float32)
    picks = (expert_ids[:, :, None] == jnp.arange(new_place.shape[0], dtype=jnp.int32)).astype(jnp.float32)
    by_expert = jnp.sum(picks * gate_values[:, :, None], axis=1)
    return jnp.sum(by_expert[:, :, None] * matches[None, :, :], axis=1)


def split_exact(value):
    pieces = []
    for _ in range(3):
        piece = lax.reduce_precision(value, exponent_bits=8, mantissa_bits=7)
        pieces.append(piece.astype(jnp.bfloat16))
        value = value - piece
    return pieces


class Digit:
    def __init__(self, name, ways, stride, size):
        self.name, self.ways, self.stride, self.size = name, ways, stride, size

    def shift(self, value, step):
        pairs = []
        for index in range(self.ways):
            digit = index // self.stride % self.size
            target = (digit + step) % self.size
            pairs.append((index, index + (target - digit) * self.stride))
        return lax.ppermute(value, self.name, pairs)

    def gather(self, block, dim):
        return jnp.stack([block] + [self.shift(block, s) for s in range(1, self.size)], axis=dim)

    def reduce(self, slots, dim):
        own = lax.index_in_dim(slots, 0, dim, keepdims=False).astype(jnp.float32)
        for s in range(1, self.size):
            sent = lax.index_in_dim(slots, s, dim, keepdims=False)
            own = own + self.shift(sent, self.size - s).astype(jnp.float32)
        return own.astype(jnp.bfloat16)


def digits_of(name, ways, low=1):
    digits, stride = [], low
    while stride < ways:
        left = ways // stride
        size = 2 if left % 2 == 0 else left
        digits.append(Digit(name, ways, stride, size))
        stride *= size
    return digits[::-1]


def resident(value):
    return pltpu.with_memory_space_constraint(value, pltpu.VMEM)


def in_hbm(value):
    return pltpu.with_memory_space_constraint(value, pltpu.HBM)


def fetch_kernel(take, w_ref, after_ref, out_ref, sem):
    del after_ref
    copy = pltpu.make_async_copy(take(w_ref), out_ref, sem)
    copy.start()
    copy.wait()


def fetched(weight, take, shape, after):
    def kernel(*refs):
        fetch_kernel(take, *refs)

    return pl.pallas_call(
        kernel,
        in_specs=[pl.BlockSpec(memory_space=pl.ANY)] * 2,
        out_specs=pl.BlockSpec(memory_space=pltpu.VMEM),
        out_shape=pltpu.VMEM(shape, weight.dtype),
        scratch_shapes=[pltpu.SemaphoreType.DMA],
        compiler_params=pltpu.CompilerParams(vmem_limit_bytes=FETCH_LIMIT),
        cost_estimate=pl.CostEstimate(
            flops=0, bytes_accessed=4 * math.prod(shape), transcendentals=0
        ),
    )(in_hbm(weight), after)


def gate_up_kernel(last, take, pieces, row_ref, *refs):
    if last:
        sum_ref, refs = refs[0], refs[1:]
    w_refs, (next_hbm, out_ref, next_ref, sem) = refs[:pieces], refs[pieces:]
    held, _, sliver, half = w_refs[0].shape
    experts = held * pieces
    group = experts // 2 if experts % 2 == 0 else experts
    units = 2 * sliver
    middle = -(-half // (2 * MATRIX)) * MATRIX if last else half
    copy = pltpu.make_async_copy(take(next_hbm), next_ref, sem)
    pl.when(pl.program_id(0) == 0)(copy.start)
    if last:
        extra = row_ref[:, half:].astype(jnp.float32)
        lane = lax.broadcasted_iota(jnp.int32, extra.shape, 1)
    for first in range(0, experts, group):
        columns = slice(first * units, (first + group) * units)
        w_ref, at_slot = w_refs[first // held], first % held
        pre = sum_ref[:, columns] if last else None
        for at, end in ((0, middle), (middle, half))[: 1 + (middle < half)]:
            product = lax.dot_general(
                row_ref[:, at:end],
                w_ref[at_slot : at_slot + group, :, :, at:end].reshape(group * units, end - at),
                (((1,), (1,)), ((), ())),
                preferred_element_type=jnp.float32,
            )
            pre = product if pre is None else pre + product
        if not last:
            out_ref[:, columns] = pre
            continue
        for slot in range(first, first + group):
            at = (slot - first) * units
            gate, up = pre[:, at : at + sliver], pre[:, at + sliver : at + units]
            mine = (lane == slot) | (lane == slot + experts) | (lane == slot + 2 * experts)
            weigh = jnp.sum(jnp.where(mine, extra, 0.0), axis=1, keepdims=True)
            hidden = (0.5 * gate) * (1.0 + jnp.tanh(0.5 * gate)) * up * weigh
            out_ref[slot] = hidden.astype(out_ref.dtype)
    pl.when(pl.program_id(0) == 0)(copy.wait)


def gate_up_of(row_part, sums, weights, next_weight, take, next_shape):
    held, _, sliver, half = weights[0].shape
    pieces = len(weights)
    experts = held * pieces
    rows = row_part.shape[0]
    row_block = min(ROW_BLOCK, rows)
    whole = rows == row_block
    last = sums is not None
    units = experts * 2 * sliver
    operands = [row_part, sums] if last else [row_part]
    if whole:
        specs = [pl.BlockSpec(memory_space=pltpu.VMEM)] * len(operands)
        operands = [resident(operand) for operand in operands]
    else:
        specs = [
            pl.BlockSpec((row_block, operand.shape[1]), lambda r: (r, 0)) for operand in operands
        ]
    if last:
        out_spec = pl.BlockSpec((experts, row_block, sliver), lambda r: (0, r, 0))
        out_shape = jax.ShapeDtypeStruct((experts, rows, sliver), jnp.bfloat16)
    else:
        out_spec = pl.BlockSpec((row_block, units), lambda r: (r, 0))
        out_shape = jax.ShapeDtypeStruct((rows, units), jnp.float32)
    if whole:
        out_spec = pl.BlockSpec(memory_space=pltpu.VMEM)
        out_shape = pltpu.VMEM(out_shape.shape, out_shape.dtype)

    def kernel(*refs):
        gate_up_kernel(last, take, pieces, *refs)

    return pl.pallas_call(
        kernel,
        grid=(rows // row_block,),
        in_specs=specs
        + [pl.BlockSpec(memory_space=pltpu.VMEM)] * pieces
        + [pl.BlockSpec(memory_space=pl.ANY)],
        out_specs=[out_spec, pl.BlockSpec(memory_space=pltpu.VMEM)],
        out_shape=[out_shape, pltpu.VMEM(next_shape, next_weight.dtype)],
        scratch_shapes=[pltpu.SemaphoreType.DMA],
        compiler_params=pltpu.CompilerParams(vmem_limit_bytes=GATE_UP_LIMIT),
        cost_estimate=pl.CostEstimate(
            flops=4 * rows * experts * sliver * half,
            bytes_accessed=2 * math.prod(next_shape) + 4 * rows * units,
            transcendentals=rows * experts * sliver,
        ),
    )(*operands, *(resident(weight) for weight in weights), in_hbm(next_weight))


def down_kernel(start, hidden_ref, w_ref, out_ref):
    experts, _, sliver = hidden_ref.shape
    columns = out_ref.shape[1]
    hidden = jnp.concatenate([hidden_ref[slot] for slot in range(experts)], axis=1)
    weights = w_ref[:, :, start : start + columns].reshape(experts * sliver, columns)
    out_ref[...] = jnp.dot(hidden, weights, preferred_element_type=jnp.float32).astype(
        out_ref.dtype
    )


def down_of(hidden, down_weight, start, columns):
    experts, rows, sliver = hidden.shape
    row_block = min(ROW_BLOCK, rows)

    def kernel(*refs):
        down_kernel(start, *refs)

    return pl.pallas_call(
        kernel,
        grid=(rows // row_block,),
        in_specs=[
            pl.BlockSpec((experts, row_block, sliver), lambda r: (0, r, 0)),
            pl.BlockSpec(memory_space=pltpu.VMEM),
        ],
        out_specs=pl.BlockSpec((row_block, columns), lambda r: (r, 0)),
        out_shape=jax.ShapeDtypeStruct((rows, columns), jnp.bfloat16),
        compiler_params=pltpu.CompilerParams(vmem_limit_bytes=DOWN_LIMIT),
        cost_estimate=pl.CostEstimate(
            flops=2 * rows * experts * sliver * columns,
            bytes_accessed=2 * (experts * sliver * columns + rows * experts * sliver + rows * columns),
            transcendentals=0,
        ),
    )(hidden, down_weight)


def reorder_kernel(order_ref, rows_ref, out_ref):
    for place in range(out_ref.shape[0]):
        out_ref[place] = rows_ref[order_ref[place]]


def reordered(order, blocks):
    return pl.pallas_call(
        reorder_kernel,
        in_specs=[pl.BlockSpec(memory_space=pltpu.SMEM), pl.BlockSpec(memory_space=pltpu.VMEM)],
        out_specs=pl.BlockSpec(memory_space=pltpu.VMEM),
        out_shape=jax.ShapeDtypeStruct(blocks.shape, blocks.dtype),
        compiler_params=pltpu.CompilerParams(vmem_limit_bytes=REORDER_LIMIT),
        cost_estimate=pl.CostEstimate(
            flops=0, bytes_accessed=4 * blocks.size, transcendentals=0
        ),
    )(order, blocks)


def row_orders(ways, dim_order):
    devices = math.prod(ways.values())
    number = jnp.arange(devices, dtype=jnp.int32)
    mine = {name: lax.axis_index(name) for name in AXES}
    weight, left = {}, 1
    for name in AXES[::-1]:
        weight[name] = left
        left *= ways[name]
    owner, block, stride = jnp.zeros_like(number), jnp.zeros_like(number), 1
    for digit in dim_order[::-1]:
        me = mine[digit.name] // digit.stride % digit.size
        slot = number // stride % digit.size
        owner += (me + digit.size - slot) % digit.size * digit.stride * weight[digit.name]
        other = number // weight[digit.name] % ways[digit.name] // digit.stride % digit.size
        block += (me + digit.size - other) % digit.size * stride
        stride *= digit.size
    return owner, block


def local(
    tokens, gate_up_weight, down_weight, expert_ids, slot_ids, gate_values, old_place, new_place
):
    model_width = tokens.shape[1]
    rows = tokens.shape[0]
    large = -(-model_width * 5 // (12 * MATRIX)) * MATRIX
    middle = 2 * large
    ways = {name: lax.axis_size(name) for name in AXES}
    cores = 2 if ways["shard"] % 2 == 0 else 1
    x_digits = digits_of("dp", ways["dp"])
    z_digits = digits_of("expert", ways["expert"])
    y_digits = digits_of("shard", ways["shard"], cores)
    core_digits = [Digit("shard", ways["shard"], 1, cores)]
    dim_order = core_digits + x_digits[::-1] + y_digits[::-1] + z_digits[::-1]
    routes = [z_digits + y_digits + x_digits, z_digits + x_digits + y_digits]

    coefficients = slot_coefficients(expert_ids, gate_values, old_place, new_place)
    extra = jnp.concatenate(split_exact(coefficients), axis=1)
    extra = jnp.pad(extra, ((0, 0), (0, -extra.shape[1] % LANES)))
    parts = [
        jnp.concatenate([tokens[:, :large], extra], axis=1),
        tokens[:, large:middle],
    ]
    outer_shape = gate_up_weight.shape[:3]
    first_shape = outer_shape + (large,)
    second_shape = outer_shape + (model_width - large,)

    def take_second(ref):
        return ref.at[:, :, :, pl.ds(large, model_width - large)]

    def take_first(ref):
        return ref.at[:, :, :, pl.ds(0, large)]

    rest = lax.all_gather(tokens[:, middle:], AXES, axis=0, tiled=False)
    owner, block_of = row_orders(ways, dim_order)
    parts[0], owner, block_of = lax.optimization_barrier((parts[0], owner, block_of))

    blocks, held = list(parts), [[], []]
    last = len(routes[0]) - 1
    for step in range(last + 2):
        if step == last:
            before_last = blocks[0]
        if step == last + 1:
            first_weights = fetched(gate_up_weight, take_second, second_shape, before_last)
            blocks[1], first_weights = lax.optimization_barrier((blocks[1], first_weights))
        for number in (1, 0):
            digit = (routes[number] + core_digits)[step]
            dim = sum(dim_order.index(other) < dim_order.index(digit) for other in held[number])
            blocks[number] = digit.gather(blocks[number], dim)
            held[number].append(digit)
    gathered = [block.reshape(-1, part.shape[1]) for block, part in zip(blocks, parts)]
    rest = reordered(owner, rest).reshape(-1, model_width - middle)
    gathered[1] = jnp.concatenate([gathered[1], rest], axis=1)
    sums, next_weights = gate_up_of(
        gathered[1], None, [first_weights], gate_up_weight, take_first, first_shape
    )
    hidden, down_weight = gate_up_of(
        gathered[0], sums, [next_weights], down_weight, lambda ref: ref, down_weight.shape
    )
    down_weight = resident(down_weight)
    rest = down_of(hidden, down_weight, middle, model_width - middle)
    rest = reordered(block_of, rest.reshape(-1, rows, model_width - middle))
    rest = lax.psum_scatter(rest, AXES, scatter_dimension=0, tiled=False)
    results = []
    for number, route in enumerate(routes):
        block = down_of(hidden, down_weight, number * large, large)
        block = block.reshape([digit.size for digit in dim_order] + [rows, large])
        held = list(dim_order)
        for digit in core_digits + route[::-1]:
            block = digit.reduce(block, held.index(digit))
            held.remove(digit)
        results.append(block)
    results.append(rest)
    return jnp.concatenate(results, axis=1)


def solution(mesh):
    in_specs = (
        P(AXES, None),
        P(None, None, AXES, None),
        P(None, AXES, None),
        P(AXES, None),
        P(AXES, None),
        P(AXES, None),
        P(),
        P(),
    )
    return jax.shard_map(
        local, mesh=mesh, in_specs=in_specs, out_specs=P(AXES, None), check_vma=False
    )
```

```python
import math

import jax
import jax.numpy as jnp
from jax import lax
from jax.experimental import pallas as pl
from jax.experimental.pallas import tpu as pltpu
from jax.sharding import PartitionSpec as P

AXES = ("dp", "expert", "shard")
LANES = 128
ROW_BLOCK = 256
FETCH_LIMIT = 1 * 2**20
GATE_UP_LIMIT = 8 * 2**20
DOWN_LIMIT = 8 * 2**20


def pack_kernel(tokens_ref, ids_ref, gates_ref, old_ref, new_ref, out_ref, other_ref):
    rows, width = tokens_ref.shape[0], tokens_ref.shape[1] - other_ref.shape[1]
    other_ref[...] = tokens_ref[:, width:]
    choices = ids_ref.shape[0]
    out_ref[:, :width] = tokens_ref[:, :width]
    square = (rows, rows)
    diagonal = lax.broadcasted_iota(jnp.int32, square, 0) == lax.broadcasted_iota(
        jnp.int32, square, 1
    )
    lane = lax.broadcasted_iota(jnp.int32, (rows, out_ref.shape[1] - width), 1)
    extra = jnp.zeros(lane.shape, jnp.float32)
    old = old_ref[...]
    index = lax.broadcasted_iota(jnp.int32, old.shape, 1).astype(jnp.float32)
    for choice in range(choices):
        ids = ids_ref[choice : choice + 1, :]
        slot = jnp.zeros(ids.shape, jnp.float32)
        for expert in range(old_ref.shape[1]):
            place = new_ref[:, expert : expert + 1]
            of_expert = jnp.sum(jnp.where(old == place, index, 0.0), axis=1, keepdims=True)
            slot = jnp.where(ids == expert, of_expert, slot)
        left = gates_ref[choice : choice + 1, :]
        values = [slot]
        for _ in range(3):
            values.append(left.astype(jnp.bfloat16).astype(jnp.float32))
            left = left - values[-1]
        for place, value in enumerate(values):
            column = jnp.sum(jnp.where(diagonal, value, 0.0), axis=1, keepdims=True)
            extra = jnp.where(lane == place * choices + choice, column, extra)
    out_ref[:, width:] = extra.astype(out_ref.dtype)


def packed(tokens, width, expert_ids, gate_values, old_place, new_place):
    rows, choices = expert_ids.shape
    experts = old_place.shape[0]
    lanes = -(-4 * choices // LANES) * LANES
    small = pl.BlockSpec((choices, rows), lambda i: (0, 0))
    place = pl.BlockSpec((1, experts), lambda i: (0, 0))
    operands = (tokens, expert_ids.T, gate_values.T, old_place[None, :], new_place[None, :])
    model_width = tokens.shape[1]
    return pl.pallas_call(
        pack_kernel,
        grid=(1,),
        in_specs=[pl.BlockSpec(tokens.shape, lambda i: (0, 0)), small, small, place, place],
        out_specs=[pl.BlockSpec(memory_space=pltpu.VMEM)] * 2,
        out_shape=[
            pltpu.VMEM((rows, width + lanes), tokens.dtype),
            pltpu.VMEM((rows, model_width - width), tokens.dtype),
        ],
        compiler_params=pltpu.CompilerParams(vmem_limit_bytes=FETCH_LIMIT),
        cost_estimate=pl.CostEstimate(flops=0, bytes_accessed=4 * tokens.size, transcendentals=0),
    )(*(in_hbm(operand) for operand in operands))


class Digit:
    def __init__(self, name, ways, stride, size):
        self.name, self.ways, self.stride, self.size = name, ways, stride, size

    def shift(self, value, step):
        pairs = []
        for index in range(self.ways):
            digit = index // self.stride % self.size
            target = (digit + step) % self.size
            pairs.append((index, index + (target - digit) * self.stride))
        return lax.ppermute(value, self.name, pairs)

    def gather(self, block, dim):
        return jnp.stack([block] + [self.shift(block, s) for s in range(1, self.size)], axis=dim)

    def reduce(self, slots, dim):
        own = lax.index_in_dim(slots, 0, dim, keepdims=False).astype(jnp.float32)
        for s in range(1, self.size):
            sent = lax.index_in_dim(slots, s, dim, keepdims=False)
            own = own + self.shift(sent, self.size - s).astype(jnp.float32)
        return own.astype(jnp.bfloat16)


def digits_of(name, ways, low=1):
    digits, stride = [], low
    while stride < ways:
        left = ways // stride
        size = 2 if left % 2 == 0 else left
        digits.append(Digit(name, ways, stride, size))
        stride *= size
    return digits[::-1]


def resident(value):
    return pltpu.with_memory_space_constraint(value, pltpu.VMEM)


def in_hbm(value):
    return pltpu.with_memory_space_constraint(value, pltpu.HBM)


def fetch_kernel(take, w_ref, after_ref, out_ref, sem):
    del after_ref
    copy = pltpu.make_async_copy(take(w_ref), out_ref, sem)
    copy.start()
    copy.wait()


def fetched(weight, take, shape, after):
    def kernel(*refs):
        fetch_kernel(take, *refs)

    return pl.pallas_call(
        kernel,
        in_specs=[pl.BlockSpec(memory_space=pl.ANY)] * 2,
        out_specs=pl.BlockSpec(memory_space=pltpu.VMEM),
        out_shape=pltpu.VMEM(shape, weight.dtype),
        scratch_shapes=[pltpu.SemaphoreType.DMA],
        compiler_params=pltpu.CompilerParams(vmem_limit_bytes=FETCH_LIMIT),
        cost_estimate=pl.CostEstimate(
            flops=0, bytes_accessed=4 * math.prod(shape), transcendentals=0
        ),
    )(in_hbm(weight), after)


def gate_up_kernel(choices, take, pieces, row_ref, *refs):
    last = choices > 0
    if last:
        sum_ref, refs = refs[0], refs[1:]
    w_refs, (next_hbm, out_ref, next_ref, sem) = refs[:pieces], refs[pieces:]
    held, _, sliver, half = w_refs[0].shape
    experts = held * pieces
    group = experts // 2 if experts % 2 == 0 else experts
    units = 2 * sliver
    depths = 2 if last else 1
    depth = half // depths
    copy = pltpu.make_async_copy(take(next_hbm), next_ref, sem)
    pl.when(pl.program_id(0) == 0)(copy.start)
    if last:
        extra = row_ref[:, half:].astype(jnp.float32)
        lane = lax.broadcasted_iota(jnp.int32, extra.shape, 1)
        chosen, gates = [], []
        for choice in range(choices):
            mine = (lane >= choices) & (lane < 4 * choices) & (lane % choices == choice)
            chosen.append(jnp.sum(jnp.where(lane == choice, extra, 0.0), axis=1, keepdims=True))
            gates.append(jnp.sum(jnp.where(mine, extra, 0.0), axis=1, keepdims=True))
    for first in range(0, experts, group):
        columns = slice(first * units, (first + group) * units)
        w_ref, at_slot = w_refs[first // held], first % held
        pre = sum_ref[:, columns] if last else None
        for at in range(0, half, depth):
            product = lax.dot_general(
                row_ref[:, at : at + depth],
                w_ref[at_slot : at_slot + group, :, :, at : at + depth].reshape(
                    group * units, depth
                ),
                (((1,), (1,)), ((), ())),
                preferred_element_type=jnp.float32,
            )
            pre = product if pre is None else pre + product
        if not last:
            out_ref[:, columns] = pre
            continue
        for slot in range(first, first + group):
            at = (slot - first) * units
            gate, up = pre[:, at : at + sliver], pre[:, at + sliver : at + units]
            weigh = sum(
                jnp.where(choice == slot, gate_value, 0.0)
                for choice, gate_value in zip(chosen, gates)
            )
            hidden = (0.5 * gate) * (1.0 + jnp.tanh(0.5 * gate)) * up * weigh
            out_ref[slot] = hidden.astype(out_ref.dtype)
    pl.when(pl.program_id(0) == 0)(copy.wait)


def gate_up_of(row_part, others, weights, next_weight, take, next_shape, choices=0):
    held, _, sliver, half = weights[0].shape
    pieces = len(weights)
    experts = held * pieces
    rows = row_part.shape[0]
    row_block = min(ROW_BLOCK, rows)
    whole = rows == row_block
    last = choices > 0
    units = experts * 2 * sliver
    operands = [row_part] + others
    if whole:
        specs = [pl.BlockSpec(memory_space=pltpu.VMEM)] * len(operands)
        operands = [resident(operand) for operand in operands]
    else:
        specs = [
            pl.BlockSpec((row_block, operand.shape[1]), lambda r: (r, 0)) for operand in operands
        ]
    if last:
        out_spec = pl.BlockSpec((experts, row_block, sliver), lambda r: (0, r, 0))
        out_shape = jax.ShapeDtypeStruct((experts, rows, sliver), jnp.bfloat16)
    else:
        out_spec = pl.BlockSpec((row_block, units), lambda r: (r, 0))
        out_shape = jax.ShapeDtypeStruct((rows, units), jnp.float32)
    if whole:
        out_spec = pl.BlockSpec(memory_space=pltpu.VMEM)
        out_shape = pltpu.VMEM(out_shape.shape, out_shape.dtype)

    def kernel(*refs):
        gate_up_kernel(choices, take, pieces, *refs)

    return pl.pallas_call(
        kernel,
        grid=(rows // row_block,),
        in_specs=specs
        + [pl.BlockSpec(memory_space=pltpu.VMEM)] * pieces
        + [pl.BlockSpec(memory_space=pl.ANY)],
        out_specs=[out_spec, pl.BlockSpec(memory_space=pltpu.VMEM)],
        out_shape=[out_shape, pltpu.VMEM(next_shape, next_weight.dtype)],
        scratch_shapes=[pltpu.SemaphoreType.DMA],
        compiler_params=pltpu.CompilerParams(vmem_limit_bytes=GATE_UP_LIMIT),
        cost_estimate=pl.CostEstimate(
            flops=4 * rows * experts * sliver * half,
            bytes_accessed=2 * math.prod(next_shape) + 4 * rows * units,
            transcendentals=rows * experts * sliver,
        ),
    )(*operands, *(resident(weight) for weight in weights), in_hbm(next_weight))


def down_kernel(part, hidden_ref, w_ref, out_ref):
    experts, _, sliver = hidden_ref.shape
    columns = out_ref.shape[1]
    block = next(size for size in (1536, 1024, 512, 384, 256, 128, columns) if columns % size == 0)

    def one_block(step, carry):
        at = pl.multiple_of(step * block, block)
        taken = pl.ds(pl.multiple_of(part * columns + step * block, block), block)
        hidden = jnp.concatenate([hidden_ref[slot] for slot in range(experts)], axis=1)
        weights = w_ref[:, :, taken].reshape(experts * sliver, block)
        out_ref[:, pl.ds(at, block)] = jnp.dot(
            hidden, weights, preferred_element_type=jnp.float32
        ).astype(out_ref.dtype)
        return carry

    lax.fori_loop(0, columns // block, one_block, 0)


def down_of(hidden, down_weight, part, columns):
    experts, rows, sliver = hidden.shape
    row_block = min(ROW_BLOCK, rows)

    def kernel(*refs):
        down_kernel(part, *refs)

    return pl.pallas_call(
        kernel,
        grid=(rows // row_block,),
        in_specs=[
            pl.BlockSpec((experts, row_block, sliver), lambda r: (0, r, 0)),
            pl.BlockSpec(memory_space=pltpu.VMEM),
        ],
        out_specs=pl.BlockSpec((row_block, columns), lambda r: (r, 0)),
        out_shape=jax.ShapeDtypeStruct((rows, columns), jnp.bfloat16),
        compiler_params=pltpu.CompilerParams(vmem_limit_bytes=DOWN_LIMIT),
        cost_estimate=pl.CostEstimate(
            flops=2 * rows * experts * sliver * columns,
            bytes_accessed=2 * (experts * sliver * columns + rows * experts * sliver + rows * columns),
            transcendentals=0,
        ),
    )(hidden, down_weight)


def local(
    tokens, gate_up_weight, down_weight, expert_ids, slot_ids, gate_values, old_place, new_place
):
    model_width = tokens.shape[1]
    rows = tokens.shape[0]
    half = model_width // 2
    ways = {name: lax.axis_size(name) for name in AXES}
    cores = 2 if ways["shard"] % 2 == 0 else 1
    x_digits = digits_of("dp", ways["dp"])
    z_digits = digits_of("expert", ways["expert"])
    y_digits = digits_of("shard", ways["shard"], cores)
    core_digits = [Digit("shard", ways["shard"], 1, cores)]
    dim_order = core_digits + x_digits[::-1] + y_digits[::-1] + z_digits[::-1]
    routes = [z_digits + y_digits + x_digits, z_digits + x_digits + y_digits]

    choices = expert_ids.shape[1]
    parts = packed(tokens, half, expert_ids, gate_values, old_place, new_place)
    half_shape = gate_up_weight.shape[:3] + (half,)

    def take_second(ref):
        return ref.at[:, :, :, pl.ds(half, half)]

    def take_first(ref):
        return ref.at[:, :, :, pl.ds(0, half)]

    blocks, held = list(parts), [[], []]
    last = len(routes[0]) - 1
    for step in range(last + 2):
        if step == last:
            before_last = blocks[0]
        if step == last + 1:
            first_weights = fetched(gate_up_weight, take_second, half_shape, before_last)
            blocks[1], first_weights = lax.optimization_barrier((blocks[1], first_weights))
        for number in (1, 0):
            digit = (routes[number] + core_digits)[step]
            dim = sum(dim_order.index(other) < dim_order.index(digit) for other in held[number])
            blocks[number] = digit.gather(blocks[number], dim)
            held[number].append(digit)
    gathered = [block.reshape(-1, part.shape[1]) for block, part in zip(blocks, parts)]
    sums, next_weights = gate_up_of(
        gathered[1], [], [first_weights], gate_up_weight, take_first, half_shape
    )
    hidden, down_weight = gate_up_of(
        gathered[0],
        [sums],
        [next_weights],
        down_weight,
        lambda ref: ref,
        down_weight.shape,
        choices,
    )
    down_weight = resident(down_weight)
    results = []
    for number, route in enumerate(routes):
        block = down_of(hidden, down_weight, number, half)
        block = block.reshape([digit.size for digit in dim_order] + [rows, half])
        held = list(dim_order)
        for digit in core_digits + route[::-1]:
            block = digit.reduce(block, held.index(digit))
            held.remove(digit)
        results.append(block)
    return jnp.concatenate(results, axis=1)


def solution(mesh):
    in_specs = (
        P(AXES, None),
        P(None, None, AXES, None),
        P(None, AXES, None),
        P(AXES, None),
        P(AXES, None),
        P(AXES, None),
        P(),
        P(),
    )
    return jax.shard_map(
        local, mesh=mesh, in_specs=in_specs, out_specs=P(AXES, None), check_vma=False
    )
```

```python
import math

import jax
import jax.numpy as jnp
from jax import lax
from jax.experimental import pallas as pl
from jax.experimental.pallas import tpu as pltpu
from jax.sharding import PartitionSpec as P

AXES = ("dp", "expert", "shard")
LANES = 128
ROW_BLOCK = 256
FETCH_LIMIT = 1 * 2**20
GATE_UP_LIMIT = 8 * 2**20
DOWN_LIMIT = 8 * 2**20


def pack_kernel(tokens_ref, ids_ref, gates_ref, old_ref, new_ref, out_ref, other_ref):
    rows, width = tokens_ref.shape[0], tokens_ref.shape[1] - other_ref.shape[1]
    other_ref[...] = tokens_ref[:, width:]
    choices = ids_ref.shape[0]
    out_ref[:, :width] = tokens_ref[:, :width]
    square = (rows, rows)
    diagonal = lax.broadcasted_iota(jnp.int32, square, 0) == lax.broadcasted_iota(
        jnp.int32, square, 1
    )
    lane = lax.broadcasted_iota(jnp.int32, (rows, out_ref.shape[1] - width), 1)
    extra = jnp.zeros(lane.shape, jnp.float32)
    old = old_ref[...]
    index = lax.broadcasted_iota(jnp.int32, old.shape, 1).astype(jnp.float32)
    for choice in range(choices):
        ids = ids_ref[choice : choice + 1, :]
        slot = jnp.zeros(ids.shape, jnp.float32)
        for expert in range(old_ref.shape[1]):
            place = new_ref[:, expert : expert + 1]
            of_expert = jnp.sum(jnp.where(old == place, index, 0.0), axis=1, keepdims=True)
            slot = jnp.where(ids == expert, of_expert, slot)
        left = gates_ref[choice : choice + 1, :]
        values = [slot]
        for _ in range(3):
            values.append(left.astype(jnp.bfloat16).astype(jnp.float32))
            left = left - values[-1]
        for place, value in enumerate(values):
            column = jnp.sum(jnp.where(diagonal, value, 0.0), axis=1, keepdims=True)
            extra = jnp.where(lane == place * choices + choice, column, extra)
    out_ref[:, width:] = extra.astype(out_ref.dtype)


def packed(tokens, width, expert_ids, gate_values, old_place, new_place):
    rows, choices = expert_ids.shape
    experts = old_place.shape[0]
    lanes = -(-4 * choices // LANES) * LANES
    small = pl.BlockSpec((choices, rows), lambda i: (0, 0))
    place = pl.BlockSpec((1, experts), lambda i: (0, 0))
    operands = (tokens, expert_ids.T, gate_values.T, old_place[None, :], new_place[None, :])
    model_width = tokens.shape[1]
    return pl.pallas_call(
        pack_kernel,
        grid=(1,),
        in_specs=[pl.BlockSpec(tokens.shape, lambda i: (0, 0)), small, small, place, place],
        out_specs=[pl.BlockSpec(memory_space=pltpu.VMEM)] * 2,
        out_shape=[
            pltpu.VMEM((rows, width + lanes), tokens.dtype),
            pltpu.VMEM((rows, model_width - width), tokens.dtype),
        ],
        compiler_params=pltpu.CompilerParams(vmem_limit_bytes=FETCH_LIMIT),
        cost_estimate=pl.CostEstimate(flops=0, bytes_accessed=4 * tokens.size, transcendentals=0),
    )(*(in_hbm(operand) for operand in operands))


class Digit:
    def __init__(self, name, ways, stride, size):
        self.name, self.ways, self.stride, self.size = name, ways, stride, size

    def shift(self, value, step):
        pairs = []
        for index in range(self.ways):
            digit = index // self.stride % self.size
            target = (digit + step) % self.size
            pairs.append((index, index + (target - digit) * self.stride))
        return lax.ppermute(value, self.name, pairs)

    def gather(self, block, dim):
        return jnp.stack([block] + [self.shift(block, s) for s in range(1, self.size)], axis=dim)

    def reduce(self, slots, dim):
        own = lax.index_in_dim(slots, 0, dim, keepdims=False).astype(jnp.float32)
        for s in range(1, self.size):
            sent = lax.index_in_dim(slots, s, dim, keepdims=False)
            own = own + self.shift(sent, self.size - s).astype(jnp.float32)
        return own.astype(jnp.bfloat16)


def digits_of(name, ways, low=1):
    digits, stride = [], low
    while stride < ways:
        left = ways // stride
        size = 2 if left % 2 == 0 else left
        digits.append(Digit(name, ways, stride, size))
        stride *= size
    return digits[::-1]


def resident(value):
    return pltpu.with_memory_space_constraint(value, pltpu.VMEM)


def in_hbm(value):
    return pltpu.with_memory_space_constraint(value, pltpu.HBM)


def fetch_kernel(take, w_ref, after_ref, out_ref, sem):
    del after_ref
    copy = pltpu.make_async_copy(take(w_ref), out_ref, sem)
    copy.start()
    copy.wait()


def fetched(weight, take, shape, after):
    def kernel(*refs):
        fetch_kernel(take, *refs)

    return pl.pallas_call(
        kernel,
        in_specs=[pl.BlockSpec(memory_space=pl.ANY)] * 2,
        out_specs=pl.BlockSpec(memory_space=pltpu.VMEM),
        out_shape=pltpu.VMEM(shape, weight.dtype),
        scratch_shapes=[pltpu.SemaphoreType.DMA],
        compiler_params=pltpu.CompilerParams(vmem_limit_bytes=FETCH_LIMIT),
        cost_estimate=pl.CostEstimate(
            flops=0, bytes_accessed=4 * math.prod(shape), transcendentals=0
        ),
    )(in_hbm(weight), after)


def gate_up_kernel(choices, take, pieces, row_ref, *refs):
    last = choices > 0
    if last:
        sum_ref, refs = refs[0], refs[1:]
    w_refs, (next_hbm, out_ref, next_ref, sem) = refs[:pieces], refs[pieces:]
    held, _, sliver, half = w_refs[0].shape
    experts = held * pieces
    group = experts // 2 if experts % 2 == 0 else experts
    units = 2 * sliver
    depths = 2 if last else 1
    depth = half // depths
    copy = pltpu.make_async_copy(take(next_hbm), next_ref, sem)
    pl.when(pl.program_id(0) == 0)(copy.start)
    if last:
        extra = row_ref[:, half:].astype(jnp.float32)
        lane = lax.broadcasted_iota(jnp.int32, extra.shape, 1)
        chosen, gates = [], []
        for choice in range(choices):
            mine = (lane >= choices) & (lane < 4 * choices) & (lane % choices == choice)
            chosen.append(jnp.sum(jnp.where(lane == choice, extra, 0.0), axis=1, keepdims=True))
            gates.append(jnp.sum(jnp.where(mine, extra, 0.0), axis=1, keepdims=True))
    for first in range(0, experts, group):
        columns = slice(first * units, (first + group) * units)
        w_ref, at_slot = w_refs[first // held], first % held
        pre = sum_ref[:, columns] if last else None
        for at in range(0, half, depth):
            product = lax.dot_general(
                row_ref[:, at : at + depth],
                w_ref[at_slot : at_slot + group, :, :, at : at + depth].reshape(
                    group * units, depth
                ),
                (((1,), (1,)), ((), ())),
                preferred_element_type=jnp.float32,
            )
            pre = product if pre is None else pre + product
        if not last:
            out_ref[:, columns] = pre
            continue
        for slot in range(first, first + group):
            at = (slot - first) * units
            gate, up = pre[:, at : at + sliver], pre[:, at + sliver : at + units]
            weigh = sum(
                jnp.where(choice == slot, gate_value, 0.0)
                for choice, gate_value in zip(chosen, gates)
            )
            hidden = (0.5 * gate) * (1.0 + jnp.tanh(0.5 * gate)) * up * weigh
            out_ref[slot] = hidden.astype(out_ref.dtype)
    pl.when(pl.program_id(0) == 0)(copy.wait)


def gate_up_of(row_part, others, weights, next_weight, take, next_shape, choices=0):
    held, _, sliver, half = weights[0].shape
    pieces = len(weights)
    experts = held * pieces
    rows = row_part.shape[0]
    row_block = min(ROW_BLOCK, rows)
    whole = rows == row_block
    last = choices > 0
    units = experts * 2 * sliver
    operands = [row_part] + others
    if whole:
        specs = [pl.BlockSpec(memory_space=pltpu.VMEM)] * len(operands)
        operands = [resident(operand) for operand in operands]
    else:
        specs = [
            pl.BlockSpec((row_block, operand.shape[1]), lambda r: (r, 0)) for operand in operands
        ]
    if last:
        out_spec = pl.BlockSpec((experts, row_block, sliver), lambda r: (0, r, 0))
        out_shape = jax.ShapeDtypeStruct((experts, rows, sliver), jnp.bfloat16)
    else:
        out_spec = pl.BlockSpec((row_block, units), lambda r: (r, 0))
        out_shape = jax.ShapeDtypeStruct((rows, units), jnp.float32)
    if whole:
        out_spec = pl.BlockSpec(memory_space=pltpu.VMEM)
        out_shape = pltpu.VMEM(out_shape.shape, out_shape.dtype)

    def kernel(*refs):
        gate_up_kernel(choices, take, pieces, *refs)

    return pl.pallas_call(
        kernel,
        grid=(rows // row_block,),
        in_specs=specs
        + [pl.BlockSpec(memory_space=pltpu.VMEM)] * pieces
        + [pl.BlockSpec(memory_space=pl.ANY)],
        out_specs=[out_spec, pl.BlockSpec(memory_space=pltpu.VMEM)],
        out_shape=[out_shape, pltpu.VMEM(next_shape, next_weight.dtype)],
        scratch_shapes=[pltpu.SemaphoreType.DMA],
        compiler_params=pltpu.CompilerParams(vmem_limit_bytes=GATE_UP_LIMIT),
        cost_estimate=pl.CostEstimate(
            flops=4 * rows * experts * sliver * half,
            bytes_accessed=2 * math.prod(next_shape) + 4 * rows * units,
            transcendentals=rows * experts * sliver,
        ),
    )(*operands, *(resident(weight) for weight in weights), in_hbm(next_weight))


def down_kernel(part, hidden_ref, w_ref, out_ref):
    experts, _, sliver = hidden_ref.shape
    columns = out_ref.shape[1]
    block = next(size for size in (1536, 1024, 512, 384, 256, 128, columns) if columns % size == 0)

    def one_block(step, carry):
        at = pl.multiple_of(step * block, block)
        taken = pl.ds(pl.multiple_of(part * columns + step * block, block), block)
        hidden = jnp.concatenate([hidden_ref[slot] for slot in range(experts)], axis=1)
        weights = w_ref[:, :, taken].reshape(experts * sliver, block)
        out_ref[:, pl.ds(at, block)] = jnp.dot(
            hidden, weights, preferred_element_type=jnp.float32
        ).astype(out_ref.dtype)
        return carry

    lax.fori_loop(0, columns // block, one_block, 0)


def down_of(hidden, down_weight, part, columns):
    experts, rows, sliver = hidden.shape
    row_block = min(ROW_BLOCK, rows)

    def kernel(*refs):
        down_kernel(part, *refs)

    return pl.pallas_call(
        kernel,
        grid=(rows // row_block,),
        in_specs=[
            pl.BlockSpec((experts, row_block, sliver), lambda r: (0, r, 0)),
            pl.BlockSpec(memory_space=pltpu.VMEM),
        ],
        out_specs=pl.BlockSpec((row_block, columns), lambda r: (r, 0)),
        out_shape=jax.ShapeDtypeStruct((rows, columns), jnp.bfloat16),
        compiler_params=pltpu.CompilerParams(vmem_limit_bytes=DOWN_LIMIT),
        cost_estimate=pl.CostEstimate(
            flops=2 * rows * experts * sliver * columns,
            bytes_accessed=2 * (experts * sliver * columns + rows * experts * sliver + rows * columns),
            transcendentals=0,
        ),
    )(hidden, down_weight)


def local(
    tokens, gate_up_weight, down_weight, expert_ids, slot_ids, gate_values, old_place, new_place
):
    model_width = tokens.shape[1]
    rows = tokens.shape[0]
    half = model_width // 2
    ways = {name: lax.axis_size(name) for name in AXES}
    cores = 2 if ways["shard"] % 2 == 0 else 1
    x_digits = digits_of("dp", ways["dp"])
    z_digits = digits_of("expert", ways["expert"])
    y_digits = digits_of("shard", ways["shard"], cores)
    core_digits = [Digit("shard", ways["shard"], 1, cores)]
    dim_order = core_digits + x_digits[::-1] + y_digits[::-1] + z_digits[::-1]
    routes = [z_digits + y_digits + x_digits, z_digits[::-1] + x_digits + y_digits]

    choices = expert_ids.shape[1]
    parts = packed(tokens, half, expert_ids, gate_values, old_place, new_place)
    half_shape = gate_up_weight.shape[:3] + (half,)

    def take_second(ref):
        return ref.at[:, :, :, pl.ds(half, half)]

    def take_first(ref):
        return ref.at[:, :, :, pl.ds(0, half)]

    blocks, held = list(parts), [[], []]
    last = len(routes[0]) - 1
    for step in range(last + 2):
        if step == last:
            before_last = blocks[0]
        if step == last + 1:
            first_weights = fetched(gate_up_weight, take_second, half_shape, before_last)
            blocks[1], first_weights = lax.optimization_barrier((blocks[1], first_weights))
        for number in (1, 0):
            digit = (routes[number] + core_digits)[step]
            dim = sum(dim_order.index(other) < dim_order.index(digit) for other in held[number])
            blocks[number] = digit.gather(blocks[number], dim)
            held[number].append(digit)
    gathered = [block.reshape(-1, part.shape[1]) for block, part in zip(blocks, parts)]
    sums, next_weights = gate_up_of(
        gathered[1], [], [first_weights], gate_up_weight, take_first, half_shape
    )
    hidden, down_weight = gate_up_of(
        gathered[0],
        [sums],
        [next_weights],
        down_weight,
        lambda ref: ref,
        down_weight.shape,
        choices,
    )
    down_weight = resident(down_weight)
    results = []
    for number, route in enumerate(routes):
        block = down_of(hidden, down_weight, number, half)
        block = block.reshape([digit.size for digit in dim_order] + [rows, half])
        held = list(dim_order)
        for digit in core_digits + route[::-1]:
            block = digit.reduce(block, held.index(digit))
            held.remove(digit)
        results.append(block)
    return jnp.concatenate(results, axis=1)


def solution(mesh):
    in_specs = (
        P(AXES, None),
        P(None, None, AXES, None),
        P(None, AXES, None),
        P(AXES, None),
        P(AXES, None),
        P(AXES, None),
        P(),
        P(),
    )
    return jax.shard_map(
        local, mesh=mesh, in_specs=in_specs, out_specs=P(AXES, None), check_vma=False
    )
```

```python
import math

import jax
import jax.numpy as jnp
from jax import lax
from jax.experimental import pallas as pl
from jax.experimental.pallas import tpu as pltpu
from jax.sharding import PartitionSpec as P

AXES = ("dp", "expert", "shard")
LANES = 128
ROW_BLOCK = 256
FETCH_LIMIT = 1 * 2**20
GATE_UP_LIMIT = 8 * 2**20
DOWN_LIMIT = 8 * 2**20


def slot_coefficients(expert_ids, gate_values, old_place, new_place):
    matches = (new_place[:, None] == old_place[None, :]).astype(jnp.float32)
    picks = (expert_ids[:, :, None] == jnp.arange(new_place.shape[0], dtype=jnp.int32)).astype(jnp.float32)
    by_expert = jnp.sum(picks * gate_values[:, :, None], axis=1)
    return jnp.sum(by_expert[:, :, None] * matches[None, :, :], axis=1)


def split_exact(value):
    pieces = []
    for _ in range(3):
        piece = lax.reduce_precision(value, exponent_bits=8, mantissa_bits=7)
        pieces.append(piece.astype(jnp.bfloat16))
        value = value - piece
    return pieces


class Digit:
    def __init__(self, name, ways, stride, size):
        self.name, self.ways, self.stride, self.size = name, ways, stride, size

    def shift(self, value, step):
        pairs = []
        for index in range(self.ways):
            digit = index // self.stride % self.size
            target = (digit + step) % self.size
            pairs.append((index, index + (target - digit) * self.stride))
        return lax.ppermute(value, self.name, pairs)

    def gather(self, block, dim):
        return jnp.stack([block] + [self.shift(block, s) for s in range(1, self.size)], axis=dim)

    def reduce(self, slots, dim):
        own = lax.index_in_dim(slots, 0, dim, keepdims=False).astype(jnp.float32)
        for s in range(1, self.size):
            sent = lax.index_in_dim(slots, s, dim, keepdims=False)
            own = own + self.shift(sent, self.size - s).astype(jnp.float32)
        return own.astype(jnp.bfloat16)


def digits_of(name, ways, low=1):
    digits, stride = [], low
    while stride < ways:
        left = ways // stride
        size = 2 if left % 2 == 0 else left
        digits.append(Digit(name, ways, stride, size))
        stride *= size
    return digits[::-1]


def resident(value):
    return pltpu.with_memory_space_constraint(value, pltpu.VMEM)


def in_hbm(value):
    return pltpu.with_memory_space_constraint(value, pltpu.HBM)


def fetch_kernel(take, w_ref, after_ref, out_ref, sem):
    del after_ref
    copy = pltpu.make_async_copy(take(w_ref), out_ref, sem)
    copy.start()
    copy.wait()


def fetched(weight, take, shape, after):
    def kernel(*refs):
        fetch_kernel(take, *refs)

    return pl.pallas_call(
        kernel,
        in_specs=[pl.BlockSpec(memory_space=pl.ANY)] * 2,
        out_specs=pl.BlockSpec(memory_space=pltpu.VMEM),
        out_shape=pltpu.VMEM(shape, weight.dtype),
        scratch_shapes=[pltpu.SemaphoreType.DMA],
        compiler_params=pltpu.CompilerParams(vmem_limit_bytes=FETCH_LIMIT),
        cost_estimate=pl.CostEstimate(
            flops=0, bytes_accessed=4 * math.prod(shape), transcendentals=0
        ),
    )(in_hbm(weight), after)


def gate_up_kernel(last, take, pieces, row_ref, *refs):
    if last:
        sum_ref, refs = refs[0], refs[1:]
    w_refs, (next_hbm, out_ref, next_ref, sem) = refs[:pieces], refs[pieces:]
    held, _, sliver, half = w_refs[0].shape
    experts = held * pieces
    group = experts // 2 if experts % 2 == 0 else experts
    units = 2 * sliver
    depths = 2 if last else 1
    depth = half // depths
    copy = pltpu.make_async_copy(take(next_hbm), next_ref, sem)
    pl.when(pl.program_id(0) == 0)(copy.start)
    if last:
        extra = row_ref[:, half:].astype(jnp.float32)
        lane = lax.broadcasted_iota(jnp.int32, extra.shape, 1)
    for first in range(0, experts, group):
        columns = slice(first * units, (first + group) * units)
        w_ref, at_slot = w_refs[first // held], first % held
        pre = sum_ref[:, columns] if last else None
        for at in range(0, half, depth):
            product = lax.dot_general(
                row_ref[:, at : at + depth],
                w_ref[at_slot : at_slot + group, :, :, at : at + depth].reshape(
                    group * units, depth
                ),
                (((1,), (1,)), ((), ())),
                preferred_element_type=jnp.float32,
            )
            pre = product if pre is None else pre + product
        if not last:
            out_ref[:, columns] = pre
            continue
        for slot in range(first, first + group):
            at = (slot - first) * units
            gate, up = pre[:, at : at + sliver], pre[:, at + sliver : at + units]
            mine = (lane == slot) | (lane == slot + experts) | (lane == slot + 2 * experts)
            weigh = jnp.sum(jnp.where(mine, extra, 0.0), axis=1, keepdims=True)
            hidden = (0.5 * gate) * (1.0 + jnp.tanh(0.5 * gate)) * up * weigh
            out_ref[slot] = hidden.astype(out_ref.dtype)
    pl.when(pl.program_id(0) == 0)(copy.wait)


def gate_up_of(row_part, sums, weights, next_weight, take, next_shape):
    held, _, sliver, half = weights[0].shape
    pieces = len(weights)
    experts = held * pieces
    rows = row_part.shape[0]
    row_block = min(ROW_BLOCK, rows)
    whole = rows == row_block
    last = sums is not None
    units = experts * 2 * sliver
    operands = [row_part, sums] if last else [row_part]
    if whole:
        specs = [pl.BlockSpec(memory_space=pltpu.VMEM)] * len(operands)
        operands = [resident(operand) for operand in operands]
    else:
        specs = [
            pl.BlockSpec((row_block, operand.shape[1]), lambda r: (r, 0)) for operand in operands
        ]
    if last:
        out_spec = pl.BlockSpec((experts, row_block, sliver), lambda r: (0, r, 0))
        out_shape = jax.ShapeDtypeStruct((experts, rows, sliver), jnp.bfloat16)
    else:
        out_spec = pl.BlockSpec((row_block, units), lambda r: (r, 0))
        out_shape = jax.ShapeDtypeStruct((rows, units), jnp.float32)
    if whole:
        out_spec = pl.BlockSpec(memory_space=pltpu.VMEM)
        out_shape = pltpu.VMEM(out_shape.shape, out_shape.dtype)

    def kernel(*refs):
        gate_up_kernel(last, take, pieces, *refs)

    return pl.pallas_call(
        kernel,
        grid=(rows // row_block,),
        in_specs=specs
        + [pl.BlockSpec(memory_space=pltpu.VMEM)] * pieces
        + [pl.BlockSpec(memory_space=pl.ANY)],
        out_specs=[out_spec, pl.BlockSpec(memory_space=pltpu.VMEM)],
        out_shape=[out_shape, pltpu.VMEM(next_shape, next_weight.dtype)],
        scratch_shapes=[pltpu.SemaphoreType.DMA],
        compiler_params=pltpu.CompilerParams(vmem_limit_bytes=GATE_UP_LIMIT),
        cost_estimate=pl.CostEstimate(
            flops=4 * rows * experts * sliver * half,
            bytes_accessed=2 * math.prod(next_shape) + 4 * rows * units,
            transcendentals=rows * experts * sliver,
        ),
    )(*operands, *(resident(weight) for weight in weights), in_hbm(next_weight))


def down_kernel(part, hidden_ref, w_ref, out_ref):
    experts, _, sliver = hidden_ref.shape
    columns = out_ref.shape[1]
    block = next(size for size in (1536, 1024, 512, 384, 256, 128, columns) if columns % size == 0)

    def one_block(step, carry):
        at = pl.multiple_of(step * block, block)
        taken = pl.ds(pl.multiple_of(part * columns + step * block, block), block)
        hidden = jnp.concatenate([hidden_ref[slot] for slot in range(experts)], axis=1)
        weights = w_ref[:, :, taken].reshape(experts * sliver, block)
        out_ref[:, pl.ds(at, block)] = jnp.dot(
            hidden, weights, preferred_element_type=jnp.float32
        ).astype(out_ref.dtype)
        return carry

    lax.fori_loop(0, columns // block, one_block, 0)


def down_of(hidden, down_weight, part, columns):
    experts, rows, sliver = hidden.shape
    row_block = min(ROW_BLOCK, rows)

    def kernel(*refs):
        down_kernel(part, *refs)

    return pl.pallas_call(
        kernel,
        grid=(rows // row_block,),
        in_specs=[
            pl.BlockSpec((experts, row_block, sliver), lambda r: (0, r, 0)),
            pl.BlockSpec(memory_space=pltpu.VMEM),
        ],
        out_specs=pl.BlockSpec((row_block, columns), lambda r: (r, 0)),
        out_shape=jax.ShapeDtypeStruct((rows, columns), jnp.bfloat16),
        compiler_params=pltpu.CompilerParams(vmem_limit_bytes=DOWN_LIMIT),
        cost_estimate=pl.CostEstimate(
            flops=2 * rows * experts * sliver * columns,
            bytes_accessed=2 * (experts * sliver * columns + rows * experts * sliver + rows * columns),
            transcendentals=0,
        ),
    )(hidden, down_weight)


def local(
    tokens, gate_up_weight, down_weight, expert_ids, slot_ids, gate_values, old_place, new_place
):
    model_width = tokens.shape[1]
    rows = tokens.shape[0]
    half = model_width // 2
    ways = {name: lax.axis_size(name) for name in AXES}
    cores = 2 if ways["shard"] % 2 == 0 else 1
    x_digits = digits_of("dp", ways["dp"])
    z_digits = digits_of("expert", ways["expert"])
    y_digits = digits_of("shard", ways["shard"], cores)
    core_digits = [Digit("shard", ways["shard"], 1, cores)]
    dim_order = core_digits + x_digits[::-1] + y_digits[::-1] + z_digits[::-1]
    routes = [z_digits + y_digits + x_digits, z_digits[::-1] + x_digits + y_digits]

    coefficients = slot_coefficients(expert_ids, gate_values, old_place, new_place)
    extra = jnp.concatenate(split_exact(coefficients), axis=1)
    extra = jnp.pad(extra, ((0, 0), (0, -extra.shape[1] % LANES)))
    parts = [
        jnp.concatenate([tokens[:, :half], extra], axis=1),
        tokens[:, half:],
    ]
    half_shape = gate_up_weight.shape[:3] + (half,)

    def take_second(ref):
        return ref.at[:, :, :, pl.ds(half, half)]

    def take_first(ref):
        return ref.at[:, :, :, pl.ds(0, half)]

    blocks, held = list(parts), [[], []]
    last = len(routes[0]) - 1
    for step in range(last + 2):
        if step == last:
            before_last = blocks[0]
        if step == last + 1:
            first_weights = fetched(gate_up_weight, take_second, half_shape, before_last)
            blocks[1], first_weights = lax.optimization_barrier((blocks[1], first_weights))
        for number in (1, 0):
            digit = (routes[number] + core_digits)[step]
            dim = sum(dim_order.index(other) < dim_order.index(digit) for other in held[number])
            blocks[number] = digit.gather(blocks[number], dim)
            held[number].append(digit)
    gathered = [block.reshape(-1, part.shape[1]) for block, part in zip(blocks, parts)]
    sums, next_weights = gate_up_of(
        gathered[1], None, [first_weights], gate_up_weight, take_first, half_shape
    )
    hidden, down_weight = gate_up_of(
        gathered[0], sums, [next_weights], down_weight, lambda ref: ref, down_weight.shape
    )
    down_weight = resident(down_weight)
    results = []
    for number, route in enumerate(routes):
        block = down_of(hidden, down_weight, number, half)
        block = block.reshape([digit.size for digit in dim_order] + [rows, half])
        held = list(dim_order)
        for digit in core_digits + route[::-1]:
            block = digit.reduce(block, held.index(digit))
            held.remove(digit)
        results.append(block)
    return jnp.concatenate(results, axis=1)


def solution(mesh):
    in_specs = (
        P(AXES, None),
        P(None, None, AXES, None),
        P(None, AXES, None),
        P(AXES, None),
        P(AXES, None),
        P(AXES, None),
        P(),
        P(),
    )
    return jax.shard_map(
        local, mesh=mesh, in_specs=in_specs, out_specs=P(AXES, None), check_vma=False
    )
```

```python
import math

import jax
import jax.numpy as jnp
from jax import lax
from jax.experimental import pallas as pl
from jax.experimental.pallas import tpu as pltpu
from jax.sharding import PartitionSpec as P

AXES = ("dp", "expert", "shard")
LANES = 128
ROW_BLOCK = 256
FETCH_LIMIT = 1 * 2**20
GATE_UP_LIMIT = 8 * 2**20
DOWN_LIMIT = 8 * 2**20


def pack_kernel(tokens_ref, ids_ref, gates_ref, old_ref, new_ref, out_ref, other_ref):
    rows, width = tokens_ref.shape[0], tokens_ref.shape[1] - other_ref.shape[1]
    other_ref[...] = tokens_ref[:, width:]
    choices = ids_ref.shape[0]
    out_ref[:, :width] = tokens_ref[:, :width]
    square = (rows, rows)
    diagonal = lax.broadcasted_iota(jnp.int32, square, 0) == lax.broadcasted_iota(
        jnp.int32, square, 1
    )
    lane = lax.broadcasted_iota(jnp.int32, (rows, out_ref.shape[1] - width), 1)
    extra = jnp.zeros(lane.shape, jnp.float32)
    old = old_ref[...]
    index = lax.broadcasted_iota(jnp.int32, old.shape, 1).astype(jnp.float32)
    for choice in range(choices):
        ids = ids_ref[choice : choice + 1, :]
        slot = jnp.zeros(ids.shape, jnp.float32)
        for expert in range(old_ref.shape[1]):
            place = new_ref[:, expert : expert + 1]
            of_expert = jnp.sum(jnp.where(old == place, index, 0.0), axis=1, keepdims=True)
            slot = jnp.where(ids == expert, of_expert, slot)
        left = gates_ref[choice : choice + 1, :]
        values = [slot]
        for _ in range(3):
            values.append(left.astype(jnp.bfloat16).astype(jnp.float32))
            left = left - values[-1]
        for place, value in enumerate(values):
            column = jnp.sum(jnp.where(diagonal, value, 0.0), axis=1, keepdims=True)
            extra = jnp.where(lane == place * choices + choice, column, extra)
    out_ref[:, width:] = extra.astype(out_ref.dtype)


def packed(tokens, width, expert_ids, gate_values, old_place, new_place):
    rows, choices = expert_ids.shape
    experts = old_place.shape[0]
    lanes = -(-4 * choices // LANES) * LANES
    small = pl.BlockSpec((choices, rows), lambda i: (0, 0))
    place = pl.BlockSpec((1, experts), lambda i: (0, 0))
    operands = (tokens, expert_ids.T, gate_values.T, old_place[None, :], new_place[None, :])
    model_width = tokens.shape[1]
    return pl.pallas_call(
        pack_kernel,
        grid=(1,),
        in_specs=[pl.BlockSpec(tokens.shape, lambda i: (0, 0)), small, small, place, place],
        out_specs=[pl.BlockSpec(memory_space=pltpu.VMEM)] * 2,
        out_shape=[
            pltpu.VMEM((rows, width + lanes), tokens.dtype),
            pltpu.VMEM((rows, model_width - width), tokens.dtype),
        ],
        compiler_params=pltpu.CompilerParams(vmem_limit_bytes=FETCH_LIMIT),
        cost_estimate=pl.CostEstimate(flops=0, bytes_accessed=4 * tokens.size, transcendentals=0),
    )(*(in_hbm(operand) for operand in operands))


class Digit:
    def __init__(self, name, ways, stride, size):
        self.name, self.ways, self.stride, self.size = name, ways, stride, size

    def shift(self, value, step):
        pairs = []
        for index in range(self.ways):
            digit = index // self.stride % self.size
            target = (digit + step) % self.size
            pairs.append((index, index + (target - digit) * self.stride))
        return lax.ppermute(value, self.name, pairs)

    def gather(self, block, dim):
        return jnp.stack([block] + [self.shift(block, s) for s in range(1, self.size)], axis=dim)

    def reduce(self, slots, dim):
        own = lax.index_in_dim(slots, 0, dim, keepdims=False).astype(jnp.float32)
        for s in range(1, self.size):
            sent = lax.index_in_dim(slots, s, dim, keepdims=False)
            own = own + self.shift(sent, self.size - s).astype(jnp.float32)
        return own.astype(jnp.bfloat16)


def digits_of(name, ways, low=1):
    digits, stride = [], low
    while stride < ways:
        left = ways // stride
        size = 2 if left % 2 == 0 else left
        digits.append(Digit(name, ways, stride, size))
        stride *= size
    return digits[::-1]


def resident(value):
    return pltpu.with_memory_space_constraint(value, pltpu.VMEM)


def in_hbm(value):
    return pltpu.with_memory_space_constraint(value, pltpu.HBM)


def fetch_kernel(take, w_ref, after_ref, out_ref, sem):
    del after_ref
    copy = pltpu.make_async_copy(take(w_ref), out_ref, sem)
    copy.start()
    copy.wait()


def fetched(weight, take, shape, after):
    def kernel(*refs):
        fetch_kernel(take, *refs)

    return pl.pallas_call(
        kernel,
        in_specs=[pl.BlockSpec(memory_space=pl.ANY)] * 2,
        out_specs=pl.BlockSpec(memory_space=pltpu.VMEM),
        out_shape=pltpu.VMEM(shape, weight.dtype),
        scratch_shapes=[pltpu.SemaphoreType.DMA],
        compiler_params=pltpu.CompilerParams(vmem_limit_bytes=FETCH_LIMIT),
        cost_estimate=pl.CostEstimate(
            flops=0, bytes_accessed=4 * math.prod(shape), transcendentals=0
        ),
    )(in_hbm(weight), after)


def gate_up_kernel(choices, take, pieces, row_ref, *refs):
    last = choices > 0
    if last:
        sum_ref, refs = refs[0], refs[1:]
    w_refs, (next_hbm, out_ref, next_ref, sem) = refs[:pieces], refs[pieces:]
    held, _, sliver, half = w_refs[0].shape
    experts = held * pieces
    group = experts // 2 if experts % 2 == 0 else experts
    units = 2 * sliver
    depths = 2 if last else 1
    depth = half // depths
    copy = pltpu.make_async_copy(take(next_hbm), next_ref, sem)
    pl.when(pl.program_id(0) == 0)(copy.start)
    if last:
        extra = row_ref[:, half:].astype(jnp.float32)
        lane = lax.broadcasted_iota(jnp.int32, extra.shape, 1)
        chosen, gates = [], []
        for choice in range(choices):
            mine = (lane >= choices) & (lane < 4 * choices) & (lane % choices == choice)
            chosen.append(jnp.sum(jnp.where(lane == choice, extra, 0.0), axis=1, keepdims=True))
            gates.append(jnp.sum(jnp.where(mine, extra, 0.0), axis=1, keepdims=True))
    for first in range(0, experts, group):
        columns = slice(first * units, (first + group) * units)
        w_ref, at_slot = w_refs[first // held], first % held
        pre = sum_ref[:, columns] if last else None
        for at in range(0, half, depth):
            product = lax.dot_general(
                row_ref[:, at : at + depth],
                w_ref[at_slot : at_slot + group, :, :, at : at + depth].reshape(
                    group * units, depth
                ),
                (((1,), (1,)), ((), ())),
                preferred_element_type=jnp.float32,
            )
            pre = product if pre is None else pre + product
        if not last:
            out_ref[:, columns] = pre
            continue
        for slot in range(first, first + group):
            at = (slot - first) * units
            gate, up = pre[:, at : at + sliver], pre[:, at + sliver : at + units]
            weigh = sum(
                jnp.where(choice == slot, gate_value, 0.0)
                for choice, gate_value in zip(chosen, gates)
            )
            hidden = (0.5 * gate) * (1.0 + jnp.tanh(0.5 * gate)) * up * weigh
            out_ref[slot] = hidden.astype(out_ref.dtype)
    pl.when(pl.program_id(0) == 0)(copy.wait)


def gate_up_of(row_part, others, weights, next_weight, take, next_shape, choices=0):
    held, _, sliver, half = weights[0].shape
    pieces = len(weights)
    experts = held * pieces
    rows = row_part.shape[0]
    row_block = min(ROW_BLOCK, rows)
    whole = rows == row_block
    last = choices > 0
    units = experts * 2 * sliver
    operands = [row_part] + others
    if whole:
        specs = [pl.BlockSpec(memory_space=pltpu.VMEM)] * len(operands)
        operands = [resident(operand) for operand in operands]
    else:
        specs = [
            pl.BlockSpec((row_block, operand.shape[1]), lambda r: (r, 0)) for operand in operands
        ]
    if last:
        out_spec = pl.BlockSpec((experts, row_block, sliver), lambda r: (0, r, 0))
        out_shape = jax.ShapeDtypeStruct((experts, rows, sliver), jnp.bfloat16)
    else:
        out_spec = pl.BlockSpec((row_block, units), lambda r: (r, 0))
        out_shape = jax.ShapeDtypeStruct((rows, units), jnp.float32)
    if whole:
        out_spec = pl.BlockSpec(memory_space=pltpu.VMEM)
        out_shape = pltpu.VMEM(out_shape.shape, out_shape.dtype)

    def kernel(*refs):
        gate_up_kernel(choices, take, pieces, *refs)

    return pl.pallas_call(
        kernel,
        grid=(rows // row_block,),
        in_specs=specs
        + [pl.BlockSpec(memory_space=pltpu.VMEM)] * pieces
        + [pl.BlockSpec(memory_space=pl.ANY)],
        out_specs=[out_spec, pl.BlockSpec(memory_space=pltpu.VMEM)],
        out_shape=[out_shape, pltpu.VMEM(next_shape, next_weight.dtype)],
        scratch_shapes=[pltpu.SemaphoreType.DMA],
        compiler_params=pltpu.CompilerParams(vmem_limit_bytes=GATE_UP_LIMIT),
        cost_estimate=pl.CostEstimate(
            flops=4 * rows * experts * sliver * half,
            bytes_accessed=2 * math.prod(next_shape) + 4 * rows * units,
            transcendentals=rows * experts * sliver,
        ),
    )(*operands, *(resident(weight) for weight in weights), in_hbm(next_weight))


def down_kernel(part, hidden_ref, w_ref, out_ref):
    experts, _, sliver = hidden_ref.shape
    columns = out_ref.shape[1]
    block = next(size for size in (1536, 1024, 512, 384, 256, 128, columns) if columns % size == 0)

    def one_block(step, carry):
        at = pl.multiple_of(step * block, block)
        taken = pl.ds(pl.multiple_of(part * columns + step * block, block), block)
        hidden = jnp.concatenate([hidden_ref[slot] for slot in range(experts)], axis=1)
        weights = w_ref[:, :, taken].reshape(experts * sliver, block)
        out_ref[:, pl.ds(at, block)] = jnp.dot(
            hidden, weights, preferred_element_type=jnp.float32
        ).astype(out_ref.dtype)
        return carry

    lax.fori_loop(0, columns // block, one_block, 0)


def down_of(hidden, down_weight, part, columns):
    experts, rows, sliver = hidden.shape
    row_block = min(ROW_BLOCK, rows)

    def kernel(*refs):
        down_kernel(part, *refs)

    return pl.pallas_call(
        kernel,
        grid=(rows // row_block,),
        in_specs=[
            pl.BlockSpec((experts, row_block, sliver), lambda r: (0, r, 0)),
            pl.BlockSpec(memory_space=pltpu.VMEM),
        ],
        out_specs=pl.BlockSpec((row_block, columns), lambda r: (r, 0)),
        out_shape=jax.ShapeDtypeStruct((rows, columns), jnp.bfloat16),
        compiler_params=pltpu.CompilerParams(vmem_limit_bytes=DOWN_LIMIT),
        cost_estimate=pl.CostEstimate(
            flops=2 * rows * experts * sliver * columns,
            bytes_accessed=2 * (experts * sliver * columns + rows * experts * sliver + rows * columns),
            transcendentals=0,
        ),
    )(hidden, down_weight)


def local(
    tokens, gate_up_weight, down_weight, expert_ids, slot_ids, gate_values, old_place, new_place
):
    model_width = tokens.shape[1]
    rows = tokens.shape[0]
    half = model_width // 2
    ways = {name: lax.axis_size(name) for name in AXES}
    cores = 2 if ways["shard"] % 2 == 0 else 1
    x_digits = digits_of("dp", ways["dp"])
    z_digits = digits_of("expert", ways["expert"])
    y_digits = digits_of("shard", ways["shard"], cores)
    core_digits = [Digit("shard", ways["shard"], 1, cores)]
    dim_order = core_digits + x_digits[::-1] + y_digits[::-1] + z_digits[::-1]
    routes = [z_digits + y_digits + x_digits, z_digits[::-1] + x_digits + y_digits]

    choices = expert_ids.shape[1]
    parts = packed(tokens, half, expert_ids, gate_values, old_place, new_place)
    half_shape = gate_up_weight.shape[:3] + (half,)

    def take_second(ref):
        return ref.at[:, :, :, pl.ds(half, half)]

    def take_first(ref):
        return ref.at[:, :, :, pl.ds(0, half)]

    blocks, held = list(parts), [[], []]
    last = len(routes[0]) - 1
    for step in range(last + 2):
        if step == last:
            before_last = blocks[0]
        if step == last + 1:
            first_weights = fetched(gate_up_weight, take_second, half_shape, before_last)
            blocks[1], first_weights = lax.optimization_barrier((blocks[1], first_weights))
        for number in (1, 0):
            digit = (routes[number] + core_digits)[step]
            dim = sum(dim_order.index(other) < dim_order.index(digit) for other in held[number])
            blocks[number] = digit.gather(blocks[number], dim)
            held[number].append(digit)
    gathered = [block.reshape(-1, part.shape[1]) for block, part in zip(blocks, parts)]
    sums, next_weights = gate_up_of(
        gathered[1], [], [first_weights], gate_up_weight, take_first, half_shape
    )
    hidden, down_weight = gate_up_of(
        gathered[0],
        [sums],
        [next_weights],
        down_weight,
        lambda ref: ref,
        down_weight.shape,
        choices,
    )
    down_weight = resident(down_weight)
    results = []
    for number, route in enumerate(routes):
        block = down_of(hidden, down_weight, number, half)
        block = block.reshape([digit.size for digit in dim_order] + [rows, half])
        held = list(dim_order)
        along_z = routes[1 - number][: len(z_digits)][::-1]
        for digit in core_digits + route[len(z_digits) :][::-1] + along_z:
            block = digit.reduce(block, held.index(digit))
            held.remove(digit)
        results.append(block)
    return jnp.concatenate(results, axis=1)


def solution(mesh):
    in_specs = (
        P(AXES, None),
        P(None, None, AXES, None),
        P(None, AXES, None),
        P(AXES, None),
        P(AXES, None),
        P(AXES, None),
        P(),
        P(),
    )
    return jax.shard_map(
        local, mesh=mesh, in_specs=in_specs, out_specs=P(AXES, None), check_vma=False
    )
```
